32 devices in a mesh: dp: 8 (over z, y), head: 4 (over x, core).
Axes of the slice: x: 2, y: 2, z: 4, core: 2. Of those that a mesh axis runs over, the one named last changes fastest.
Arguments:
- tokens: bfloat16 [8192, 768], P('dp'), may hold values from -6 to 6
- lengths: int32 [16], P('dp'), may hold values from 128 to 512, as said below
- boxes: int32 [2, 8192], P(None, 'dp'), may hold values from 0 to 1023
- query_weight: bfloat16 [768, 768], P('dp', 'head'), may hold values from -0.21875 to 0.21875
- key_weight: bfloat16 [768, 768], P('dp', 'head'), may hold values from -0.21875 to 0.21875
- value_weight: bfloat16 [768, 768], P('dp', 'head'), may hold values from -0.21875 to 0.21875
- query_bias: bfloat16 [768], P('head'), may hold values from -3 to 3
- key_bias: bfloat16 [768], P('head'), may hold values from -3 to 3
- value_bias: bfloat16 [768], P('head'), may hold values from -3 to 3
- box_key_weight: bfloat16 [768, 768], P('dp', 'head'), may hold values from -0.3125 to 0.3125
- box_query_weight: bfloat16 [768, 768], P('dp', 'head'), may hold values from -0.3125 to 0.3125
- out_weight: bfloat16 [768, 768], P('head', 'dp'), may hold values from -1.75 to 1.75
- out_bias: bfloat16 [768], replicated, may hold values from -3 to 3
- first_gain: bfloat16 [768], replicated, may hold values from 0.25 to 1.75
- first_shift: bfloat16 [768], replicated, may hold values from -3 to 3
- up_weight: bfloat16 [768, 3072], P('dp', 'head'), may hold values from -0.21875 to 0.21875
- up_bias: bfloat16 [3072], P('head'), may hold values from -3 to 3
- down_weight: bfloat16 [3072, 768], P('head', 'dp'), may hold values from -0.109375 to 0.109375
- down_bias: bfloat16 [768], replicated, may hold values from -3 to 3
- second_gain: bfloat16 [768], replicated, may hold values from 0.25 to 1.75
- second_shift: bfloat16 [768], replicated, may hold values from -3 to 3
- output_grad: bfloat16 [8192, 768], P('dp'), may hold values from -6 to 6
Outputs:
- output: bfloat16 [8192, 768], P('dp')
- tokens_grad: bfloat16 [8192, 768], P('dp')
- query_weight_grad: float32 [768, 768], P('dp', 'head')
- key_weight_grad: float32 [768, 768], P('dp', 'head')
- value_weight_grad: float32 [768, 768], P('dp', 'head')
- query_bias_grad: float32 [768], P('head')
- key_bias_grad: float32 [768], P('head')
- value_bias_grad: float32 [768], P('head')
- box_key_weight_grad: float32 [768, 768], P('dp', 'head')
- box_query_weight_grad: float32 [768, 768], P('dp', 'head')
- out_weight_grad: float32 [768, 768], P('head', 'dp')
- out_bias_grad: float32 [768], replicated
- first_gain_grad: float32 [768], replicated
- first_shift_grad: float32 [768], replicated
- up_weight_grad: float32 [768, 3072], P('dp', 'head')
- up_bias_grad: float32 [3072], P('head')
- down_weight_grad: float32 [3072, 768], P('head', 'dp')
- down_bias_grad: float32 [768], replicated
- second_gain_grad: float32 [768], replicated
- second_shift_grad: float32 [768], replicated
The draws below stay inside these ranges and needn't reach their ends.
Inputs may be any that keep to these rules, and one draw needn't show every extreme that they name: `lengths`: each page's count of real tokens; some page has all 512 in every draw.
All inputs are finite; a program needn't handle non-finite values.
Results may differ from the reference program's by a relative error of at most 0.025.
Values may be sent and summed in bfloat16 or wider, within the bound.
No kernel may reach another device: no remote copies, remote signals or barrier semaphores. Data moves between devices by JAX's collectives and lax.ppermute only.
A program may use at most 128 MiB of HBM per device.

```python
import jax
import jax.numpy as jnp
from jax import lax

D = 768
HEAD_DIM = 64
FF = 3072
E = 768
L = 512
PAGES = 16
TOKENS = 8192


def draw_lengths(key, part):
    key = jax.random.fold_in(key, 7)
    key_div, key_jit, key_pick = jax.random.split(key, 3)
    divisor = jax.random.randint(key_div, (PAGES,), 1, 5)
    jitter = jax.random.randint(key_jit, (PAGES,), 0, L // 8 + 1)
    values = jnp.minimum(L // divisor + jitter, L)
    chosen = jax.random.randint(key_pick, (), 0, PAGES)
    return jnp.where(jnp.arange(PAGES) == chosen, L, values).astype(jnp.int32)


def touch_ends(entries, own_key, least, high):
    dims = entries.shape
    index_at = [jax.random.randint(jax.random.fold_in(own_key, axis), (), 0, dims[axis]) for axis in range(len(dims))]
    entries = entries.at[tuple(index_at)].set(least)
    longest = dims.index(max(dims))
    index_at[longest] = (index_at[longest] + 1) % dims[longest]
    return entries.at[tuple(index_at)].set(high)


def block_levels(stream_key, extent, pieces, smallest, largest):
    level, own = 1.0, jax.random.fold_in(stream_key, 6)
    for dim, blocks in pieces:
        steps = jnp.exp(jax.random.uniform(jax.random.fold_in(own, dim), (blocks,), jnp.float32, smallest / len(pieces), largest / len(pieces)))
        level = level * jnp.repeat(steps, extent[dim] // blocks).reshape([-1 if axis == dim else 1 for axis in range(len(extent))])
    return level


def noise(key, shape, scale, reach, shards=(), kind=jnp.bfloat16):
    values = scale * jax.random.normal(key, shape, jnp.float32)
    if shards:
        values = values * block_levels(key, shape, shards, -0.22, 0.18)
    return jnp.clip(values, -reach, reach).astype(kind)


def setup_inputs(seed: int = 0) -> dict:
    key_list = jax.random.split(jax.random.key(seed), 23)
    return {
        "tokens": noise(key_list[0], (TOKENS, D), 1.0, 6.0, ((0, 8),)),
        "lengths": draw_lengths(jax.random.fold_in(key_list[22], 71), 0),
        "boxes": touch_ends(jax.random.randint(key_list[2], (2, TOKENS), 0, 1024), jax.random.fold_in(key_list[2], 1), 0, 1023).astype(jnp.int32),
        "query_weight": noise(key_list[3], (D, D), D ** -0.5, 0.21875, ((0, 8), (1, 4))),
        "key_weight": noise(key_list[4], (D, D), D ** -0.5, 0.21875, ((0, 8), (1, 4))),
        "value_weight": noise(key_list[5], (D, D), D ** -0.5, 0.21875, ((0, 8), (1, 4))),
        "query_bias": noise(key_list[6], (D,), 0.5, 3.0, ((0, 4),)),
        "key_bias": noise(key_list[7], (D,), 0.5, 3.0, ((0, 4),)),
        "value_bias": noise(key_list[8], (D,), 0.5, 3.0, ((0, 4),)),
        "box_key_weight": noise(key_list[9], (E, D), (E // 2) ** -0.5, 0.3125, ((0, 8), (1, 4))),
        "box_query_weight": noise(key_list[10], (E, D), (E // 2) ** -0.5, 0.3125, ((0, 8), (1, 4))),
        "out_weight": noise(key_list[11], (D, D), (max(D // 64, 4)) ** -0.5, 1.75, ((0, 4), (1, 8))),
        "out_bias": noise(key_list[12], (D,), 0.5, 3.0),
        "first_gain": jnp.clip(1.0 + 0.15 * jax.random.normal(key_list[13], (D,), jnp.float32), 0.25, 1.75).astype(jnp.bfloat16),
        "first_shift": noise(key_list[14], (D,), 0.5, 3.0),
        "up_weight": noise(key_list[15], (D, FF), D ** -0.5, 0.21875, ((0, 8), (1, 4))),
        "up_bias": noise(key_list[16], (FF,), 0.5, 3.0, ((0, 4),)),
        "down_weight": noise(key_list[17], (FF, D), FF ** -0.5, 0.109375, ((0, 4), (1, 8))),
        "down_bias": noise(key_list[18], (D,), 0.5, 3.0),
        "second_gain": jnp.clip(1.0 + 0.15 * jax.random.normal(key_list[19], (D,), jnp.float32), 0.25, 1.75).astype(jnp.bfloat16),
        "second_shift": noise(key_list[20], (D,), 0.5, 3.0),
        "output_grad": noise(key_list[21], (TOKENS, D), 1.0, 6.0, ((0, 8),)),
    }


@jax.custom_vjp
def low(v):
    return lax.optimization_barrier(v.astype(jnp.bfloat16)).astype(jnp.float32)

@jax.custom_vjp
def low_back(v):
    return v

def low_keep(v):
    return (low(v), None)

def low_pass(kept, grad):
    return (grad,)

def back_keep(v):
    return (v, None)

def back_low(kept, grad):
    return (low(grad),)
low.defvjp(low_keep, low_pass)
low_back.defvjp(back_keep, back_low)
exact_mode = lax.Precision.HIGHEST
norm_eps = 1e-05
sqrt_half = 0.7071067811865476

def matmul(left, right):
    return jnp.dot(left, right, precision=exact_mode)

def box_tables(boxes, quarter):
    frequency = 10000.0 ** (-jnp.arange(quarter, dtype=jnp.float32) / quarter)
    angles = boxes.T.astype(jnp.float32)[:, :, None] * frequency
    return (jnp.cos(angles), jnp.sin(angles))

def split_halves(values, quarter):
    shaped = values.reshape(values.shape[:-1] + (2, 2, quarter))
    return (shaped[..., 0, :], shaped[..., 1, :])

def join_halves(upper, lower):
    joined = jnp.stack([upper, lower], -2)
    return joined.reshape(joined.shape[:-3] + (joined.shape[-3] * 2 * joined.shape[-1],))

def turn_query(values, cosine, sine):
    sine_part, cosine_part = split_halves(values, cosine.shape[-1])
    return join_halves(sine_part * cosine + cosine_part * sine, cosine_part * cosine - sine_part * sine)

def turn_key(values, cosine, sine):
    sine_part, cosine_part = split_halves(values, cosine.shape[-1])
    return join_halves(sine_part * sine + cosine_part * cosine, cosine_part * sine - sine_part * cosine)

def layer_norm(values, gain, shift):
    average = lax.optimization_barrier(jnp.mean(values, -1, keepdims=True))
    centered = values - average
    variance = lax.optimization_barrier(jnp.mean(centered * centered, -1, keepdims=True))
    return centered * lax.rsqrt(variance + norm_eps) * gain + shift

def page_attention(query_page, key_page, value_page, cosine, sine, length, box_key, box_query):
    page_len, model_width = query_page.shape
    head_count = box_key.shape[1] // HEAD_DIM
    table_width = box_key.shape[0]
    query_heads = query_page.reshape(page_len, head_count, HEAD_DIM)
    key_heads = key_page.reshape(page_len, head_count, HEAD_DIM)
    value_heads = value_page.reshape(page_len, head_count, HEAD_DIM)
    cosine_heads = cosine[:, None]
    sine_heads = sine[:, None]
    boxkey_heads = box_key.reshape(table_width, head_count, HEAD_DIM)
    boxquery_heads = box_query.reshape(table_width, head_count, HEAD_DIM)
    query_proj = low_back(jnp.einsum('lhc,ehc->lhe', query_heads, boxkey_heads, precision=exact_mode))
    key_proj = low_back(jnp.einsum('lhc,ehc->lhe', key_heads, boxquery_heads, precision=exact_mode))
    query_turn = low(turn_query(query_proj, cosine_heads, sine_heads))
    key_turn = low(turn_key(key_proj, cosine_heads, sine_heads))
    key_table = low(join_halves(sine, cosine))
    query_table = low(join_halves(cosine, sine))
    wide_shape = (page_len, head_count, table_width)
    query_full = jnp.concatenate([query_heads, query_turn, jnp.broadcast_to(query_table[:, None, :], wide_shape)], -1)
    key_full = jnp.concatenate([key_heads, jnp.broadcast_to(key_table[:, None, :], wide_shape), key_turn], -1)
    raw_scores = low_back(jnp.einsum('qhc,khc->hqk', query_full, key_full, precision=exact_mode))
    valid = jnp.arange(page_len) < length
    scores = jnp.where(valid[None, None, :], raw_scores * HEAD_DIM ** (-0.5), -1000000000.0)
    highest = lax.optimization_barrier(jnp.max(scores, -1, keepdims=True))
    exponent = jnp.exp(scores - highest)
    attention_weights = exponent / lax.optimization_barrier(jnp.sum(exponent, -1, keepdims=True))
    context = jnp.einsum('hqk,khc->qhc', low(attention_weights), value_heads, precision=exact_mode)
    return context.reshape(page_len, model_width)

def forward(tokens, query_weight, key_weight, value_weight, query_bias, key_bias, value_bias, box_key_weight, box_query_weight, out_weight, out_bias, first_gain, first_shift, up_weight, up_bias, down_weight, down_bias, second_gain, second_shift, lengths, boxes):
    query = low(low_back(matmul(tokens, query_weight) + query_bias))
    key_rows = low(low_back(matmul(tokens, key_weight) + key_bias))
    value_rows = low(low_back(matmul(tokens, value_weight) + value_bias))
    cosine, sine = box_tables(boxes, box_key_weight.shape[0] // 4)
    page_count = lengths.shape[0]

    def pages_of(values):
        return values.reshape((page_count, -1) + values.shape[1:])
    checked = jax.checkpoint(page_attention)
    context = lax.map(lambda bundle: checked(*bundle, box_key_weight, box_query_weight), (pages_of(query), pages_of(key_rows), pages_of(value_rows), pages_of(cosine), pages_of(sine), lengths))
    context = low(low_back(context.reshape(tokens.shape)))
    attention = low_back(matmul(context, out_weight))
    hidden_one = layer_norm(tokens + attention + out_bias, first_gain, first_shift)
    inner = low_back(matmul(low(hidden_one), up_weight) + up_bias)
    active = low(0.5 * inner * (1.0 + lax.erf(inner * sqrt_half)))
    feed = low_back(matmul(active, down_weight))
    return layer_norm(hidden_one + feed + down_bias, second_gain, second_shift)

def reference(tokens, lengths, boxes, query_weight, key_weight, value_weight, query_bias, key_bias, value_bias, box_key_weight, box_query_weight, out_weight, out_bias, first_gain, first_shift, up_weight, up_bias, down_weight, down_bias, second_gain, second_shift, output_grad):
    params = (tokens, query_weight, key_weight, value_weight, query_bias, key_bias, value_bias, box_key_weight, box_query_weight, out_weight, out_bias, first_gain, first_shift, up_weight, up_bias, down_weight, down_bias, second_gain, second_shift)
    floats = tuple((member.astype(jnp.float32) for member in params))
    result, pullback = jax.vjp(lambda *inputs: forward(*inputs, lengths, boxes), *floats)
    gradients = pullback(output_grad.astype(jnp.float32))
    return (result.astype(jnp.bfloat16), gradients[0].astype(jnp.bfloat16), gradients[1], gradients[2], gradients[3], gradients[4], gradients[5], gradients[6], gradients[7], gradients[8], gradients[9], gradients[10], gradients[11], gradients[12], gradients[13], gradients[14], gradients[15], gradients[16], gradients[17], gradients[18])
```

```python
import jax
import jax.numpy as jnp
from jax import lax
from jax.sharding import PartitionSpec as P

HEAD_DIM = 64
norm_eps = 1e-05
sqrt_half = 0.7071067811865476
inv_root_two_pi = 0.3989422804014327
low = jnp.bfloat16
f32 = jnp.float32


def dot(left, right, axes=((1,), (0,))):
    return lax.dot_general(left, right, (axes, ((), ())), preferred_element_type=f32)


def swap_core(a):
    n = lax.axis_size("head")
    return lax.ppermute(a, "head", [(i, i ^ 1) for i in range(n)])


def swap_page(a):
    n = lax.axis_size("head")
    return lax.ppermute(a, "head", [(i, i ^ 2) for i in range(n)])


def swap_dp(a, bit):
    n = lax.axis_size("dp")
    return lax.ppermute(a, "dp", [(i, i ^ bit) for i in range(n)])


def turn_dp(a, step):
    n = lax.axis_size("dp")
    return lax.ppermute(a, "dp", [(i, (i + step) % n) for i in range(n)])


def gather_weights(shard):
    n = lax.axis_size("dp")
    rows, width = shard.shape
    if n != 8:
        own = lax.all_gather(shard, "dp", axis=0, tiled=True)
        return own, swap_page(own)
    index = lax.axis_index("dp")
    z, y = index // 2, index % 2
    line = jnp.zeros((4, rows, width), low)
    for k in range(4):
        piece = turn_dp(shard, 2 * k) if k else shard
        line = lax.dynamic_update_slice(line, piece[None], ((z - k) % 4, 0, 0))
    across = swap_page(line)
    beside = swap_dp(line, 1)
    far = jnp.concatenate([swap_dp(across[:2], 1), swap_page(beside[2:])], 0)

    def place(near, other):
        both = jnp.zeros((4, 2, rows, width), low)
        both = lax.dynamic_update_slice(both, near[:, None], (0, y, 0, 0))
        both = lax.dynamic_update_slice(both, other[:, None], (0, 1 - y, 0, 0))
        return both.reshape(8 * rows, width)

    return place(line, beside), place(across, far)


def scatter_grads(own, other):
    n = lax.axis_size("dp")
    rows, width = own.shape[0] // n, own.shape[1]
    own = own.astype(low)
    other = other.astype(low)
    if n != 8:
        mine = own.astype(f32) + swap_page(other).astype(f32)
        return lax.psum_scatter(mine.astype(low), "dp", scatter_dimension=0, tiled=True).astype(f32)
    index = lax.axis_index("dp")
    z, y = index // 2, index % 2
    own = own.reshape(4, 2, rows, width)
    other = other.reshape(4, 2, rows, width)

    def pick(a, at):
        return lax.dynamic_slice(a, (0, at, 0, 0), (4, 1, rows, width))[:, 0]

    line, beside = pick(own, y), pick(own, 1 - y)
    across, far = pick(other, y), pick(other, 1 - y)
    half_a = swap_page(far[:2])
    half_b = swap_dp(far[2:], 1)
    beside = jnp.concatenate(
        [(beside[:2].astype(f32) + half_a.astype(f32)).astype(low), beside[2:]], 0
    )
    across = jnp.concatenate(
        [across[:2], (across[2:].astype(f32) + half_b.astype(f32)).astype(low)], 0
    )
    line = line.astype(f32) + swap_page(across).astype(f32) + swap_dp(beside, 1).astype(f32)
    total = lax.dynamic_slice(line, (z, 0, 0), (1, rows, width))[0]
    line = line.astype(low)
    for k in range(1, 4):
        piece = lax.dynamic_slice(line, ((z + k) % 4, 0, 0), (1, rows, width))[0]
        total = total + turn_dp(piece, 2 * k).astype(f32)
    return total


def sum_dp(a):
    n = lax.axis_size("dp")
    bit = 1
    while bit < n:
        a = a + swap_dp(a, bit)
        bit *= 2
    return a


def pair_sum(partial):
    partial = partial.astype(low)
    return partial.astype(f32) + swap_core(partial).astype(f32)


def box_tables(boxes, quarter):
    frequency = 10000.0 ** (-jnp.arange(quarter, dtype=f32) / quarter)
    angles = boxes.T.astype(f32)[:, :, None] * frequency
    return jnp.cos(angles), jnp.sin(angles)


def split_halves(values, quarter):
    shaped = values.reshape(values.shape[:-1] + (2, 2, quarter))
    return shaped[..., 0, :], shaped[..., 1, :]


def join_halves(upper, lower):
    joined = jnp.stack([upper, lower], -2)
    return joined.reshape(joined.shape[:-3] + (joined.shape[-3] * 2 * joined.shape[-1],))


def normalize(values, gain, shift):
    average = jnp.mean(values, -1, keepdims=True)
    centered = values - average
    inverse = lax.rsqrt(jnp.mean(centered * centered, -1, keepdims=True) + norm_eps)
    scaled = centered * inverse
    return scaled * gain + shift, scaled, inverse


def normalize_back(grad_values, scaled, inverse, gain):
    upstream = grad_values * gain
    return inverse * (
        upstream
        - jnp.mean(upstream, -1, keepdims=True)
        - scaled * jnp.mean(upstream * scaled, -1, keepdims=True)
    )


def local(
    tokens, lengths, boxes, query_weight, key_weight, value_weight, query_bias, key_bias, value_bias,
    box_key_weight, box_query_weight, out_weight, out_bias, first_gain, first_shift, up_weight, up_bias,
    down_weight, down_bias, second_gain, second_shift, output_grad,
):
    pages = lengths.shape[0]
    page_len = tokens.shape[0] // pages
    width = tokens.shape[1]
    page = lax.axis_index("head") // (lax.axis_size("head") // pages)
    start = page * page_len
    rows = lax.dynamic_slice_in_dim(tokens, start, page_len, 0)
    grad_rows = lax.dynamic_slice_in_dim(output_grad, start, page_len, 0).astype(f32)
    box_rows = lax.dynamic_slice_in_dim(boxes, start, page_len, 1)
    length = lax.dynamic_slice_in_dim(lengths, page, 1, 0)[0]

    head_cols = query_weight.shape[1]
    first = jnp.concatenate([query_weight, key_weight, value_weight, box_key_weight, box_query_weight], 1)
    second = jnp.concatenate([out_weight.T, up_weight], 1)
    third = down_weight.T
    own_1, oth_1 = gather_weights(first)
    own_2, oth_2 = gather_weights(second)
    own_3, oth_3 = gather_weights(third)
    biases = jnp.concatenate([query_bias, key_bias, value_bias, up_bias])[None].astype(low)
    biases = jnp.concatenate([biases, swap_page(biases)], 0).astype(f32)

    def cut(own, oth, at, size):
        return jnp.concatenate([own[:, at : at + size], oth[:, at : at + size]], 1)

    def bias_of(at, size):
        return biases[:, at : at + size].reshape(1, -1)

    hc = head_cols
    w_query, w_key, w_value, w_boxkey, w_boxquery = (cut(own_1, oth_1, i * hc, hc) for i in range(5))
    w_out_t = cut(own_2, oth_2, 0, hc)
    w_up = cut(own_2, oth_2, hc, up_weight.shape[1])
    w_down_t = jnp.concatenate([own_3, oth_3], 1)
    b_out, g_one, s_one, b_down, g_two, s_two = (
        v.astype(f32) for v in (out_bias, first_gain, first_shift, down_bias, second_gain, second_shift)
    )

    heads = 2 * hc // HEAD_DIM
    quarter = w_boxkey.shape[0] // 4
    scale = HEAD_DIM**-0.5
    cosine, sine = box_tables(box_rows, quarter)
    key_table = join_halves(sine, cosine).astype(low)
    query_table = join_halves(cosine, sine).astype(low)
    cos_h, sin_h = cosine[:, None], sine[:, None]

    query = (dot(rows, w_query) + bias_of(0, hc)).astype(low)
    key = (dot(rows, w_key) + bias_of(hc, hc)).astype(low)
    value = (dot(rows, w_value) + bias_of(2 * hc, hc)).astype(low)
    shape = (page_len, heads, HEAD_DIM)
    qh, kh, vh = query.reshape(shape), key.reshape(shape), value.reshape(shape)
    bk = w_boxkey.reshape(-1, heads, HEAD_DIM)
    bq = w_boxquery.reshape(-1, heads, HEAD_DIM)
    a_s, a_c = split_halves(jnp.einsum("lhc,ehc->lhe", qh, bk, preferred_element_type=f32), quarter)
    b_s, b_c = split_halves(jnp.einsum("lhc,ehc->lhe", kh, bq, preferred_element_type=f32), quarter)
    query_turn = join_halves(a_s * cos_h + a_c * sin_h, a_c * cos_h - a_s * sin_h).astype(low)
    key_turn = join_halves(b_s * sin_h + b_c * cos_h, b_c * sin_h - b_s * cos_h).astype(low)
    wide = (page_len, heads, 4 * quarter)
    query_full = jnp.concatenate([qh, query_turn, jnp.broadcast_to(query_table[:, None], wide)], -1)
    key_full = jnp.concatenate([kh, jnp.broadcast_to(key_table[:, None], wide), key_turn], -1)
    raw = jnp.einsum("qhc,khc->hqk", query_full, key_full, preferred_element_type=f32)
    scores = jnp.where(jnp.arange(page_len)[None, None] < length, raw * scale, -1e9)
    exponent = jnp.exp(scores - jnp.max(scores, -1, keepdims=True))
    probs = exponent / jnp.sum(exponent, -1, keepdims=True)
    probs_low = probs.astype(low)
    context = jnp.einsum("hqk,khc->qhc", probs_low, vh, preferred_element_type=f32).astype(low)
    context = context.reshape(page_len, heads * HEAD_DIM)
    attention = pair_sum(dot(context, w_out_t, ((1,), (1,))))
    hidden, scaled_one, inverse_one = normalize(rows.astype(f32) + attention + b_out, g_one, s_one)
    hidden_low = hidden.astype(low)
    inner = dot(hidden_low, w_up) + bias_of(3 * hc, up_weight.shape[1])
    cumulative = 0.5 * (1.0 + lax.erf(inner * sqrt_half))
    active = (inner * cumulative).astype(low)
    slope = cumulative + inner * (jnp.exp(-0.5 * inner * inner) * inv_root_two_pi)
    feed = pair_sum(dot(active, w_down_t, ((1,), (1,))))
    result, scaled_two, inverse_two = normalize(hidden + feed + b_down, g_two, s_two)

    grad_two = normalize_back(grad_rows, scaled_two, inverse_two, g_two)
    feed_low = grad_two.astype(low)
    gw_down_t = dot(feed_low, active, ((0,), (0,)))
    grad_inner = (dot(feed_low, w_down_t) * slope).astype(low)
    gw_up = dot(hidden_low, grad_inner, ((0,), (0,)))
    grad_hidden = grad_two + pair_sum(dot(grad_inner, w_up, ((1,), (1,))))
    grad_one = normalize_back(grad_hidden, scaled_one, inverse_one, g_one)
    attn_low = grad_one.astype(low)
    gw_out_t = dot(attn_low, context, ((0,), (0,)))
    grad_context = dot(attn_low, w_out_t).astype(low).reshape(shape)
    grad_value = jnp.einsum("hqk,qhc->khc", probs_low, grad_context, preferred_element_type=f32).astype(low)
    grad_probs = jnp.einsum("qhc,khc->hqk", grad_context, vh, preferred_element_type=f32)
    row_inner = jnp.sum(probs * grad_probs, -1, keepdims=True)
    draw = (scale * (probs * (grad_probs - row_inner))).astype(low)
    gq_direct = jnp.einsum("hqk,khc->qhc", draw, kh, preferred_element_type=f32)
    g_u, g_l = split_halves(jnp.einsum("hqk,ke->qhe", draw, key_table, preferred_element_type=f32), quarter)
    d_a = join_halves(g_u * cos_h - g_l * sin_h, g_u * sin_h + g_l * cos_h).astype(low)
    gk_direct = jnp.einsum("hqk,qhc->khc", draw, qh, preferred_element_type=f32)
    g_u, g_l = split_halves(jnp.einsum("hqk,qe->khe", draw, query_table, preferred_element_type=f32), quarter)
    d_b = join_halves(g_u * sin_h - g_l * cos_h, g_u * cos_h + g_l * sin_h).astype(low)
    grad_query = gq_direct + jnp.einsum("qhe,ehc->qhc", d_a, bk, preferred_element_type=f32)
    grad_key = gk_direct + jnp.einsum("khe,ehc->khc", d_b, bq, preferred_element_type=f32)
    gw_boxkey = jnp.einsum("lhe,lhc->ehc", d_a, qh, preferred_element_type=f32).reshape(-1, 2 * hc)
    gw_boxquery = jnp.einsum("lhe,lhc->ehc", d_b, kh, preferred_element_type=f32).reshape(-1, 2 * hc)
    flat = (page_len, 2 * hc)
    grad_query = grad_query.astype(low).reshape(flat)
    grad_key = grad_key.astype(low).reshape(flat)
    grad_value = grad_value.reshape(flat)
    gw_query = dot(rows, grad_query, ((0,), (0,)))
    gw_key = dot(rows, grad_key, ((0,), (0,)))
    gw_value = dot(rows, grad_value, ((0,), (0,)))
    input_part = dot(grad_query, w_query, ((1,), (1,)))
    input_part = input_part + dot(grad_key, w_key, ((1,), (1,)))
    input_part = input_part + dot(grad_value, w_value, ((1,), (1,)))
    token_grad = (grad_one + pair_sum(input_part)).astype(low)

    sum_3 = scatter_grads(gw_down_t[:, : third.shape[1]], gw_down_t[:, third.shape[1] :])

    def parts(grads, side):
        return jnp.concatenate(
            [g[:, side * (g.shape[1] // 2) : (side + 1) * (g.shape[1] // 2)] for g in grads], 1
        )

    grads_2 = (gw_out_t, gw_up)
    sum_2 = scatter_grads(parts(grads_2, 0), parts(grads_2, 1))
    grads_1 = (gw_query, gw_key, gw_value, gw_boxkey, gw_boxquery)
    sum_1 = scatter_grads(parts(grads_1, 0), parts(grads_1, 1))

    def col(v):
        return jnp.sum(v.astype(f32), 0)

    by_head = [col(grad_query), col(grad_key), col(grad_value), col(grad_inner)]
    own_b = jnp.concatenate([v[: v.shape[0] // 2] for v in by_head])
    oth_b = jnp.concatenate([v[v.shape[0] // 2 :] for v in by_head])
    norms = jnp.concatenate(
        [col(grad_one), col(grad_hidden * scaled_one), col(grad_hidden), col(grad_two),
         col(grad_rows * scaled_two), col(grad_rows)]
    )
    size = own_b.shape[0]
    small = jnp.concatenate([own_b, norms])[None]
    swapped = swap_page(jnp.concatenate([oth_b, norms])[None])
    small = sum_dp(small + swapped)[0]
    bias_q, bias_k, bias_v = (small[i * hc : (i + 1) * hc] for i in range(3))
    bias_up = small[3 * hc : size]
    norms = [small[size + i * width : size + (i + 1) * width] for i in range(6)]

    def rows_of(mine):
        theirs = swap_page(mine)
        both = jnp.zeros((pages * page_len, width), low)
        both = lax.dynamic_update_slice(both, mine, (start, 0))
        return lax.dynamic_update_slice(both, theirs, (page_len - start, 0))

    return (
        rows_of(result.astype(low)),
        rows_of(token_grad),
        sum_1[:, :hc],
        sum_1[:, hc : 2 * hc],
        sum_1[:, 2 * hc : 3 * hc],
        bias_q,
        bias_k,
        bias_v,
        sum_1[:, 3 * hc : 4 * hc],
        sum_1[:, 4 * hc :],
        sum_2[:, :hc].T,
        norms[0],
        norms[1],
        norms[2],
        sum_2[:, hc:],
        bias_up,
        sum_3.T,
        norms[3],
        norms[4],
        norms[5],
    )


def solution(mesh):
    row, vec, mat, tam, all_ = P("dp", None), P("head"), P("dp", "head"), P("head", "dp"), P()
    return jax.shard_map(
        local,
        mesh=mesh,
        in_specs=(
            row, P("dp"), P(None, "dp"), mat, mat, mat, vec, vec, vec, mat, mat, tam, all_, all_, all_,
            mat, vec, tam, all_, all_, all_, row,
        ),
        out_specs=(
            row, row, mat, mat, mat, vec, vec, vec, mat, mat, tam, all_, all_, all_, mat, vec, tam,
            all_, all_, all_,
        ),
        check_vma=False,
    )
```

```python
import functools

import jax
import jax.numpy as jnp
from jax import lax
from jax.experimental import pallas as pl
from jax.experimental.pallas import tpu as pltpu
from jax.sharding import PartitionSpec as P

HEAD_DIM = 64
norm_eps = 1e-05
sqrt_half = 0.7071067811865476
inv_root_two_pi = 0.3989422804014327
low = jnp.bfloat16
f32 = jnp.float32


def dot(left, right, axes=((1,), (0,))):
    return lax.dot_general(left, right, (axes, ((), ())), preferred_element_type=f32)


def swap_core(a):
    n = lax.axis_size("head")
    return lax.ppermute(a, "head", [(i, i ^ 1) for i in range(n)])


def swap_page(a):
    n = lax.axis_size("head")
    return lax.ppermute(a, "head", [(i, i ^ 2) for i in range(n)])


def swap_dp(a, bit):
    n = lax.axis_size("dp")
    return lax.ppermute(a, "dp", [(i, i ^ bit) for i in range(n)])


def turn_dp(a, step):
    n = lax.axis_size("dp")
    return lax.ppermute(a, "dp", [(i, (i + step) % n) for i in range(n)])


VMEM_LIMIT = 56 * 1024 * 1024
BLOCKS = 8


def grid_dp():
    return (4, 2) if lax.axis_size("dp") == 8 else (1, 1)


def place_dp():
    index = lax.axis_index("dp")
    return (index // 2, index % 2) if lax.axis_size("dp") == 8 else (index * 0, index * 0)


def gather_weights(shard):
    nz, ny = grid_dp()
    if nz == 1:
        line = lax.all_gather(shard, "dp", axis=0, tiled=True)[None]
        return (line, swap_page(line))
    line = jnp.stack([shard] + [turn_dp(shard, ny * k) for k in range(1, nz)])
    across = swap_page(line)
    beside = swap_dp(line, 1)
    half = nz // 2
    return (line, across, beside, swap_dp(across[:half], 1), swap_page(beside[half:]))


def scatter_grads(parts):
    nz, ny = grid_dp()
    if nz == 1:
        line, across = parts
        mine = line.astype(f32) + swap_page(across).astype(f32)
        return lax.psum_scatter(mine.astype(low)[0], "dp", scatter_dimension=0, tiled=True).astype(f32)
    line, across, beside, far_a, far_b = parts
    half = nz // 2

    def add(a, b):
        return (a.astype(f32) + b.astype(f32)).astype(low)

    far_a = swap_page(far_a)
    far_b = swap_dp(far_b, 1)
    beside = jnp.concatenate([add(beside[:half], far_a), beside[half:]], 0)
    across = jnp.concatenate([across[:half], add(across[half:], far_b)], 0)
    line = line.astype(f32) + swap_page(across).astype(f32) + swap_dp(beside, 1).astype(f32)
    total = line[0]
    line = line.astype(low)
    for k in range(1, nz):
        total = total + turn_dp(line[k], ny * k).astype(f32)
    return total


def part_shapes(blocks, width, dtype=low):
    nz, ny = grid_dp()
    rows = blocks // (nz * ny)
    sizes = [nz, nz] if ny == 1 else [nz, nz, nz, nz // 2, nz // 2]
    return [jax.ShapeDtypeStruct((s, rows, width), dtype) for s in sizes]


def slots(parts, place, dims, sign, turned):
    nz, ny = dims
    found = []
    for side in range(2):
        for ky in range(ny):
            for kz in range(nz):
                if ky == 0:
                    piece = parts[side].at[kz]
                elif side == 0:
                    piece = parts[2].at[kz]
                else:
                    piece = parts[3].at[kz] if kz < nz // 2 else parts[4].at[kz - nz // 2]
                rows = piece.shape[0]
                z = lax.rem(place[0] + (sign * kz) % nz, nz) if nz > 1 else 0
                y = lax.rem(place[1] + ky, ny) if ny > 1 else 0
                block = z * ny + y
                if not turned:
                    found.append((piece, side, pl.multiple_of(block * rows, rows)))
                    continue
                size = rows * nz * ny // BLOCKS
                for sub in range(rows // size):
                    b = block * (rows // size) + sub
                    b = lax.rem(lax.div(b, 2), 2) * 4 + lax.div(b, 4) * 2 + lax.rem(b, 2)
                    found.append((piece.at[pl.ds(sub * size, size)], side, pl.multiple_of(b * size, size)))
    return found


def fetch(parts, whole, sems, place, dims, turned=False, columns=None):
    copies = []
    for i, (piece, side, row) in enumerate(slots(parts, place, dims, -1, turned)):
        source = piece if columns is None else piece.at[:, pl.ds(columns[0], columns[1])]
        copies.append(pltpu.make_async_copy(source, whole.at[side, pl.ds(row, piece.shape[0])], sems.at[i]))
    for copy in copies:
        copy.start()
    return copies


def deal(whole, parts, sems, place, dims, turned=False, columns=None):
    copies = []
    for i, (piece, side, row) in enumerate(slots(parts, place, dims, 1, turned)):
        target = piece if columns is None else piece.at[:, pl.ds(columns[0], columns[1])]
        copies.append(pltpu.make_async_copy(whole.at[side, pl.ds(row, piece.shape[0])], target, sems.at[i]))
    for copy in copies:
        copy.start()
    return copies


def finish(copies):
    for copy in copies:
        copy.wait()


SMEM = pl.BlockSpec(memory_space=pltpu.SMEM)
VMEM = pl.BlockSpec(memory_space=pltpu.VMEM)
ANYWHERE = pl.BlockSpec(memory_space=pl.ANY)
COPIES = pltpu.SemaphoreType.DMA((2 * BLOCKS,))


def call(kernel, name, flops, moved, outs, out_specs, in_specs, scratch, args, grid=None, exps=0):
    extra = {} if grid is None else {"grid": grid}
    return pl.pallas_call(
        kernel,
        out_shape=outs,
        in_specs=in_specs,
        out_specs=out_specs,
        scratch_shapes=scratch,
        compiler_params=pltpu.CompilerParams(vmem_limit_bytes=VMEM_LIMIT),
        cost_estimate=pl.CostEstimate(flops=int(flops), bytes_accessed=int(moved), transcendentals=int(exps)),
        name=name,
        **extra,
    )(*args)


def shape(*dims, dtype=low):
    return jax.ShapeDtypeStruct(dims, dtype)


NT = ((1,), (1,))


def attend_kernel(dims, count, scale, scal, rows, bias, cos, sin, cos_t, sin_t, *refs):
    parts, refs = refs[:count], refs[count:]
    (q_o, k_o, v_o, ctx_o, p_o, part_o), (box, proj, key_t, bk_t, bq, sems, more_sems) = refs[:6], refs[6:]
    step = pl.program_id(0)
    hc = box.shape[2] // 2
    half = cos.shape[1]

    @pl.when(step == 0)
    def _():
        place = (scal[0], scal[1])
        first = fetch(parts, proj, more_sems, place, dims, False, (2 * hc, 4 * hc))
        second = fetch(parts, box, sems, place, dims, True, (0, 2 * hc))
        finish(first)
        for side in range(2):
            at = slice(side * hc, (side + 1) * hc)
            qkv = (dot(rows[...], proj[side, :, : 3 * hc]) + bias[side : side + 1]).astype(low)
            q_o[:, at] = qkv[:, :hc]
            k_o[:, at] = qkv[:, hc : 2 * hc]
            v_o[:, at] = qkv[:, 2 * hc :]
        finish(second)
        for side in range(2):
            at = slice(side * hc, (side + 1) * hc)
            bk_t[at] = box[side, :, :hc].T
            bq[:, at] = box[side, :, hc:]
        key_t[...] = k_o[...].T

    pair = pl.ds(pl.multiple_of(step * 2 * HEAD_DIM, 2 * HEAD_DIM), 2 * HEAD_DIM)
    q2, v2, bq2 = q_o[:, pair], v_o[:, pair], bq[:, pair]
    kt2, bkt2 = key_t[pair], bk_t[pair]
    cos_low, sin_low = cos[...].astype(low), sin[...].astype(low)
    cost_low, sint_low = cos_t[...].astype(low), sin_t[...].astype(low)
    valid = lax.broadcasted_iota(jnp.int32, (1, kt2.shape[1]), 1) < scal[2]
    outs = []
    for j in range(2):
        at = slice(j * HEAD_DIM, (j + 1) * HEAD_DIM)
        a = dot(q2[:, at], bkt2[at])
        a_s, a_c = a[:, :half], a[:, half:]
        raw = dot(q2[:, at], kt2[at])
        raw = raw + dot((a_s * cos[...] + a_c * sin[...]).astype(low), sint_low)
        raw = raw + dot((a_c * cos[...] - a_s * sin[...]).astype(low), cost_low)
        b = dot(bq2[:, at], kt2[at])
        b_s, b_c = b[:half], b[half:]
        raw = raw + dot(cos_low, (b_s * sin_t[...] + b_c * cos_t[...]).astype(low))
        raw = raw + dot(sin_low, (b_c * sin_t[...] - b_s * cos_t[...]).astype(low))
        scores = jnp.where(valid, raw * scale, -1e9)
        exponent = jnp.exp(scores - jnp.max(scores, -1, keepdims=True))
        probs = (exponent / jnp.sum(exponent, -1, keepdims=True)).astype(low)
        p_o[j] = probs
        outs.append(dot(probs, v2[:, at]))
    ctx_o[:, pair] = jnp.concatenate(outs, 1).astype(low)

    @pl.when(step == pl.num_programs(0) - 1)
    def _():
        ctx = ctx_o[...]
        total = dot(ctx[:, :hc], proj[0, :, 3 * hc :], NT) + dot(ctx[:, hc:], proj[1, :, 3 * hc :], NT)
        part_o[...] = total.astype(low)


def attend(scal, rows, bias, tables, parts):
    length, width = rows.shape
    hc = parts[0].shape[2] // 6
    heads = 2 * hc // HEAD_DIM
    half = tables[0].shape[1]
    flops = 2 * length * (8 * width * hc + heads * (4 * half * HEAD_DIM + length * (4 * half + 2 * HEAD_DIM)))
    full = pl.BlockSpec((length, 2 * hc), lambda p: (0, 0))
    return call(
        functools.partial(attend_kernel, grid_dp(), len(parts), HEAD_DIM**-0.5),
        "attend",
        flops,
        12e6,
        [shape(length, 2 * hc)] * 4 + [shape(heads, length, length), shape(length, width)],
        [full] * 4 + [pl.BlockSpec((2, length, length), lambda p: (p, 0, 0)), pl.BlockSpec((length, width), lambda p: (0, 0))],
        [SMEM] + [VMEM] * 6 + [ANYWHERE] * len(parts),
        [
            pltpu.VMEM((2, width, 2 * hc), low),
            pltpu.VMEM((2, width, 4 * hc), low),
            pltpu.VMEM((2 * hc, length), low),
            pltpu.VMEM((2 * hc, width), low),
            pltpu.VMEM((width, 2 * hc), low),
            COPIES,
            COPIES,
        ],
        (scal, rows, bias, *tables, *parts),
        (heads // 2,),
        heads * length * length,
    )


def standard(values):
    centered = values - jnp.mean(values, -1, keepdims=True)
    inverse = lax.rsqrt(jnp.mean(centered * centered, -1, keepdims=True) + norm_eps)
    return centered * inverse, inverse


def standard_back(upstream, scaled, inverse):
    return inverse * (
        upstream - jnp.mean(upstream, -1, keepdims=True) - scaled * jnp.mean(upstream * scaled, -1, keepdims=True)
    )


def col(values):
    return jnp.sum(values, 0, keepdims=True)


def feed_kernel(dims, count, scal, mine, theirs, rows, vecs, bias, *refs):
    ups, downs, refs = refs[:count], refs[count : 2 * count], refs[2 * count :]
    (hidden_o, low_o, scaled_o, inverse_o, active_o, slope_o, part_o), (up, down, sems, more_sems) = refs[:7], refs[7:]
    place = (scal[0], scal[1])
    first = fetch(ups, up, sems, place, dims)
    second = fetch(downs, down, more_sems, place, dims)
    total = rows[...].astype(f32) + (mine[...].astype(f32) + theirs[...].astype(f32)) + vecs[0:1]
    scaled, inverse = standard(total)
    hidden = scaled * vecs[1:2] + vecs[2:3]
    hidden_o[...] = hidden
    scaled_o[...] = scaled
    inverse_o[...] = inverse
    hidden_low = hidden.astype(low)
    low_o[...] = hidden_low
    finish(first)
    width = up.shape[2]
    size = 256
    for side in range(2):
        for at in range(0, width, size):
            inner = dot(hidden_low, up[side, :, at : at + size]) + bias[side : side + 1, at : at + size]
            cumulative = 0.5 * (1.0 + lax.erf(inner * sqrt_half))
            density = jnp.exp(-0.5 * inner * inner) * inv_root_two_pi
            active_o[:, side * width + at : side * width + at + size] = (inner * cumulative).astype(low)
            slope_o[:, side * width + at : side * width + at + size] = (cumulative + inner * density).astype(low)
    finish(second)
    part = dot(active_o[:, :width], down[0], NT) + dot(active_o[:, width:], down[1], NT)
    part_o[...] = part.astype(low)


def feed_forward(scal, mine, theirs, rows, vecs, bias, ups, downs):
    length, width = rows.shape
    units = ups[0].shape[2]
    return call(
        functools.partial(feed_kernel, grid_dp(), len(ups)),
        "feed_forward",
        8 * length * width * units,
        14e6,
        [
            shape(length, width, dtype=f32),
            shape(length, width),
            shape(length, width, dtype=f32),
            shape(length, 1, dtype=f32),
            shape(length, 2 * units),
            shape(length, 2 * units),
            shape(length, width),
        ],
        [VMEM] * 7,
        [SMEM] + [VMEM] * 5 + [ANYWHERE] * (2 * len(ups)),
        [pltpu.VMEM((2, width, units), low)] * 2 + [COPIES] * 2,
        (scal, mine, theirs, rows, vecs, bias, *ups, *downs),
        exps=2 * length * units,
    )


def feed_back_kernel(dims, count, scal, mine, theirs, hidden, grad_out, vecs, active, *refs):
    (result_o, grad_o, low_o, sums_o), outs, (grads, sems) = refs[:4], refs[4 : 4 + count], refs[4 + count :]
    scaled, inverse = standard(hidden[...] + (mine[...].astype(f32) + theirs[...].astype(f32)) + vecs[0:1])
    result_o[...] = (scaled * vecs[1:2] + vecs[2:3]).astype(low)
    grad = grad_out[...].astype(f32)
    sums_o[1:2] = col(grad * scaled)
    sums_o[2:3] = col(grad)
    grad = standard_back(grad * vecs[1:2], scaled, inverse)
    sums_o[0:1] = col(grad)
    grad_o[...] = grad
    grad_low = grad.astype(low)
    low_o[...] = grad_low
    turned = grad_low.T
    units = grads.shape[2]
    for side in range(2):
        grads[side] = dot(turned, active[:, side * units : (side + 1) * units]).astype(low)
    finish(deal(grads, outs, sems, (scal[0], scal[1]), dims))


def feed_back(scal, mine, theirs, hidden, grad_out, vecs, active):
    length, width = hidden.shape
    units = active.shape[1] // 2
    parts = part_shapes(width, units)
    out = call(
        functools.partial(feed_back_kernel, grid_dp(), len(parts)),
        "feed_back",
        4 * length * width * units,
        12e6,
        [shape(length, width), shape(length, width, dtype=f32), shape(length, width), shape(3, width, dtype=f32)] + parts,
        [VMEM] * 4 + [ANYWHERE] * len(parts),
        [SMEM] + [VMEM] * 6,
        [pltpu.VMEM((2, width, units), low), COPIES],
        (scal, mine, theirs, hidden, grad_out, vecs, active),
    )
    return out[:4], out[4:]


def inner_back_kernel(dims, count, scal, grad_low, slope, *refs):
    downs, ups, refs = refs[:count], refs[count : 2 * count], refs[2 * count :]
    (inner_o, sums_o, part_o), (down, up, sems, more_sems) = refs[:3], refs[3:]
    place = (scal[0], scal[1])
    first = fetch(downs, down, sems, place, dims)
    second = fetch(ups, up, more_sems, place, dims)
    finish(first)
    units = up.shape[2]
    for side in range(2):
        at = slice(side * units, (side + 1) * units)
        grad = (dot(grad_low[...], down[side]) * slope[:, at].astype(f32)).astype(low)
        inner_o[:, at] = grad
        sums_o[side : side + 1] = col(grad.astype(f32))
    finish(second)
    part = dot(inner_o[:, :units], up[0], NT) + dot(inner_o[:, units:], up[1], NT)
    part_o[...] = part.astype(low)


def inner_back(scal, grad_low, slope, downs, ups):
    length, width = grad_low.shape
    units = slope.shape[1] // 2
    return call(
        functools.partial(inner_back_kernel, grid_dp(), len(ups)),
        "inner_back",
        8 * length * width * units,
        10e6,
        [shape(length, 2 * units), shape(2, units, dtype=f32), shape(length, width)],
        [VMEM] * 3,
        [SMEM] + [VMEM] * 2 + [ANYWHERE] * (2 * len(ups)),
        [pltpu.VMEM((2, width, units), low)] * 2 + [COPIES] * 2,
        (scal, grad_low, slope, *downs, *ups),
    )


def norm_back_kernel(dims, count, given, scal, mine, theirs, grad_two, scaled, inverse, vecs, hidden_low, grad_inner, ctx, *refs):
    weights, refs = refs[:given], refs[given:]
    (grad_o, dctx_o, sums_o), outs, (out_w, grads, sems) = refs[:3], refs[3 : 3 + count], refs[3 + count :]
    place = (scal[0], scal[1])
    hc = out_w.shape[2] // 2
    copies = fetch(weights, out_w, sems, place, dims, False, (4 * hc, 2 * hc))
    grad = grad_two[...] + (mine[...].astype(f32) + theirs[...].astype(f32))
    sums_o[1:2] = col(grad * scaled[...])
    sums_o[2:3] = col(grad)
    grad = standard_back(grad * vecs[1:2], scaled[...], inverse[...])
    sums_o[0:1] = col(grad)
    grad_o[...] = grad
    grad_low = grad.astype(low)
    finish(copies)
    for side in range(2):
        dctx_o[:, side * hc : (side + 1) * hc] = dot(grad_low, out_w[side, :, hc:]).astype(low)
    units = grads.shape[2] - hc
    turned = hidden_low[...].T
    for side in range(2):
        grads[side, :, :units] = dot(turned, grad_inner[:, side * units : (side + 1) * units]).astype(low)
    grad_ctx = dot(grad_low.T, ctx[...]).astype(low)
    for side in range(2):
        grads[side, :, units:] = grad_ctx[:, side * hc : (side + 1) * hc]
    finish(deal(grads, outs, sems, place, dims))


def norm_back(scal, mine, theirs, grad_two, scaled, inverse, vecs, hidden_low, grad_inner, ctx, weights):
    length, width = grad_two.shape
    units, hc = grad_inner.shape[1] // 2, ctx.shape[1] // 2
    parts = part_shapes(width, units + hc)
    out = call(
        functools.partial(norm_back_kernel, grid_dp(), len(parts), len(weights)),
        "norm_back",
        4 * length * width * (units + 2 * hc),
        14e6,
        [shape(length, width, dtype=f32), shape(length, 2 * hc), shape(3, width, dtype=f32)] + parts,
        [VMEM] * 3 + [ANYWHERE] * len(parts),
        [SMEM] + [VMEM] * 9 + [ANYWHERE] * len(weights),
        [pltpu.VMEM((2, width, 2 * hc), low), pltpu.VMEM((2, width, units + hc), low), COPIES],
        (scal, mine, theirs, grad_two, scaled, inverse, vecs, hidden_low, grad_inner, ctx, *weights),
    )
    return out[:3], out[3:]


def attend_back_kernel(dims, count, scale, scal, dctx, probs, q, k, v, cos, sin, cos_t, sin_t, *refs):
    parts, refs = refs[:count], refs[count:]
    (dq_o, dk_o, dv_o, gbk_o, gbq_o), (box, bk, bq_t, sems) = refs[:5], refs[5:]
    step = pl.program_id(0)
    hc = box.shape[2] // 2
    half = cos.shape[1]

    @pl.when(step == 0)
    def _():
        finish(fetch(parts, box, sems, (scal[0], scal[1]), dims, True, (0, 2 * hc)))
        for side in range(2):
            at = slice(side * hc, (side + 1) * hc)
            bk[:, at] = box[side, :, :hc]
            bq_t[at] = box[side, :, hc:].T

    pair = pl.ds(pl.multiple_of(step * 2 * HEAD_DIM, 2 * HEAD_DIM), 2 * HEAD_DIM)
    bk2, bqt2 = bk[:, pair], bq_t[pair]
    q2, k2, v2, dctx2 = q[...], k[...], v[...], dctx[...]
    qt2, vt2, dctxt2 = q2.T, v2.T, dctx2.T
    cos_low, sin_low = cos[...].astype(low), sin[...].astype(low)
    cost_low, sint_low = cos_t[...].astype(low), sin_t[...].astype(low)
    dqs, dks, dvs, gbks = [], [], [], []
    for j in range(2):
        at = slice(j * HEAD_DIM, (j + 1) * HEAD_DIM)
        weights = probs[j]
        wide = weights.astype(f32)
        dprobs = dot(dctx2[:, at], vt2[at])
        inner = jnp.sum(wide * dprobs, -1, keepdims=True)
        draw = (scale * (wide * (dprobs - inner))).astype(low)
        dvs.append(dot(dctxt2[at], weights))
        g_u, g_l = dot(draw, sin_low), dot(draw, cos_low)
        da_u = (g_u * cos[...] - g_l * sin[...]).astype(low)
        da_l = (g_u * sin[...] + g_l * cos[...]).astype(low)
        dqs.append(dot(draw, k2[:, at]) + dot(da_u, bk2[:half, at]) + dot(da_l, bk2[half:, at]))
        gbks.append(jnp.concatenate([dot(qt2[at], da_u), dot(qt2[at], da_l)], 1))
        g_u, g_l = dot(cost_low, draw), dot(sint_low, draw)
        db_u = (g_u * sin_t[...] - g_l * cos_t[...]).astype(low)
        db_l = (g_u * cos_t[...] + g_l * sin_t[...]).astype(low)
        dks.append(dot(qt2[at], draw) + dot(bqt2[at, :half], db_u) + dot(bqt2[at, half:], db_l))
        gbq_o[:half, at] = dot(db_u, k2[:, at]).astype(low)
        gbq_o[half:, at] = dot(db_l, k2[:, at]).astype(low)
    dq_o[...] = jnp.concatenate(dqs, 1).astype(low)
    dk_o[...] = jnp.concatenate(dks, 0).astype(low).T
    dv_o[...] = jnp.concatenate(dvs, 0).astype(low).T
    gbk_o[...] = jnp.concatenate(gbks, 0).astype(low)


def attend_back(scal, dctx, probs, q, k, v, tables, parts):
    length = dctx.shape[0]
    hc = parts[0].shape[2] // 6
    heads = 2 * hc // HEAD_DIM
    half = tables[0].shape[1]
    width = 2 * half
    pair = pl.BlockSpec((length, 2 * HEAD_DIM), lambda p: (0, p))
    flops = 2 * length * heads * (8 * half * HEAD_DIM + length * (4 * half + 4 * HEAD_DIM))
    return call(
        functools.partial(attend_back_kernel, grid_dp(), len(parts), HEAD_DIM**-0.5),
        "attend_back",
        flops,
        15e6,
        [shape(length, 2 * hc)] * 3 + [shape(2 * hc, width), shape(width, 2 * hc)],
        [pair] * 3
        + [pl.BlockSpec((2 * HEAD_DIM, width), lambda p: (p, 0)), pl.BlockSpec((width, 2 * HEAD_DIM), lambda p: (0, p))],
        [SMEM, pair, pl.BlockSpec((2, length, length), lambda p: (p, 0, 0))] + [pair] * 3 + [VMEM] * 4 + [ANYWHERE] * len(parts),
        [
            pltpu.VMEM((2, width, 2 * hc), low),
            pltpu.VMEM((width, 2 * hc), low),
            pltpu.VMEM((2 * hc, width), low),
            COPIES,
        ],
        (scal, dctx, probs, q, k, v, *tables, *parts),
        (heads // 2,),
    )


def project_back_kernel(dims, count, scal, rows_t, dq, dk, dv, gbk, gbq, *refs):
    sums_o, outs, (box, proj, sems, more_sems) = refs[0], refs[1 : 1 + count], refs[1 + count :]
    place = (scal[0], scal[1])
    hc = box.shape[2] // 2
    for side in range(2):
        at = slice(side * hc, (side + 1) * hc)
        box[side, :, :hc] = gbk[at].T
        box[side, :, hc:] = gbq[:, at]
    first = deal(box, outs, sems, place, dims, True, (0, 2 * hc))
    for i, ref in enumerate((dq, dk, dv)):
        value = ref[...]
        sums_o[i : i + 1] = col(value.astype(f32))
        grad = dot(rows_t[...], value).astype(low)
        for side in range(2):
            proj[side, :, i * hc : (i + 1) * hc] = grad[:, side * hc : (side + 1) * hc]
    second = deal(proj, outs, more_sems, place, dims, False, (2 * hc, 3 * hc))
    finish(first)
    finish(second)


def project_back(scal, rows_t, dq, dk, dv, gbk, gbq):
    width, length = rows_t.shape
    hc = dq.shape[1] // 2
    parts = part_shapes(width, 5 * hc)
    out = call(
        functools.partial(project_back_kernel, grid_dp(), len(parts)),
        "project_back",
        12 * length * width * hc,
        6e6,
        [shape(3, 2 * hc, dtype=f32)] + parts,
        [VMEM] + [ANYWHERE] * len(parts),
        [SMEM] + [VMEM] * 6,
        [pltpu.VMEM((2, width, 2 * hc), low), pltpu.VMEM((2, width, 3 * hc), low), COPIES, COPIES],
        (scal, rows_t, dq, dk, dv, gbk, gbq),
    )
    return out[0], out[1:]


def tokens_back_kernel(dims, count, scal, dq, dk, dv, *refs):
    parts, (part_o, proj, sems) = refs[:count], refs[count:]
    hc = proj.shape[2] // 4
    finish(fetch(parts, proj, sems, (scal[0], scal[1]), dims, False, (2 * hc, 4 * hc)))
    total = None
    for side in range(2):
        at = slice(side * hc, (side + 1) * hc)
        grads = jnp.concatenate([dq[:, at], dk[:, at], dv[:, at]], 1)
        term = dot(grads, proj[side, :, : 3 * hc], NT)
        total = term if total is None else total + term
    part_o[...] = total.astype(low)


def tokens_back(scal, dq, dk, dv, parts):
    length = dq.shape[0]
    hc = dq.shape[1] // 2
    width = parts[0].shape[1] * grid_dp()[0] * grid_dp()[1]
    return call(
        functools.partial(tokens_back_kernel, grid_dp(), len(parts)),
        "tokens_back",
        12 * length * width * hc,
        5e6,
        shape(length, width),
        VMEM,
        [SMEM] + [VMEM] * 3 + [ANYWHERE] * len(parts),
        [pltpu.VMEM((2, width, 4 * hc), low), COPIES],
        (scal, dq, dk, dv, *parts),
    )


def sum_dp(a):
    n = lax.axis_size("dp")
    bit = 1
    while bit < n:
        a = a + swap_dp(a, bit)
        bit *= 2
    return a


def local(
    tokens, lengths, boxes, query_weight, key_weight, value_weight, query_bias, key_bias, value_bias,
    box_key_weight, box_query_weight, out_weight, out_bias, first_gain, first_shift, up_weight, up_bias,
    down_weight, down_bias, second_gain, second_shift, output_grad,
):
    pages = lengths.shape[0]
    page_len = tokens.shape[0] // pages
    width = tokens.shape[1]
    hc = query_weight.shape[1]
    units = up_weight.shape[1]

    first = jnp.concatenate(
        [box_key_weight, box_query_weight, query_weight, key_weight, value_weight, out_weight.T], 1
    )
    parts_1 = gather_weights(first)
    parts_2 = gather_weights(up_weight)
    parts_3 = gather_weights(down_weight.T)
    biases = jnp.concatenate([query_bias, key_bias, value_bias, up_bias])[None].astype(low)
    biases = jnp.concatenate([biases, swap_page(biases)], 0).astype(f32)

    page = lax.axis_index("head") // (lax.axis_size("head") // pages)
    start = page * page_len
    rows = lax.dynamic_slice_in_dim(tokens, start, page_len, 0)
    grad_rows = lax.dynamic_slice_in_dim(output_grad, start, page_len, 0)
    box_rows = lax.dynamic_slice_in_dim(boxes, start, page_len, 1)
    length = lax.dynamic_slice_in_dim(lengths, page, 1, 0)[0]
    vecs_one = jnp.stack([out_bias, first_gain, first_shift]).astype(f32)
    vecs_two = jnp.stack([down_bias, second_gain, second_shift]).astype(f32)
    frequency = 10000.0 ** (-jnp.arange(width // 4, dtype=f32) / (width // 4))
    angles = (box_rows.T.astype(f32)[:, :, None] * frequency).reshape(page_len, width // 2)
    cosine, sine = jnp.cos(angles), jnp.sin(angles)
    tables = (cosine, sine, cosine.T, sine.T)
    z, y = place_dp()
    scal = jnp.stack([z, y, length]).astype(jnp.int32)

    query, key, value, context, probs, mine = attend(scal, rows, biases[:, : 3 * hc], tables, parts_1)
    hidden, hidden_low, scaled_one, inverse_one, active, slope, feed = feed_forward(
        scal, mine, swap_core(mine), rows, vecs_one, biases[:, 3 * hc :], parts_2, parts_3
    )
    (result, grad_two, feed_low, sums_two), grads_3 = feed_back(
        scal, feed, swap_core(feed), hidden, grad_rows, vecs_two, active
    )
    sum_3 = scatter_grads(grads_3)
    grad_inner, sums_up, mine = inner_back(scal, feed_low, slope, parts_3, parts_2)
    (grad_one, grad_context, sums_one), grads_2 = norm_back(
        scal, mine, swap_core(mine), grad_two, scaled_one, inverse_one, vecs_one, hidden_low, grad_inner, context, parts_1
    )
    sum_2 = scatter_grads(grads_2)
    dq, dk, dv, gbk, gbq = attend_back(scal, grad_context, probs, query, key, value, tables, parts_1)
    sums_qkv, grads_1 = project_back(scal, rows.T, dq, dk, dv, gbk, gbq)
    sum_1 = scatter_grads(grads_1)
    mine = tokens_back(scal, dq, dk, dv, parts_1)
    token_grad = (grad_one + (mine.astype(f32) + swap_core(mine).astype(f32))).astype(low)

    norms = jnp.concatenate([sums_one, sums_two], 0).reshape(-1)
    own_b = jnp.concatenate([sums_qkv[:, :hc].reshape(-1), sums_up[0]])
    oth_b = jnp.concatenate([sums_qkv[:, hc:].reshape(-1), sums_up[1]])
    size = own_b.shape[0]
    small = jnp.concatenate([own_b, norms])[None]
    small = sum_dp(small + swap_page(jnp.concatenate([oth_b, norms])[None]))[0]
    bias_q, bias_k, bias_v = (small[i * hc : (i + 1) * hc] for i in range(3))
    norms = [small[size + i * width : size + (i + 1) * width] for i in range(6)]

    def rows_of(mine):
        theirs = swap_page(mine)
        both = jnp.zeros((pages * page_len, width), low)
        both = lax.dynamic_update_slice(both, mine, (start, 0))
        return lax.dynamic_update_slice(both, theirs, (page_len - start, 0))

    return (
        rows_of(result),
        rows_of(token_grad),
        sum_1[:, 2 * hc : 3 * hc],
        sum_1[:, 3 * hc : 4 * hc],
        sum_1[:, 4 * hc :],
        bias_q,
        bias_k,
        bias_v,
        sum_1[:, :hc],
        sum_1[:, hc : 2 * hc],
        sum_2[:, units:].T,
        norms[0],
        norms[1],
        norms[2],
        sum_2[:, :units],
        small[3 * hc : size],
        sum_3.T,
        norms[3],
        norms[4],
        norms[5],
    )


def solution(mesh):
    row, vec, mat, tam, all_ = P("dp", None), P("head"), P("dp", "head"), P("head", "dp"), P()
    return jax.shard_map(
        local,
        mesh=mesh,
        in_specs=(
            row, P("dp"), P(None, "dp"), mat, mat, mat, vec, vec, vec, mat, mat, tam, all_, all_, all_,
            mat, vec, tam, all_, all_, all_, row,
        ),
        out_specs=(
            row, row, mat, mat, mat, vec, vec, vec, mat, mat, tam, all_, all_, all_, mat, vec, tam,
            all_, all_, all_,
        ),
        check_vma=False,
    )
```

```python
import functools

import jax
import jax.numpy as jnp
from jax import lax
from jax.experimental import pallas as pl
from jax.experimental.pallas import tpu as pltpu
from jax.sharding import PartitionSpec as P

HEAD_DIM = 64
norm_eps = 1e-05
sqrt_half = 0.7071067811865476
inv_root_two_pi = 0.3989422804014327
low = jnp.bfloat16
f32 = jnp.float32


def dot(left, right, axes=((1,), (0,))):
    return lax.dot_general(left, right, (axes, ((), ())), preferred_element_type=f32)


def permute(a, axis, name, partner):
    pairs = [(i, partner(i)) for i in range(lax.axis_size(axis))]
    with jax.named_scope("%s_%d_%d" % (name, a.shape[0], a.shape[-1])):
        return lax.ppermute(a, axis, pairs)


def swap_core(a):
    return permute(a, "head", "core", lambda i: i ^ 1)


def swap_page(a):
    return permute(a, "head", "page", lambda i: i ^ 2)


def swap_dp(a, bit):
    return permute(a, "dp", "column", lambda i: i ^ bit)


def turn_dp(a, step):
    n = lax.axis_size("dp")
    return permute(a, "dp", "line", lambda i: (i + step) % n)


VMEM_LIMIT = 56 * 1024 * 1024
BLOCKS = 8


def grid_dp():
    return (4, 2) if lax.axis_size("dp") == 8 else (1, 1)


def place_dp():
    index = lax.axis_index("dp")
    return (index // 2, index % 2) if lax.axis_size("dp") == 8 else (index * 0, index * 0)


def after(value, *done):
    return lax.optimization_barrier((value, *done))[0] if done else value


def block_plan(kind):
    nz, ny = grid_dp()
    if nz == 1:
        return (((0, 0, 0),), ((1, 0, 0),))
    half = nz // 2

    def run(side, ky, start, end):
        return tuple((side, ky, k) for k in range(start, end))

    far = (run(1, 1, 0, half), run(1, 1, half, nz))
    if kind == "early":
        return tuple(run(*block, *cut) for cut in ((0, 1), (1, nz)) for block in ((0, 0), (1, 0), (0, 1))) + far
    if kind == "scatter":
        return (run(0, 0, 0, nz),) + tuple(run(*block, *cut) for block in ((1, 0), (0, 1)) for cut in ((0, half), (half, nz))) + far
    return tuple(run(*block, 0, nz) for block in ((0, 0), (1, 0), (0, 1))) + far


def gather_line(shard):
    nz, ny = grid_dp()
    if nz == 1:
        return [lax.all_gather(shard, "dp", axis=0, tiled=True)[None]]
    return [shard[None]] + [turn_dp(shard, ny * k)[None] for k in range(1, nz)]


def gather_near(line):
    if grid_dp()[0] == 1:
        return [line, swap_page(line)]
    return [line, swap_page(line), swap_dp(line, 1)]


def gather_far(parts, done=()):
    half = grid_dp()[0] // 2
    if half == 0:
        return parts
    line, across, beside = parts
    far_a, far_b = after((across[:half], beside[half:]), *done)
    return [line, across, beside, swap_dp(far_a, 1), swap_page(far_b)]


def gather_early(line, near_done, far_done):
    nz = grid_dp()[0]
    if nz == 1:
        return gather_near(line[0])
    own = gather_near(line[0])
    rest = gather_near(after(jnp.concatenate(line[1:], 0), *own, *near_done))
    cut = nz // 2 - 1
    far_a, far_b = after((jnp.concatenate([own[1], rest[1][:cut]], 0), rest[2][cut:]), *rest[1:], *far_done)
    return own + rest + [swap_dp(far_a, 1), swap_page(far_b)]


def add(a, b):
    return (a.astype(f32) + b.astype(f32)).astype(low)


def scatter_far(parts):
    if grid_dp()[0] == 1:
        return parts
    line, across_a, across_b, beside_a, beside_b, far_a, far_b = parts
    far_a = swap_page(far_a)
    far_b = swap_dp(far_b, 1)
    beside = jnp.concatenate([add(beside_a, far_a), beside_b], 0)
    across = jnp.concatenate([across_a, add(across_b, far_b)], 0)
    return [line, across, beside]


def scatter_near(parts):
    line = parts[0].astype(f32) + swap_page(parts[1]).astype(f32)
    if len(parts) > 2:
        line = line + swap_dp(parts[2], 1).astype(f32)
    return [line[0]] + [line[k].astype(low) for k in range(1, line.shape[0])]


def scatter_line(line):
    if grid_dp()[0] == 1:
        return lax.psum_scatter(line[0].astype(low), "dp", scatter_dimension=0, tiled=True).astype(f32)
    total = line[0]
    for k in range(1, len(line)):
        total = total + turn_dp(line[k], grid_dp()[1] * k).astype(f32)
    return total


def part_shapes(blocks, width):
    nz, ny = grid_dp()
    return [jax.ShapeDtypeStruct((len(p), blocks // (nz * ny), width), low) for p in block_plan("scatter")]


def slots(parts, place, dims, sign, turned, plan):
    nz, ny = dims
    found = []
    for part, blocks in zip(parts, plan):
        for i, (side, ky, kz) in enumerate(blocks):
            piece = part.at[i]
            rows = piece.shape[0]
            z = lax.rem(place[0] + (sign * kz) % nz, nz) if nz > 1 else 0
            y = lax.rem(place[1] + ky, ny) if ny > 1 else 0
            block = z * ny + y
            if not turned:
                found.append((piece, side, pl.multiple_of(block * rows, rows)))
                continue
            size = rows * nz * ny // BLOCKS
            for sub in range(rows // size):
                b = block * (rows // size) + sub
                b = lax.rem(lax.div(b, 2), 2) * 4 + lax.div(b, 4) * 2 + lax.rem(b, 2)
                found.append((piece.at[pl.ds(sub * size, size)], side, pl.multiple_of(b * size, size)))
    return found


def fetch(parts, whole, sems, place, plan, turned=False, columns=None, start=True):
    dims, plan = plan
    copies = []
    for i, (piece, side, row) in enumerate(slots(parts, place, dims, -1, turned, plan)):
        source = piece if columns is None else piece.at[:, pl.ds(columns[0], columns[1])]
        copies.append(pltpu.make_async_copy(source, whole.at[side, pl.ds(row, piece.shape[0])], sems.at[i]))
    for copy in copies if start else []:
        copy.start()
    return copies


def deal(whole, parts, sems, place, plan, turned=False, columns=None):
    dims, plan = plan
    copies = []
    for i, (piece, side, row) in enumerate(slots(parts, place, dims, 1, turned, plan)):
        target = piece if columns is None else piece.at[:, pl.ds(columns[0], columns[1])]
        copies.append(pltpu.make_async_copy(whole.at[side, pl.ds(row, piece.shape[0])], target, sems.at[i]))
    for copy in copies:
        copy.start()
    return copies


def plans(kind):
    return grid_dp(), block_plan(kind)


def finish(copies):
    for copy in copies:
        copy.wait()


SMEM = pl.BlockSpec(memory_space=pltpu.SMEM)
VMEM = pl.BlockSpec(memory_space=pltpu.VMEM)
ANYWHERE = pl.BlockSpec(memory_space=pl.ANY)
COPIES = pltpu.SemaphoreType.DMA((2 * BLOCKS,))


def call(kernel, name, flops, moved, outs, out_specs, in_specs, scratch, args, grid=None, exps=0, done=()):
    extra = {} if grid is None else {"grid": grid}

    def body(*refs):
        kernel(*refs[: len(args)], *refs[len(args) + len(done) :])

    return pl.pallas_call(
        body,
        out_shape=outs,
        in_specs=in_specs + [ANYWHERE] * len(done),
        out_specs=out_specs,
        scratch_shapes=scratch,
        compiler_params=pltpu.CompilerParams(vmem_limit_bytes=VMEM_LIMIT),
        cost_estimate=pl.CostEstimate(flops=int(flops), bytes_accessed=int(moved), transcendentals=int(exps)),
        name=name,
        **extra,
    )(*args, *done)


def shape(*dims, dtype=low):
    return jax.ShapeDtypeStruct(dims, dtype)


NT = ((1,), (1,))


def project_kernel(count, plan, scal, rows, bias, *refs):
    parts, refs = refs[:count], refs[count:]
    (q_o, k_o, v_o, key_t, bk_t, bq, bk, bq_t), (box, proj, sems, more_sems) = refs[:8], refs[8:]
    hc = box.shape[2] // 2
    place = (scal[0], scal[1])
    first = fetch(parts, proj, more_sems, place, plan, False, (2 * hc, 4 * hc))
    second = fetch(parts, box, sems, place, plan, True, (0, 2 * hc))
    finish(first)
    heads = hc // HEAD_DIM
    pairs = [[], [], []]
    for side in range(2):
        qkv = (dot(rows[...], proj[side, :, : 3 * hc]) + bias[side : side + 1]).astype(low)
        for i in range(3):
            pairs[i].append(qkv[:, i * hc : (i + 1) * hc])

    def paired(own, other, axis):
        cut = [slice(h * HEAD_DIM, (h + 1) * HEAD_DIM) for h in range(heads)]
        both = [(own[c], other[c]) if axis == 0 else (own[:, c], other[:, c]) for c in cut]
        return jnp.concatenate([one for two in both for one in two], axis)

    for ref, two in zip((q_o, k_o, v_o), pairs):
        ref[...] = paired(*two, 1)
    key_t[...] = k_o[...].T
    finish(second)
    bk[...] = paired(box[0, :, :hc], box[1, :, :hc], 1)
    bq[...] = paired(box[0, :, hc:], box[1, :, hc:], 1)
    bk_t[...] = bk[...].T
    bq_t[...] = bq[...].T


def project(scal, rows, bias, parts, done=()):
    length, width = rows.shape
    hc = parts[0].shape[2] // 6
    return call(
        functools.partial(project_kernel, len(parts), plans("early")),
        "project",
        12 * length * width * hc,
        10e6,
        [shape(length, 2 * hc)] * 3 + [shape(2 * hc, length), shape(2 * hc, width), shape(width, 2 * hc)]
        + [shape(width, 2 * hc), shape(2 * hc, width)],
        [VMEM] * 8,
        [SMEM, VMEM, VMEM] + [ANYWHERE] * len(parts),
        [pltpu.VMEM((2, width, 2 * hc), low), pltpu.VMEM((2, width, 4 * hc), low), COPIES, COPIES],
        (scal, rows, bias, *parts),
        done=done,
    )


def attend_pair(scale, length, q, v, key_t, bk_t, bq, cos, sin, cos_t, sin_t, p_o):
    half = cos.shape[1]
    cos_low, sin_low = cos[...].astype(low), sin[...].astype(low)
    cost_low, sint_low = cos_t[...].astype(low), sin_t[...].astype(low)
    valid = lax.broadcasted_iota(jnp.int32, (1, key_t.shape[1]), 1) < length
    outs = []
    for j in range(2):
        at = slice(j * HEAD_DIM, (j + 1) * HEAD_DIM)
        a = dot(q[:, at], bk_t[at])
        a_s, a_c = a[:, :half], a[:, half:]
        raw = dot(q[:, at], key_t[at])
        raw = raw + dot((a_s * cos[...] + a_c * sin[...]).astype(low), sint_low)
        raw = raw + dot((a_c * cos[...] - a_s * sin[...]).astype(low), cost_low)
        b = dot(bq[:, at], key_t[at])
        b_s, b_c = b[:half], b[half:]
        raw = raw + dot(cos_low, (b_s * sin_t[...] + b_c * cos_t[...]).astype(low))
        raw = raw + dot(sin_low, (b_c * sin_t[...] - b_s * cos_t[...]).astype(low))
        scores = jnp.where(valid, raw * scale, -1e9)
        exponent = jnp.exp(scores - jnp.max(scores, -1, keepdims=True))
        probs = (exponent / jnp.sum(exponent, -1, keepdims=True)).astype(low)
        p_o[j] = probs
        outs.append(dot(probs, v[:, at]))
    return jnp.concatenate(outs, 1).astype(low)


def attend_kernel(scale, scal, q, v, key_t, bk_t, bq, cos, sin, cos_t, sin_t, ctx_o, p_o):
    ctx_o[...] = attend_pair(scale, scal[2], q, v, key_t, bk_t, bq, cos, sin, cos_t, sin_t, p_o)


def attend_last_kernel(
    scale, count, plan, scal, q, v, key_t, bk_t, bq, cos, sin, cos_t, sin_t, ctx_a, *refs
):
    parts, (part_o, ctx_o, p_o, out_w, pairs, sems) = refs[:count], refs[count:]
    step = pl.program_id(0)
    hc = out_w.shape[2] // 2

    @pl.when(step == 0)
    def _():
        fetch(parts, out_w, sems, (scal[0], scal[1]), plan, False, (4 * hc, 2 * hc))

    pairs[step] = attend_pair(scale, scal[2], q, v, key_t, bk_t, bq, cos, sin, cos_t, sin_t, p_o)

    @pl.when(step == pl.num_programs(0) - 1)
    def _():
        ctx = jnp.concatenate([ctx_a[...]] + [pairs[i] for i in range(pairs.shape[0])], 1)
        both = [sides(ctx, side) for side in range(2)]
        ctx_o[...] = jnp.concatenate(both, 1)
        finish(fetch(parts, out_w, sems, (scal[0], scal[1]), plan, False, (4 * hc, 2 * hc), False))
        part_o[...] = (dot(both[0], out_w[0, :, hc:], NT) + dot(both[1], out_w[1, :, hc:], NT)).astype(low)


def attend_specs(first, length, half):
    two = 2 * HEAD_DIM
    wide = pl.BlockSpec((length, two), lambda p: (0, first + p))
    return [
        SMEM,
        wide,
        wide,
        pl.BlockSpec((two, length), lambda p: (first + p, 0)),
        pl.BlockSpec((two, 2 * half), lambda p: (first + p, 0)),
        pl.BlockSpec((2 * half, two), lambda p: (0, first + p)),
    ] + [VMEM] * 4


def attend_flops(count, length, half):
    return 4 * count * length * (4 * half * HEAD_DIM + length * (4 * half + 2 * HEAD_DIM))


def attend(count, scal, q, v, key_t, bk_t, bq, tables, done=()):
    length, half = tables[0].shape
    two = 2 * HEAD_DIM
    return call(
        functools.partial(attend_kernel, HEAD_DIM**-0.5),
        "attend",
        attend_flops(count, length, half),
        count * 2e6,
        [shape(length, count * two), shape(2 * count, length, length)],
        [pl.BlockSpec((length, two), lambda p: (0, p)), pl.BlockSpec((2, length, length), lambda p: (p, 0, 0))],
        attend_specs(0, length, half),
        [],
        (scal, q, v, key_t, bk_t, bq, *tables),
        (count,),
        2 * count * length * length,
        done,
    )


def attend_last(first, scal, q, v, key_t, bk_t, bq, tables, ctx_a, parts, done=()):
    length, half = tables[0].shape
    width, hc = 2 * half, parts[0].shape[2] // 6
    count = hc // HEAD_DIM - first
    two = 2 * HEAD_DIM
    return call(
        functools.partial(attend_last_kernel, HEAD_DIM**-0.5, len(parts), plans("early")),
        "attend_last",
        attend_flops(count, length, half),
        count * 2e6,
        [shape(length, width), shape(length, 2 * hc), shape(2 * count, length, length)],
        [
            pl.BlockSpec((length, width), lambda p: (0, 0)),
            pl.BlockSpec((length, 2 * hc), lambda p: (0, 0)),
            pl.BlockSpec((2, length, length), lambda p: (p, 0, 0)),
        ],
        attend_specs(first, length, half) + [VMEM] + [ANYWHERE] * len(parts),
        [pltpu.VMEM((2, width, 2 * hc), low), pltpu.VMEM((count, length, two), low), COPIES],
        (scal, q, v, key_t, bk_t, bq, *tables, ctx_a, *parts),
        (count,),
        2 * count * length * length,
        done,
    )


def sides(values, side):
    heads = values.shape[1] // HEAD_DIM
    return jnp.concatenate([values[:, h * HEAD_DIM : (h + 1) * HEAD_DIM] for h in range(side, heads, 2)], 1)


def tables_kernel(boxes, frequency, cos_o, sin_o, cost_o, sint_o):
    width = frequency.shape[1]
    for c in range(2):
        at = slice(c * width, (c + 1) * width)
        angles = boxes[:, c : c + 1] * frequency[...]
        cos_o[:, at] = jnp.cos(angles)
        sin_o[:, at] = jnp.sin(angles)
    cost_o[...] = cos_o[...].T
    sint_o[...] = sin_o[...].T


def box_tables(boxes, frequency):
    length, half = boxes.shape[0], 2 * frequency.shape[1]
    return call(
        tables_kernel,
        "box_tables",
        40 * length * half,
        3e6,
        [shape(length, half, dtype=f32)] * 2 + [shape(half, length, dtype=f32)] * 2,
        [VMEM] * 4,
        [VMEM] * 2,
        [],
        (boxes, frequency),
    )


def standard(values):
    centered = values - jnp.mean(values, -1, keepdims=True)
    inverse = lax.rsqrt(jnp.mean(centered * centered, -1, keepdims=True) + norm_eps)
    return centered * inverse, inverse


def standard_back(upstream, scaled, inverse):
    return inverse * (
        upstream - jnp.mean(upstream, -1, keepdims=True) - scaled * jnp.mean(upstream * scaled, -1, keepdims=True)
    )


def col(values):
    return jnp.sum(values, 0, keepdims=True)


def feed_up_kernel(count, plan, scal, mine, theirs, rows, vecs, bias, *refs):
    ups, refs = refs[:count], refs[count:]
    (hidden_o, low_o, scaled_o, inverse_o, active_o, slope_o), (up, sems) = refs[:6], refs[6:]
    copies = fetch(ups, up, sems, (scal[0], scal[1]), plan)
    total = rows[...].astype(f32) + (mine[...].astype(f32) + theirs[...].astype(f32)) + vecs[0:1]
    scaled, inverse = standard(total)
    hidden = scaled * vecs[1:2] + vecs[2:3]
    hidden_o[...] = hidden
    scaled_o[...] = scaled
    inverse_o[...] = inverse
    hidden_low = hidden.astype(low)
    low_o[...] = hidden_low
    finish(copies)
    width = up.shape[2]
    size = 256
    for side in range(2):
        for at in range(0, width, size):
            inner = dot(hidden_low, up[side, :, at : at + size]) + bias[side : side + 1, at : at + size]
            cumulative = 0.5 * (1.0 + lax.erf(inner * sqrt_half))
            density = jnp.exp(-0.5 * inner * inner) * inv_root_two_pi
            active_o[:, side * width + at : side * width + at + size] = (inner * cumulative).astype(low)
            slope_o[:, side * width + at : side * width + at + size] = (cumulative + inner * density).astype(low)


def feed_up(scal, mine, theirs, rows, vecs, bias, ups, done=()):
    length, width = rows.shape
    units = ups[0].shape[2]
    return call(
        functools.partial(feed_up_kernel, len(ups), plans("gather")),
        "feed_up",
        4 * length * width * units,
        11e6,
        [
            shape(length, width, dtype=f32),
            shape(length, width),
            shape(length, width, dtype=f32),
            shape(length, 1, dtype=f32),
            shape(length, 2 * units),
            shape(length, 2 * units),
        ],
        [VMEM] * 6,
        [SMEM] + [VMEM] * 5 + [ANYWHERE] * len(ups),
        [pltpu.VMEM((2, width, units), low), COPIES],
        (scal, mine, theirs, rows, vecs, bias, *ups),
        exps=2 * length * units,
        done=done,
    )


def feed_down_kernel(count, plan, scal, active, *refs):
    downs, (part_o, down, sems) = refs[:count], refs[count:]
    finish(fetch(downs, down, sems, (scal[0], scal[1]), plan))
    units = down.shape[2]
    part_o[...] = (dot(active[:, :units], down[0], NT) + dot(active[:, units:], down[1], NT)).astype(low)


def feed_down(scal, active, downs, width, done=()):
    length, units = active.shape[0], active.shape[1] // 2
    return call(
        functools.partial(feed_down_kernel, len(downs), plans("gather")),
        "feed_down",
        4 * length * width * units,
        5e6,
        shape(length, width),
        VMEM,
        [SMEM, VMEM] + [ANYWHERE] * len(downs),
        [pltpu.VMEM((2, width, units), low), COPIES],
        (scal, active, *downs),
        done=done,
    )


def feed_back_kernel(count, plan, scal, mine, theirs, hidden, grad_out, vecs, active, *refs):
    (result_o, grad_o, low_o, sums_o), outs, (grads, sems) = refs[:4], refs[4 : 4 + count], refs[4 + count :]
    scaled, inverse = standard(hidden[...] + (mine[...].astype(f32) + theirs[...].astype(f32)) + vecs[0:1])
    result_o[...] = (scaled * vecs[1:2] + vecs[2:3]).astype(low)
    grad = grad_out[...].astype(f32)
    sums_o[1:2] = col(grad * scaled)
    sums_o[2:3] = col(grad)
    grad = standard_back(grad * vecs[1:2], scaled, inverse)
    sums_o[0:1] = col(grad)
    grad_o[...] = grad
    grad_low = grad.astype(low)
    low_o[...] = grad_low
    turned = grad_low.T
    units = grads.shape[2]
    for side in range(2):
        grads[side] = dot(turned, active[:, side * units : (side + 1) * units]).astype(low)
    finish(deal(grads, outs, sems, (scal[0], scal[1]), plan))


def feed_back(scal, mine, theirs, hidden, grad_out, vecs, active):
    length, width = hidden.shape
    units = active.shape[1] // 2
    parts = part_shapes(width, units)
    out = call(
        functools.partial(feed_back_kernel, len(parts), plans("scatter")),
        "feed_back",
        4 * length * width * units,
        12e6,
        [shape(length, width), shape(length, width, dtype=f32), shape(length, width), shape(3, width, dtype=f32)] + parts,
        [VMEM] * 4 + [ANYWHERE] * len(parts),
        [SMEM] + [VMEM] * 6,
        [pltpu.VMEM((2, width, units), low), COPIES],
        (scal, mine, theirs, hidden, grad_out, vecs, active),
    )
    return out[:4], out[4:]


def inner_back_kernel(count, plan, scal, grad_low, slope, *refs):
    downs, ups, refs = refs[:count], refs[count : 2 * count], refs[2 * count :]
    (inner_o, sums_o, part_o), (down, up, sems, more_sems) = refs[:3], refs[3:]
    place = (scal[0], scal[1])
    first = fetch(downs, down, sems, place, plan)
    second = fetch(ups, up, more_sems, place, plan)
    finish(first)
    units = up.shape[2]
    for side in range(2):
        at = slice(side * units, (side + 1) * units)
        grad = (dot(grad_low[...], down[side]) * slope[:, at].astype(f32)).astype(low)
        inner_o[:, at] = grad
        sums_o[side : side + 1] = col(grad.astype(f32))
    finish(second)
    part = dot(inner_o[:, :units], up[0], NT) + dot(inner_o[:, units:], up[1], NT)
    part_o[...] = part.astype(low)


def inner_back(scal, grad_low, slope, downs, ups):
    length, width = grad_low.shape
    units = slope.shape[1] // 2
    return call(
        functools.partial(inner_back_kernel, len(ups), plans("gather")),
        "inner_back",
        8 * length * width * units,
        10e6,
        [shape(length, 2 * units), shape(2, units, dtype=f32), shape(length, width)],
        [VMEM] * 3,
        [SMEM] + [VMEM] * 2 + [ANYWHERE] * (2 * len(ups)),
        [pltpu.VMEM((2, width, units), low)] * 2 + [COPIES] * 2,
        (scal, grad_low, slope, *downs, *ups),
    )


def norm_back_kernel(count, given, plan, given_plan, scal, mine, theirs, grad_two, scaled, inverse, vecs, hidden_low, grad_inner, ctx, *refs):
    weights, refs = refs[:given], refs[given:]
    (grad_o, dctx_o, sums_o), outs, (out_w, grads, sems) = refs[:3], refs[3 : 3 + count], refs[3 + count :]
    place = (scal[0], scal[1])
    hc = out_w.shape[2] // 2
    copies = fetch(weights, out_w, sems, place, given_plan, False, (4 * hc, 2 * hc))
    grad = grad_two[...] + (mine[...].astype(f32) + theirs[...].astype(f32))
    sums_o[1:2] = col(grad * scaled[...])
    sums_o[2:3] = col(grad)
    grad = standard_back(grad * vecs[1:2], scaled[...], inverse[...])
    sums_o[0:1] = col(grad)
    grad_o[...] = grad
    grad_low = grad.astype(low)
    finish(copies)
    both = [dot(grad_low, out_w[side, :, hc:]).astype(low) for side in range(2)]
    cut = [slice(h * HEAD_DIM, (h + 1) * HEAD_DIM) for h in range(hc // HEAD_DIM)]
    dctx_o[...] = jnp.concatenate([one[:, c] for c in cut for one in both], 1)
    units = grads.shape[2] - hc
    turned = hidden_low[...].T
    for side in range(2):
        grads[side, :, :units] = dot(turned, grad_inner[:, side * units : (side + 1) * units]).astype(low)
    grad_ctx = dot(grad_low.T, ctx[...]).astype(low)
    for side in range(2):
        grads[side, :, units:] = grad_ctx[:, side * hc : (side + 1) * hc]
    finish(deal(grads, outs, sems, place, plan))


def norm_back(scal, mine, theirs, grad_two, scaled, inverse, vecs, hidden_low, grad_inner, ctx, weights, done=()):
    length, width = grad_two.shape
    units, hc = grad_inner.shape[1] // 2, ctx.shape[1] // 2
    parts = part_shapes(width, units + hc)
    out = call(
        functools.partial(norm_back_kernel, len(parts), len(weights), plans("scatter"), plans("early")),
        "norm_back",
        4 * length * width * (units + 2 * hc),
        14e6,
        [shape(length, width, dtype=f32), shape(length, 2 * hc), shape(3, width, dtype=f32)] + parts,
        [VMEM] * 3 + [ANYWHERE] * len(parts),
        [SMEM] + [VMEM] * 9 + [ANYWHERE] * len(weights),
        [pltpu.VMEM((2, width, 2 * hc), low), pltpu.VMEM((2, width, units + hc), low), COPIES],
        (scal, mine, theirs, grad_two, scaled, inverse, vecs, hidden_low, grad_inner, ctx, *weights),
        done=done,
    )
    return out[:3], out[3:]


def attend_back_kernel(scale, scal, dctx, probs, q, k, v, bk, bq_t, cos, sin, cos_t, sin_t, dq_o, dk_o, dv_o, gbk_o, gbq_o):
    half = cos.shape[1]
    qt2, vt2, dctxt2 = q[...].T, v[...].T, dctx[...].T
    cos_low, sin_low = cos[...].astype(low), sin[...].astype(low)
    cost_low, sint_low = cos_t[...].astype(low), sin_t[...].astype(low)
    dqs, dks, dvs, gbks = [], [], [], []
    for j in range(2):
        at = slice(j * HEAD_DIM, (j + 1) * HEAD_DIM)
        weights = probs[j]
        wide = weights.astype(f32)
        dprobs = dot(dctx[:, at], vt2[at])
        inner = jnp.sum(wide * dprobs, -1, keepdims=True)
        draw = (scale * (wide * (dprobs - inner))).astype(low)
        dvs.append(dot(dctxt2[at], weights))
        g_u, g_l = dot(draw, sin_low), dot(draw, cos_low)
        da_u = (g_u * cos[...] - g_l * sin[...]).astype(low)
        da_l = (g_u * sin[...] + g_l * cos[...]).astype(low)
        dqs.append(dot(draw, k[:, at]) + dot(da_u, bk[:half, at]) + dot(da_l, bk[half:, at]))
        gbks.append(jnp.concatenate([dot(qt2[at], da_u), dot(qt2[at], da_l)], 1))
        g_u, g_l = dot(cost_low, draw), dot(sint_low, draw)
        db_u = (g_u * sin_t[...] - g_l * cos_t[...]).astype(low)
        db_l = (g_u * cos_t[...] + g_l * sin_t[...]).astype(low)
        dks.append(dot(qt2[at], draw) + dot(bq_t[at, :half], db_u) + dot(bq_t[at, half:], db_l))
        gbq_o[:half, at] = dot(db_u, k[:, at]).astype(low)
        gbq_o[half:, at] = dot(db_l, k[:, at]).astype(low)
    dq_o[...] = jnp.concatenate(dqs, 1).astype(low)
    dk_o[...] = jnp.concatenate(dks, 0).astype(low).T
    dv_o[...] = jnp.concatenate(dvs, 0).astype(low).T
    gbk_o[...] = jnp.concatenate(gbks, 0).astype(low)


def attend_back(first, count, scal, dctx, probs, q, k, v, bk, bq_t, tables, done=()):
    length = dctx.shape[0]
    half = tables[0].shape[1]
    width, two = 2 * half, 2 * HEAD_DIM
    pair = pl.BlockSpec((length, two), lambda p: (0, first + p))
    out = pl.BlockSpec((length, two), lambda p: (0, p))
    flops = 4 * count * length * (8 * half * HEAD_DIM + length * (4 * half + 4 * HEAD_DIM))
    return call(
        functools.partial(attend_back_kernel, HEAD_DIM**-0.5),
        "attend_back",
        flops,
        count * 2e6,
        [shape(length, count * two)] * 3 + [shape(count * two, width), shape(width, count * two)],
        [out] * 3 + [pl.BlockSpec((two, width), lambda p: (p, 0)), pl.BlockSpec((width, two), lambda p: (0, p))],
        [SMEM, pair, pl.BlockSpec((2, length, length), lambda p: (p, 0, 0))]
        + [pair] * 3
        + [pl.BlockSpec((width, two), lambda p: (0, first + p)), pl.BlockSpec((two, width), lambda p: (first + p, 0))]
        + [VMEM] * 4,
        [],
        (scal, dctx, probs, q, k, v, bk, bq_t, *tables),
        (count,),
        done=done,
    )


def project_back_kernel(count, plan, scal, rows_t, dq_a, dk_a, dv_a, dq_b, dk_b, dv_b, gbk_a, gbk_b, gbq_a, gbq_b, *refs):
    sums_o, outs, (grads, turned, sems) = refs[0], refs[1 : 1 + count], refs[1 + count :]
    size = turned.shape[2] // 2
    gbk = jnp.concatenate([gbk_a[...], gbk_b[...]], 0).T
    gbq = jnp.concatenate([gbq_a[...], gbq_b[...]], 1)
    for side in range(2):
        turned[side, :, :size] = sides(gbk, side)
        turned[side, :, size:] = sides(gbq, side)
    for i, (one, two) in enumerate(((dq_a, dq_b), (dk_a, dk_b), (dv_a, dv_b))):
        value = jnp.concatenate([one[...], two[...]], 1)
        value = jnp.concatenate([sides(value, side) for side in range(2)], 1)
        sums_o[i : i + 1] = col(value.astype(f32))
        grad = dot(rows_t[...], value).astype(low)
        for side in range(2):
            grads[side, :, (2 + i) * size : (3 + i) * size] = grad[:, side * size : (side + 1) * size]
    rows = turned.shape[1] // BLOCKS
    for b in range(BLOCKS):
        to = ((b // 2) % 2) * 4 + (b // 4) * 2 + b % 2
        for side in range(2):
            grads[side, b * rows : (b + 1) * rows, : 2 * size] = turned[side, to * rows : (to + 1) * rows]
    finish(deal(grads, outs, sems, (scal[0], scal[1]), plan))


def project_back(scal, rows_t, grads, boxes, done=()):
    width, length = rows_t.shape
    cols = grads[0].shape[1] + grads[3].shape[1]
    parts = part_shapes(width, 5 * cols // 2)
    out = call(
        functools.partial(project_back_kernel, len(parts), plans("scatter")),
        "project_back",
        6 * length * width * cols,
        cols * 15e3,
        [shape(3, cols, dtype=f32)] + parts,
        [VMEM] + [ANYWHERE] * len(parts),
        [SMEM] + [VMEM] * 11,
        [pltpu.VMEM((2, width, 5 * cols // 2), low), pltpu.VMEM((2, width, cols), low), COPIES],
        (scal, rows_t, *grads, *boxes),
        done=done,
    )
    return out[0], out[1:]


def tokens_back_kernel(count, plan, scal, dq_a, dk_a, dv_a, dq_b, dk_b, dv_b, *refs):
    parts, (part_o, proj, sems) = refs[:count], refs[count:]
    hc = proj.shape[2] // 4
    copies = fetch(parts, proj, sems, (scal[0], scal[1]), plan, False, (2 * hc, 4 * hc))
    both = [jnp.concatenate([a[...], b[...]], 1) for a, b in ((dq_a, dq_b), (dk_a, dk_b), (dv_a, dv_b))]
    grads = [jnp.concatenate([sides(g, side) for g in both], 1) for side in range(2)]
    finish(copies)
    total = dot(grads[0], proj[0, :, : 3 * hc], NT) + dot(grads[1], proj[1, :, : 3 * hc], NT)
    part_o[...] = total.astype(low)


def tokens_back(scal, grads, parts, width, done=()):
    length = grads[0].shape[0]
    hc = parts[0].shape[2] // 6
    return call(
        functools.partial(tokens_back_kernel, len(parts), plans("early")),
        "tokens_back",
        12 * length * width * hc,
        5e6,
        shape(length, width),
        VMEM,
        [SMEM] + [VMEM] * 6 + [ANYWHERE] * len(parts),
        [pltpu.VMEM((2, width, 4 * hc), low), COPIES],
        (scal, *grads, *parts),
        done=done,
    )


def sum_lines(a):
    nz, ny = grid_dp()
    parts = [turn_dp(a, ny * k) for k in range(1, nz)]
    return functools.reduce(jnp.add, parts, a)


def sum_columns(a):
    return a + swap_dp(a, 1) if grid_dp()[0] > 1 else lax.psum(a, "dp")


def local(
    tokens, lengths, boxes, query_weight, key_weight, value_weight, query_bias, key_bias, value_bias,
    box_key_weight, box_query_weight, out_weight, out_bias, first_gain, first_shift, up_weight, up_bias,
    down_weight, down_bias, second_gain, second_shift, output_grad,
):
    pages = lengths.shape[0]
    page_len = tokens.shape[0] // pages
    width = tokens.shape[1]
    hc = query_weight.shape[1]
    units = up_weight.shape[1]

    page = lax.axis_index("head") // (lax.axis_size("head") // pages)
    start = page * page_len
    rows = lax.dynamic_slice_in_dim(tokens, start, page_len, 0)
    grad_rows = lax.dynamic_slice_in_dim(output_grad, start, page_len, 0)
    box_rows = lax.dynamic_slice_in_dim(boxes, start, page_len, 1)
    length = lax.dynamic_slice_in_dim(lengths, page, 1, 0)[0]
    biases = jnp.concatenate([query_bias, key_bias, value_bias, up_bias])[None].astype(low)
    biases = jnp.concatenate([biases, swap_page(biases)], 0).astype(f32)
    vecs_one = jnp.stack([out_bias, first_gain, first_shift]).astype(f32)
    vecs_two = jnp.stack([down_bias, second_gain, second_shift]).astype(f32)
    frequency = (10000.0 ** (-jnp.arange(width // 4, dtype=f32) / (width // 4)))[None]
    z, y = place_dp()
    scal = jnp.stack([z, y, length]).astype(jnp.int32)
    rows_t = rows.T

    first = jnp.concatenate(
        [box_key_weight, box_query_weight, query_weight, key_weight, value_weight, out_weight.T], 1
    )
    line_1 = gather_line(first)
    tables = box_tables(after(box_rows.T, line_1[-1]).astype(f32), frequency)
    line_2 = gather_line(after(up_weight, *line_1[1:]))
    parts_1 = gather_early(line_1, (*tables, rows_t, rows, grad_rows, biases), line_2[1:])
    line_3 = gather_line(after(down_weight.T, *line_2[1:]))
    parts_2 = gather_near(after(jnp.concatenate(line_2, 0), *parts_1[-2:], *line_3[1:]))

    pairs = hc // HEAD_DIM
    query, key, value, key_t, bk_t, bq, bk, bq_t = project(scal, rows, biases[:, : 3 * hc], parts_1)
    parts_3 = gather_near(after(jnp.concatenate(line_3, 0), *parts_2[1:], query))
    near_2, near_3 = parts_2[1:], parts_3[1:]
    parts_2 = gather_far(parts_2)
    parts_3 = gather_far(parts_3)
    ctx_a, probs_a = attend(1, scal, query, value, key_t, bk_t, bq, tables)
    mine, context, probs_b = attend_last(1, scal, query, value, key_t, bk_t, bq, tables, ctx_a, parts_1, near_2)
    mine = after(mine, *near_3, *parts_2[3:])
    hidden, hidden_low, scaled_one, inverse_one, active, slope = feed_up(
        scal, mine, swap_core(mine), rows, vecs_one, biases[:, 3 * hc :], parts_2
    )
    feed = feed_down(scal, active, parts_3, width)
    (result, grad_two, feed_low, sums_two), grads_3 = feed_back(
        scal, feed, swap_core(feed), hidden, grad_rows, vecs_two, active
    )
    grads_3 = scatter_far(grads_3)
    grad_inner, sums_up, mine = inner_back(scal, feed_low, slope, parts_3, parts_2)
    (grad_one, grad_context, sums_one), grads_2 = norm_back(
        scal, mine, swap_core(mine), grad_two, scaled_one, inverse_one, vecs_one, hidden_low, grad_inner, context,
        parts_1, grads_3[1:],
    )
    grads_3 = scatter_near(grads_3)
    grads_2 = scatter_far(grads_2)
    *grads_a, gbk_a, gbq_a = attend_back(
        0, 1, scal, grad_context, probs_a, query, key, value, bk, bq_t, tables, grads_3
    )
    sum_3 = scatter_line(grads_3)
    *grads_b, gbk_b, gbq_b = attend_back(
        1, pairs - 1, scal, grad_context, probs_b, query, key, value, bk, bq_t, tables, (*grads_2[1:], gbk_a)
    )
    grads_2 = scatter_near(after(list(grads_2), gbk_a))
    grads = [*grads_a, *grads_b]
    sums_qkv, grads_1 = project_back(scal, rows_t, grads, [gbk_a, gbk_b, gbq_a, gbq_b], (*grads_2, sum_3))
    sum_2 = scatter_line(grads_2)
    grads_1 = scatter_far(grads_1)
    norms = jnp.concatenate([sums_one, sums_two], 0).reshape(-1)
    own_b = jnp.concatenate([sums_qkv[:, :hc].reshape(-1), sums_up[0]])
    oth_b = jnp.concatenate([sums_qkv[:, hc:].reshape(-1), sums_up[1]])
    grads_1 = after(list(grads_1), sum_2)
    mine = tokens_back(scal, grads, parts_1, width, grads_1[1:])
    theirs = swap_page(after(jnp.concatenate([oth_b, norms])[None], mine))
    small = jnp.concatenate([own_b, norms])[None] + theirs
    grads_1 = after(scatter_near(grads_1), mine)
    small = sum_columns(after(small, *grads_1))
    sum_1 = scatter_line(grads_1)
    small = sum_lines(small)[0]
    token_grad = (grad_one + (mine.astype(f32) + swap_core(mine).astype(f32))).astype(low)

    size = own_b.shape[0]
    bias_q, bias_k, bias_v = (small[i * hc : (i + 1) * hc] for i in range(3))
    norms = [small[size + i * width : size + (i + 1) * width] for i in range(6)]

    core = lax.axis_index("head") % (lax.axis_size("head") // pages)
    half = page_len // 2

    def rows_of(mine):
        sent = swap_page(lax.dynamic_slice_in_dim(mine, core * half, half, 0))
        passed = swap_core(sent)
        both = jnp.zeros((pages * page_len, width), low)
        both = lax.dynamic_update_slice(both, mine, (start, 0))
        both = lax.dynamic_update_slice(both, sent, (page_len - start + core * half, 0))
        return lax.dynamic_update_slice(both, passed, (page_len - start + half - core * half, 0))

    return (
        rows_of(after(result, *grads_1)),
        rows_of(after(token_grad, *grads_1)),
        sum_1[:, 2 * hc : 3 * hc],
        sum_1[:, 3 * hc : 4 * hc],
        sum_1[:, 4 * hc :],
        bias_q,
        bias_k,
        bias_v,
        sum_1[:, :hc],
        sum_1[:, hc : 2 * hc],
        sum_2[:, units:].T,
        norms[0],
        norms[1],
        norms[2],
        sum_2[:, :units],
        small[3 * hc : size],
        sum_3.T,
        norms[3],
        norms[4],
        norms[5],
    )


def solution(mesh):
    row, vec, mat, tam, all_ = P("dp", None), P("head"), P("dp", "head"), P("head", "dp"), P()
    return jax.shard_map(
        local,
        mesh=mesh,
        in_specs=(
            row, P("dp"), P(None, "dp"), mat, mat, mat, vec, vec, vec, mat, mat, tam, all_, all_, all_,
            mat, vec, tam, all_, all_, all_, row,
        ),
        out_specs=(
            row, row, mat, mat, mat, vec, vec, vec, mat, mat, tam, all_, all_, all_, mat, vec, tam,
            all_, all_, all_,
        ),
        check_vma=False,
    )
```

```python
import functools

import jax
import jax.numpy as jnp
from jax import lax
from jax.experimental import pallas as pl
from jax.experimental.pallas import tpu as pltpu
from jax.sharding import PartitionSpec as P

HEAD_DIM = 64
norm_eps = 1e-05
sqrt_half = 0.7071067811865476
inv_root_two_pi = 0.3989422804014327
low = jnp.bfloat16
f32 = jnp.float32


def dot(left, right, axes=((1,), (0,))):
    return lax.dot_general(left, right, (axes, ((), ())), preferred_element_type=f32)


def permute(a, axis, name, partner):
    pairs = [(i, partner(i)) for i in range(lax.axis_size(axis))]
    with jax.named_scope("%s_%d_%d" % (name, a.shape[0], a.shape[-1])):
        return lax.ppermute(a, axis, pairs)


def swap_core(a):
    return permute(a, "head", "core", lambda i: i ^ 1)


def swap_page(a):
    return permute(a, "head", "page", lambda i: i ^ 2)


def swap_dp(a, bit):
    return permute(a, "dp", "column", lambda i: i ^ bit)


def turn_dp(a, step):
    n = lax.axis_size("dp")
    return permute(a, "dp", "line", lambda i: (i + step) % n)


VMEM_LIMIT = 56 * 1024 * 1024
VMEM_SMALL = 24 * 1024 * 1024
SMALL = (
    "box_tables", "project", "attend", "attend_last", "feed_up", "feed_down", "tokens_back",
)
BLOCKS = 8


def grid_dp():
    return (4, 2) if lax.axis_size("dp") == 8 else (1, 1)


def place_dp():
    index = lax.axis_index("dp")
    return (index // 2, index % 2) if lax.axis_size("dp") == 8 else (index * 0, index * 0)


def after(value, *done):
    return lax.optimization_barrier((value, *done))[0] if done else value


def block_plan(kind):
    nz, ny = grid_dp()
    if nz == 1:
        return (((0, 0, 0),), ((1, 0, 0),))
    half = nz // 2

    def run(side, ky, start, end):
        return tuple((side, ky, k) for k in range(start, end))

    far = (run(1, 1, 0, half), run(1, 1, half, nz))
    if kind == "early":
        return tuple(run(*block, *cut) for cut in ((0, 1), (1, nz)) for block in ((0, 0), (1, 0), (0, 1))) + far
    if kind == "scatter":
        return (run(0, 0, 0, nz),) + tuple(run(*block, *cut) for block in ((1, 0), (0, 1)) for cut in ((0, half), (half, nz))) + far
    return tuple(run(*block, 0, nz) for block in ((0, 0), (1, 0), (0, 1))) + far


def gather_line(shard):
    nz, ny = grid_dp()
    if nz == 1:
        return [lax.all_gather(shard, "dp", axis=0, tiled=True)[None]]
    return [shard[None]] + [turn_dp(shard, ny * k)[None] for k in range(1, nz)]


def gather_near(line):
    if grid_dp()[0] == 1:
        return [line, swap_page(line)]
    return [line, swap_page(line), swap_dp(line, 1)]


def gather_far(parts, done=()):
    half = grid_dp()[0] // 2
    if half == 0:
        return parts
    line, across, beside = parts
    far_a, far_b = after((across[:half], beside[half:]), *done)
    return [line, across, beside, swap_dp(far_a, 1), swap_page(far_b)]


def gather_early(line, near_done, far_done):
    nz = grid_dp()[0]
    if nz == 1:
        return gather_near(line[0])
    own = gather_near(line[0])
    rest = gather_near(after(jnp.concatenate(line[1:], 0), *own, *near_done))
    cut = nz // 2 - 1
    far_a, far_b = after((jnp.concatenate([own[1], rest[1][:cut]], 0), rest[2][cut:]), *rest[1:], *far_done)
    return own + rest + [swap_dp(far_a, 1), swap_page(far_b)]


def add(a, b):
    return (a.astype(f32) + b.astype(f32)).astype(low)


def scatter_far(parts):
    if grid_dp()[0] == 1:
        return parts
    line, across_a, across_b, beside_a, beside_b, far_a, far_b = parts
    far_a = swap_page(far_a)
    far_b = swap_dp(far_b, 1)
    beside = jnp.concatenate([add(beside_a, far_a), beside_b], 0)
    across = jnp.concatenate([across_a, add(across_b, far_b)], 0)
    return [line, across, beside]


def scatter_near(parts):
    line = parts[0].astype(f32) + swap_page(parts[1]).astype(f32)
    if len(parts) > 2:
        line = line + swap_dp(parts[2], 1).astype(f32)
    return [line[0]] + [line[k].astype(low) for k in range(1, line.shape[0])]


def scatter_line(line, done=lambda: ()):
    nz, ny = grid_dp()
    if nz == 1:
        return lax.psum_scatter(line[0].astype(low), "dp", scatter_dimension=0, tiled=True).astype(f32)
    come = [turn_dp(line[k], ny * k) for k in range(1, nz)]
    return functools.reduce(jnp.add, [piece.astype(f32) for piece in after(come, *done())], line[0])


def sum_lines(a):
    nz, ny = grid_dp()
    return functools.reduce(jnp.add, [turn_dp(a, ny * k) for k in range(1, nz)], a)


def part_shapes(blocks, width):
    nz, ny = grid_dp()
    return [jax.ShapeDtypeStruct((len(p), blocks // (nz * ny), width), low) for p in block_plan("scatter")]


def slots(parts, place, dims, sign, turned, plan):
    nz, ny = dims
    found = []
    for part, blocks in zip(parts, plan):
        for i, (side, ky, kz) in enumerate(blocks):
            piece = part.at[i]
            rows = piece.shape[0]
            z = lax.rem(place[0] + (sign * kz) % nz, nz) if nz > 1 else 0
            y = lax.rem(place[1] + ky, ny) if ny > 1 else 0
            block = z * ny + y
            if not turned:
                found.append((piece, side, pl.multiple_of(block * rows, rows)))
                continue
            size = rows * nz * ny // BLOCKS
            for sub in range(rows // size):
                b = block * (rows // size) + sub
                b = lax.rem(lax.div(b, 2), 2) * 4 + lax.div(b, 4) * 2 + lax.rem(b, 2)
                found.append((piece.at[pl.ds(sub * size, size)], side, pl.multiple_of(b * size, size)))
    return found


def fetch(parts, whole, sems, place, plan, turned=False, columns=None, start=True):
    dims, plan = plan
    copies = []
    for i, (piece, side, row) in enumerate(slots(parts, place, dims, -1, turned, plan)):
        source = piece if columns is None else piece.at[:, pl.ds(columns[0], columns[1])]
        copies.append(pltpu.make_async_copy(source, whole.at[side, pl.ds(row, piece.shape[0])], sems.at[i]))
    for copy in copies if start else []:
        copy.start()
    return copies


def deal(whole, parts, sems, place, plan, turned=False, columns=None):
    dims, plan = plan
    copies = []
    for i, (piece, side, row) in enumerate(slots(parts, place, dims, 1, turned, plan)):
        target = piece if columns is None else piece.at[:, pl.ds(columns[0], columns[1])]
        copies.append(pltpu.make_async_copy(whole.at[side, pl.ds(row, piece.shape[0])], target, sems.at[i]))
    for copy in copies:
        copy.start()
    return copies


def plans(kind):
    return grid_dp(), block_plan(kind)


def finish(copies):
    for copy in copies:
        copy.wait()


SMEM = pl.BlockSpec(memory_space=pltpu.SMEM)
VMEM = pl.BlockSpec(memory_space=pltpu.VMEM)
ANYWHERE = pl.BlockSpec(memory_space=pl.ANY)
COPIES = pltpu.SemaphoreType.DMA((2 * BLOCKS,))


def call(kernel, name, flops, moved, outs, out_specs, in_specs, scratch, args, grid=None, exps=0, done=()):
    extra = {} if grid is None else {"grid": grid}

    def body(*refs):
        kernel(*refs[: len(args)], *refs[len(args) + len(done) :])

    return pl.pallas_call(
        body,
        out_shape=outs,
        in_specs=in_specs + [ANYWHERE] * len(done),
        out_specs=out_specs,
        scratch_shapes=scratch,
        compiler_params=pltpu.CompilerParams(vmem_limit_bytes=VMEM_SMALL if name in SMALL else VMEM_LIMIT),
        cost_estimate=pl.CostEstimate(flops=int(flops), bytes_accessed=int(moved), transcendentals=int(exps)),
        name=name,
        **extra,
    )(*args, *done)


def shape(*dims, dtype=low):
    return jax.ShapeDtypeStruct(dims, dtype)


NT = ((1,), (1,))


def project_kernel(count, plan, scal, rows, bias, *refs):
    parts, refs = refs[:count], refs[count:]
    (q_o, k_o, v_o, key_t, bk_t, bq, bk, bq_t), (box, proj, sems, more_sems) = refs[:8], refs[8:]
    hc = box.shape[2] // 2
    place = (scal[0], scal[1])
    first = fetch(parts, proj, more_sems, place, plan, False, (2 * hc, 4 * hc))
    second = fetch(parts, box, sems, place, plan, True, (0, 2 * hc))
    finish(first)
    heads = hc // HEAD_DIM
    pairs = [[], [], []]
    for side in range(2):
        qkv = (dot(rows[...], proj[side, :, : 3 * hc]) + bias[side : side + 1]).astype(low)
        for i in range(3):
            pairs[i].append(qkv[:, i * hc : (i + 1) * hc])

    def paired(own, other, axis):
        cut = [slice(h * HEAD_DIM, (h + 1) * HEAD_DIM) for h in range(heads)]
        both = [(own[c], other[c]) if axis == 0 else (own[:, c], other[:, c]) for c in cut]
        return jnp.concatenate([one for two in both for one in two], axis)

    for ref, two in zip((q_o, k_o, v_o), pairs):
        ref[...] = paired(*two, 1)
    key_t[...] = k_o[...].T
    finish(second)
    bk[...] = paired(box[0, :, :hc], box[1, :, :hc], 1)
    bq[...] = paired(box[0, :, hc:], box[1, :, hc:], 1)
    bk_t[...] = bk[...].T
    bq_t[...] = bq[...].T


def project(scal, rows, bias, parts, done=()):
    length, width = rows.shape
    hc = parts[0].shape[2] // 6
    return call(
        functools.partial(project_kernel, len(parts), plans("early")),
        "project",
        12 * length * width * hc,
        10e6,
        [shape(length, 2 * hc)] * 3 + [shape(2 * hc, length), shape(2 * hc, width), shape(width, 2 * hc)]
        + [shape(width, 2 * hc), shape(2 * hc, width)],
        [VMEM] * 8,
        [SMEM, VMEM, VMEM] + [ANYWHERE] * len(parts),
        [pltpu.VMEM((2, width, 2 * hc), low), pltpu.VMEM((2, width, 4 * hc), low), COPIES, COPIES],
        (scal, rows, bias, *parts),
        done=done,
    )


def attend_pair(scale, length, q, v, key_t, bk_t, bq, query_table, queryt_table, keyt_table, p_o):
    half = query_table.shape[1] // 2
    cos, sin = query_table[:, :half].astype(f32), query_table[:, half:].astype(f32)
    cos_t, sin_t = queryt_table[:half].astype(f32), queryt_table[half:].astype(f32)
    valid = lax.broadcasted_iota(jnp.int32, (1, key_t.shape[1]), 1) < length
    outs = []
    for j in range(2):
        at = slice(j * HEAD_DIM, (j + 1) * HEAD_DIM)
        a = dot(q[:, at], bk_t[at])
        a_s, a_c = a[:, :half], a[:, half:]
        turn = jnp.concatenate(
            [(a_s * cos + a_c * sin).astype(low), (a_c * cos - a_s * sin).astype(low)], 1
        )
        b = dot(bq[:, at], key_t[at])
        b_s, b_c = b[:half], b[half:]
        turn_t = jnp.concatenate(
            [(b_s * sin_t + b_c * cos_t).astype(low), (b_c * sin_t - b_s * cos_t).astype(low)], 0
        )
        raw = dot(q[:, at], key_t[at]) + dot(turn, keyt_table[...]) + dot(query_table[...], turn_t)
        scores = jnp.where(valid, raw * scale, -1e9)
        exponent = jnp.exp(scores - jnp.max(scores, -1, keepdims=True))
        probs = (exponent * (1.0 / jnp.sum(exponent, -1, keepdims=True))).astype(low)
        p_o[j] = probs
        outs.append(dot(probs, v[:, at]))
    return jnp.concatenate(outs, 1).astype(low)


def attend_kernel(scale, scal, q, v, key_t, bk_t, bq, query_table, queryt_table, keyt_table, ctx_o, p_o):
    ctx_o[...] = attend_pair(
        scale, scal[2], q, v, key_t, bk_t, bq, query_table, queryt_table, keyt_table, p_o
    )


def attend_last_kernel(
    scale, count, plan, scal, q, v, key_t, bk_t, bq, query_table, queryt_table, keyt_table, ctx_a, *refs
):
    parts, (part_o, ctx_o, p_o, out_w, pairs, sems) = refs[:count], refs[count:]
    step = pl.program_id(0)
    hc = out_w.shape[2] // 2

    @pl.when(step == 0)
    def _():
        fetch(parts, out_w, sems, (scal[0], scal[1]), plan, False, (4 * hc, 2 * hc))

    pairs[step] = attend_pair(
        scale, scal[2], q, v, key_t, bk_t, bq, query_table, queryt_table, keyt_table, p_o
    )

    @pl.when(step == pl.num_programs(0) - 1)
    def _():
        ctx = jnp.concatenate([ctx_a[...]] + [pairs[i] for i in range(pairs.shape[0])], 1)
        both = [sides(ctx, side) for side in range(2)]
        ctx_o[...] = jnp.concatenate(both, 1)
        finish(fetch(parts, out_w, sems, (scal[0], scal[1]), plan, False, (4 * hc, 2 * hc), False))
        part_o[...] = (dot(both[0], out_w[0, :, hc:], NT) + dot(both[1], out_w[1, :, hc:], NT)).astype(low)


def attend_specs(first, length, half):
    two = 2 * HEAD_DIM
    wide = pl.BlockSpec((length, two), lambda p: (0, first + p))
    return [
        SMEM,
        wide,
        wide,
        pl.BlockSpec((two, length), lambda p: (first + p, 0)),
        pl.BlockSpec((two, 2 * half), lambda p: (first + p, 0)),
        pl.BlockSpec((2 * half, two), lambda p: (0, first + p)),
    ] + [VMEM] * 3


def attend_flops(count, length, half):
    return 4 * count * length * (4 * half * HEAD_DIM + length * (4 * half + 2 * HEAD_DIM))


def attend(count, scal, q, v, key_t, bk_t, bq, tables, done=()):
    length, half = tables[0].shape[0], tables[0].shape[1] // 2
    two = 2 * HEAD_DIM
    return call(
        functools.partial(attend_kernel, HEAD_DIM**-0.5),
        "attend",
        attend_flops(count, length, half),
        count * 2e6,
        [shape(length, count * two), shape(2 * count, length, length)],
        [pl.BlockSpec((length, two), lambda p: (0, p)), pl.BlockSpec((2, length, length), lambda p: (p, 0, 0))],
        attend_specs(0, length, half),
        [],
        (scal, q, v, key_t, bk_t, bq, tables[0], tables[2], tables[3]),
        (count,),
        2 * count * length * length,
        done,
    )


def attend_last(first, scal, q, v, key_t, bk_t, bq, tables, ctx_a, parts, done=()):
    length, half = tables[0].shape[0], tables[0].shape[1] // 2
    width, hc = 2 * half, parts[0].shape[2] // 6
    count = hc // HEAD_DIM - first
    two = 2 * HEAD_DIM
    return call(
        functools.partial(attend_last_kernel, HEAD_DIM**-0.5, len(parts), plans("early")),
        "attend_last",
        attend_flops(count, length, half),
        count * 2e6,
        [shape(length, width), shape(length, 2 * hc), shape(2 * count, length, length)],
        [
            pl.BlockSpec((length, width), lambda p: (0, 0)),
            pl.BlockSpec((length, 2 * hc), lambda p: (0, 0)),
            pl.BlockSpec((2, length, length), lambda p: (p, 0, 0)),
        ],
        attend_specs(first, length, half) + [VMEM] + [ANYWHERE] * len(parts),
        [pltpu.VMEM((2, width, 2 * hc), low), pltpu.VMEM((count, length, two), low), COPIES],
        (scal, q, v, key_t, bk_t, bq, tables[0], tables[2], tables[3], ctx_a, *parts),
        (count,),
        2 * count * length * length,
        done,
    )


def sides(values, side):
    heads = values.shape[1] // HEAD_DIM
    return jnp.concatenate([values[:, h * HEAD_DIM : (h + 1) * HEAD_DIM] for h in range(side, heads, 2)], 1)


def tables_kernel(boxes, frequency, query_o, key_o, queryt_o, keyt_o):
    width = frequency.shape[1]
    half = 2 * width
    for c in range(2):
        angles = boxes[:, c : c + 1] * frequency[...]
        cosine, sine = jnp.cos(angles), jnp.sin(angles)
        at, past = slice(c * width, (c + 1) * width), slice(half + c * width, half + (c + 1) * width)
        query_o[:, at] = cosine.astype(low)
        query_o[:, past] = sine.astype(low)
    key_o[:, :half] = query_o[:, half:]
    key_o[:, half:] = query_o[:, :half]
    queryt_o[...] = query_o[...].T
    keyt_o[:half] = queryt_o[half:]
    keyt_o[half:] = queryt_o[:half]


def box_tables(boxes, frequency):
    length, half = boxes.shape[0], 2 * frequency.shape[1]
    return call(
        tables_kernel,
        "box_tables",
        40 * length * half,
        3e6,
        [shape(length, 2 * half)] * 2 + [shape(2 * half, length)] * 2,
        [VMEM] * 4,
        [VMEM] * 2,
        [],
        (boxes, frequency),
    )


def standard(values):
    centered = values - jnp.mean(values, -1, keepdims=True)
    inverse = lax.rsqrt(jnp.mean(centered * centered, -1, keepdims=True) + norm_eps)
    return centered * inverse, inverse


def standard_back(upstream, scaled, inverse):
    return inverse * (
        upstream - jnp.mean(upstream, -1, keepdims=True) - scaled * jnp.mean(upstream * scaled, -1, keepdims=True)
    )


def col(values):
    return jnp.sum(values, 0, keepdims=True)


def feed_up_kernel(count, plan, scal, mine, theirs, rows, vecs, bias, *refs):
    ups, refs = refs[:count], refs[count:]
    (hidden_o, low_o, scaled_o, inverse_o, active_o, slope_o), (up, sems) = refs[:6], refs[6:]
    copies = fetch(ups, up, sems, (scal[0], scal[1]), plan)
    total = rows[...].astype(f32) + (mine[...].astype(f32) + theirs[...].astype(f32)) + vecs[0:1]
    scaled, inverse = standard(total)
    hidden = scaled * vecs[1:2] + vecs[2:3]
    hidden_o[...] = hidden
    scaled_o[...] = scaled
    inverse_o[...] = inverse
    hidden_low = hidden.astype(low)
    low_o[...] = hidden_low
    finish(copies)
    width = up.shape[2]
    size = 256
    for side in range(2):
        for at in range(0, width, size):
            inner = dot(hidden_low, up[side, :, at : at + size]) + bias[side : side + 1, at : at + size]
            cumulative = 0.5 * (1.0 + lax.erf(inner * sqrt_half))
            density = jnp.exp(-0.5 * inner * inner) * inv_root_two_pi
            active_o[:, side * width + at : side * width + at + size] = (inner * cumulative).astype(low)
            slope_o[:, side * width + at : side * width + at + size] = (cumulative + inner * density).astype(low)


def feed_up(scal, mine, theirs, rows, vecs, bias, ups, done=()):
    length, width = rows.shape
    units = ups[0].shape[2]
    return call(
        functools.partial(feed_up_kernel, len(ups), plans("gather")),
        "feed_up",
        4 * length * width * units,
        11e6,
        [
            shape(length, width, dtype=f32),
            shape(length, width),
            shape(length, width, dtype=f32),
            shape(length, 1, dtype=f32),
            shape(length, 2 * units),
            shape(length, 2 * units),
        ],
        [VMEM] * 6,
        [SMEM] + [VMEM] * 5 + [ANYWHERE] * len(ups),
        [pltpu.VMEM((2, width, units), low), COPIES],
        (scal, mine, theirs, rows, vecs, bias, *ups),
        exps=2 * length * units,
        done=done,
    )


def feed_down_kernel(count, plan, scal, active, *refs):
    downs, (part_o, down, sems) = refs[:count], refs[count:]
    finish(fetch(downs, down, sems, (scal[0], scal[1]), plan))
    units = down.shape[2]
    part_o[...] = (dot(active[:, :units], down[0], NT) + dot(active[:, units:], down[1], NT)).astype(low)


def feed_down(scal, active, downs, width, done=()):
    length, units = active.shape[0], active.shape[1] // 2
    return call(
        functools.partial(feed_down_kernel, len(downs), plans("gather")),
        "feed_down",
        4 * length * width * units,
        5e6,
        shape(length, width),
        VMEM,
        [SMEM, VMEM] + [ANYWHERE] * len(downs),
        [pltpu.VMEM((2, width, units), low), COPIES],
        (scal, active, *downs),
        done=done,
    )


def feed_back_kernel(count, plan, scal, mine, theirs, hidden, grad_out, vecs, active, *refs):
    (result_o, grad_o, low_o, sums_o), outs, (grads, sems) = refs[:4], refs[4 : 4 + count], refs[4 + count :]
    scaled, inverse = standard(hidden[...] + (mine[...].astype(f32) + theirs[...].astype(f32)) + vecs[0:1])
    result_o[...] = (scaled * vecs[1:2] + vecs[2:3]).astype(low)
    grad = grad_out[...].astype(f32)
    sums_o[1:2] = col(grad * scaled)
    sums_o[2:3] = col(grad)
    grad = standard_back(grad * vecs[1:2], scaled, inverse)
    sums_o[0:1] = col(grad)
    grad_o[...] = grad
    grad_low = grad.astype(low)
    low_o[...] = grad_low
    turned = grad_low.T
    units = grads.shape[2]
    for side in range(2):
        grads[side] = dot(turned, active[:, side * units : (side + 1) * units]).astype(low)
    finish(deal(grads, outs, sems, (scal[0], scal[1]), plan))


def feed_back(scal, mine, theirs, hidden, grad_out, vecs, active):
    length, width = hidden.shape
    units = active.shape[1] // 2
    parts = part_shapes(width, units)
    out = call(
        functools.partial(feed_back_kernel, len(parts), plans("scatter")),
        "feed_back",
        4 * length * width * units,
        12e6,
        [shape(length, width), shape(length, width, dtype=f32), shape(length, width), shape(3, width, dtype=f32)] + parts,
        [VMEM] * 4 + [ANYWHERE] * len(parts),
        [SMEM] + [VMEM] * 6,
        [pltpu.VMEM((2, width, units), low), COPIES],
        (scal, mine, theirs, hidden, grad_out, vecs, active),
    )
    return out[:4], out[4:]


def inner_back_kernel(count, plan, scal, grad_low, slope, *refs):
    downs, ups, refs = refs[:count], refs[count : 2 * count], refs[2 * count :]
    (inner_o, sums_o, part_o), (down, up, sems, more_sems) = refs[:3], refs[3:]
    place = (scal[0], scal[1])
    first = fetch(downs, down, sems, place, plan)
    second = fetch(ups, up, more_sems, place, plan)
    finish(first)
    units = up.shape[2]
    for side in range(2):
        at = slice(side * units, (side + 1) * units)
        grad = (dot(grad_low[...], down[side]) * slope[:, at].astype(f32)).astype(low)
        inner_o[:, at] = grad
        sums_o[side : side + 1] = col(grad.astype(f32))
    finish(second)
    part = dot(inner_o[:, :units], up[0], NT) + dot(inner_o[:, units:], up[1], NT)
    part_o[...] = part.astype(low)


def inner_back(scal, grad_low, slope, downs, ups):
    length, width = grad_low.shape
    units = slope.shape[1] // 2
    return call(
        functools.partial(inner_back_kernel, len(ups), plans("gather")),
        "inner_back",
        8 * length * width * units,
        10e6,
        [shape(length, 2 * units), shape(2, units, dtype=f32), shape(length, width)],
        [VMEM] * 3,
        [SMEM] + [VMEM] * 2 + [ANYWHERE] * (2 * len(ups)),
        [pltpu.VMEM((2, width, units), low)] * 2 + [COPIES] * 2,
        (scal, grad_low, slope, *downs, *ups),
    )


def norm_back_kernel(count, given, plan, given_plan, scal, mine, theirs, grad_two, scaled, inverse, vecs, hidden_low, grad_inner, ctx, *refs):
    weights, refs = refs[:given], refs[given:]
    (grad_o, dctx_o, sums_o), outs, (out_w, grads, sems) = refs[:3], refs[3 : 3 + count], refs[3 + count :]
    place = (scal[0], scal[1])
    hc = out_w.shape[2] // 2
    copies = fetch(weights, out_w, sems, place, given_plan, False, (4 * hc, 2 * hc))
    grad = grad_two[...] + (mine[...].astype(f32) + theirs[...].astype(f32))
    sums_o[1:2] = col(grad * scaled[...])
    sums_o[2:3] = col(grad)
    grad = standard_back(grad * vecs[1:2], scaled[...], inverse[...])
    sums_o[0:1] = col(grad)
    grad_o[...] = grad
    grad_low = grad.astype(low)
    finish(copies)
    both = [dot(grad_low, out_w[side, :, hc:]).astype(low) for side in range(2)]
    cut = [slice(h * HEAD_DIM, (h + 1) * HEAD_DIM) for h in range(hc // HEAD_DIM)]
    dctx_o[...] = jnp.concatenate([one[:, c] for c in cut for one in both], 1)
    units = grads.shape[2] - hc
    turned = hidden_low[...].T
    for side in range(2):
        grads[side, :, :units] = dot(turned, grad_inner[:, side * units : (side + 1) * units]).astype(low)
    grad_ctx = dot(grad_low.T, ctx[...]).astype(low)
    for side in range(2):
        grads[side, :, units:] = grad_ctx[:, side * hc : (side + 1) * hc]
    finish(deal(grads, outs, sems, place, plan))


def norm_back(scal, mine, theirs, grad_two, scaled, inverse, vecs, hidden_low, grad_inner, ctx, weights, done=()):
    length, width = grad_two.shape
    units, hc = grad_inner.shape[1] // 2, ctx.shape[1] // 2
    parts = part_shapes(width, units + hc)
    out = call(
        functools.partial(norm_back_kernel, len(parts), len(weights), plans("scatter"), plans("early")),
        "norm_back",
        4 * length * width * (units + 2 * hc),
        14e6,
        [shape(length, width, dtype=f32), shape(length, 2 * hc), shape(3, width, dtype=f32)] + parts,
        [VMEM] * 3 + [ANYWHERE] * len(parts),
        [SMEM] + [VMEM] * 9 + [ANYWHERE] * len(weights),
        [pltpu.VMEM((2, width, 2 * hc), low), pltpu.VMEM((2, width, units + hc), low), COPIES],
        (scal, mine, theirs, grad_two, scaled, inverse, vecs, hidden_low, grad_inner, ctx, *weights),
        done=done,
    )
    return out[:3], out[3:]


def attend_back_kernel(
    scale, scal, dctx, probs, q, k, v, bk, bq_t, key_table, queryt_table,
    dq_o, dk_o, dv_o, gbk_o, gbq_o,
):
    half = key_table.shape[1] // 2
    sin, cos = key_table[:, :half].astype(f32), key_table[:, half:].astype(f32)
    cos_t, sin_t = queryt_table[:half].astype(f32), queryt_table[half:].astype(f32)
    qt2, vt2, dctxt2 = q[...].T, v[...].T, dctx[...].T
    dqs, dks, dvs, gbks = [], [], [], []
    for j in range(2):
        at = slice(j * HEAD_DIM, (j + 1) * HEAD_DIM)
        weights = probs[j]
        wide = weights.astype(f32)
        dprobs = dot(dctx[:, at], vt2[at])
        inner = jnp.sum(wide * dprobs, -1, keepdims=True)
        draw = (scale * (wide * (dprobs - inner))).astype(low)
        dvs.append(dot(dctxt2[at], weights))
        g = dot(draw, key_table[...])
        g_u, g_l = g[:, :half], g[:, half:]
        da = jnp.concatenate(
            [(g_u * cos - g_l * sin).astype(low), (g_u * sin + g_l * cos).astype(low)], 1
        )
        dqs.append(dot(draw, k[:, at]) + dot(da, bk[:, at]))
        gbks.append(dot(qt2[at], da))
        g = dot(queryt_table[...], draw)
        g_u, g_l = g[:half], g[half:]
        db = jnp.concatenate(
            [(g_u * sin_t - g_l * cos_t).astype(low), (g_u * cos_t + g_l * sin_t).astype(low)], 0
        )
        dks.append(dot(qt2[at], draw) + dot(bq_t[at], db))
        gbq_o[:, at] = dot(db, k[:, at]).astype(low)
    dq_o[...] = jnp.concatenate(dqs, 1).astype(low)
    dk_o[...] = jnp.concatenate(dks, 0).astype(low).T
    dv_o[...] = jnp.concatenate(dvs, 0).astype(low).T
    gbk_o[...] = jnp.concatenate(gbks, 0).astype(low)


def attend_back(first, count, scal, dctx, probs, q, k, v, bk, bq_t, tables, done=()):
    length = dctx.shape[0]
    half = tables[0].shape[1] // 2
    width, two = 2 * half, 2 * HEAD_DIM
    pair = pl.BlockSpec((length, two), lambda p: (0, first + p))
    out = pl.BlockSpec((length, two), lambda p: (0, p))
    flops = 4 * count * length * (8 * half * HEAD_DIM + length * (4 * half + 4 * HEAD_DIM))
    return call(
        functools.partial(attend_back_kernel, HEAD_DIM**-0.5),
        "attend_back",
        flops,
        count * 2e6,
        [shape(length, count * two)] * 3 + [shape(count * two, width), shape(width, count * two)],
        [out] * 3 + [pl.BlockSpec((two, width), lambda p: (p, 0)), pl.BlockSpec((width, two), lambda p: (0, p))],
        [SMEM, pair, pl.BlockSpec((2, length, length), lambda p: (p, 0, 0))]
        + [pair] * 3
        + [pl.BlockSpec((width, two), lambda p: (0, first + p)), pl.BlockSpec((two, width), lambda p: (first + p, 0))]
        + [VMEM] * 2,
        [],
        (scal, dctx, probs, q, k, v, bk, bq_t, tables[1], tables[2]),
        (count,),
        done=done,
    )


def project_back_kernel(
    count, plan, scal, rows_t, dq_a, dk_a, dv_a, dq_b, dk_b, dv_b, gbk_a, gbk_b, gbq_a, gbq_b, ups, ones, twos, *refs
):
    sums, outs, (grads, turned, sems) = refs[:2], refs[2 : 2 + count], refs[2 + count :]
    for side, ref in enumerate(sums):
        ref[...] = jnp.zeros(ref.shape, f32)
        ref[1:2, : ups.shape[1]] = ups[side : side + 1]
        ref[2:5, : ones.shape[1]] = ones[...]
        ref[5:8, : twos.shape[1]] = twos[...]
    size = turned.shape[2] // 2
    gbk = jnp.concatenate([gbk_a[...], gbk_b[...]], 0).T
    gbq = jnp.concatenate([gbq_a[...], gbq_b[...]], 1)
    for side in range(2):
        turned[side, :, :size] = sides(gbk, side)
        turned[side, :, size:] = sides(gbq, side)
    for i, (one, two) in enumerate(((dq_a, dq_b), (dk_a, dk_b), (dv_a, dv_b))):
        value = jnp.concatenate([one[...], two[...]], 1)
        value = jnp.concatenate([sides(value, side) for side in range(2)], 1)
        total = col(value.astype(f32))
        grad = dot(rows_t[...], value).astype(low)
        for side in range(2):
            sums[side][0:1, i * size : (i + 1) * size] = total[:, side * size : (side + 1) * size]
            grads[side, :, (2 + i) * size : (3 + i) * size] = grad[:, side * size : (side + 1) * size]
    rows = turned.shape[1] // BLOCKS
    for b in range(BLOCKS):
        to = ((b // 2) % 2) * 4 + (b // 4) * 2 + b % 2
        for side in range(2):
            grads[side, b * rows : (b + 1) * rows, : 2 * size] = turned[side, to * rows : (to + 1) * rows]
    finish(deal(grads, outs, sems, (scal[0], scal[1]), plan))


def project_back(scal, rows_t, grads, boxes, sums, done=()):
    width, length = rows_t.shape
    cols = grads[0].shape[1] + grads[3].shape[1]
    parts = part_shapes(width, 5 * cols // 2)
    out = call(
        functools.partial(project_back_kernel, len(parts), plans("scatter")),
        "project_back",
        6 * length * width * cols,
        cols * 15e3,
        [shape(8, 5 * cols // 2, dtype=f32)] * 2 + parts,
        [VMEM] * 2 + [ANYWHERE] * len(parts),
        [SMEM] + [VMEM] * 14,
        [pltpu.VMEM((2, width, 5 * cols // 2), low), pltpu.VMEM((2, width, cols), low), COPIES],
        (scal, rows_t, *grads, *boxes, *sums),
        done=done,
    )
    return out[0], out[1], out[2:]


def tokens_back_kernel(count, plan, scal, dq_a, dk_a, dv_a, dq_b, dk_b, dv_b, *refs):
    parts, (part_o, proj, sems) = refs[:count], refs[count:]
    hc = proj.shape[2] // 4
    copies = fetch(parts, proj, sems, (scal[0], scal[1]), plan, False, (2 * hc, 4 * hc))
    both = [jnp.concatenate([a[...], b[...]], 1) for a, b in ((dq_a, dq_b), (dk_a, dk_b), (dv_a, dv_b))]
    grads = [jnp.concatenate([sides(g, side) for g in both], 1) for side in range(2)]
    finish(copies)
    total = dot(grads[0], proj[0, :, : 3 * hc], NT) + dot(grads[1], proj[1, :, : 3 * hc], NT)
    part_o[...] = total.astype(low)


def tokens_back(scal, grads, parts, width, done=()):
    length = grads[0].shape[0]
    hc = parts[0].shape[2] // 6
    return call(
        functools.partial(tokens_back_kernel, len(parts), plans("early")),
        "tokens_back",
        12 * length * width * hc,
        5e6,
        shape(length, width),
        VMEM,
        [SMEM] + [VMEM] * 6 + [ANYWHERE] * len(parts),
        [pltpu.VMEM((2, width, 4 * hc), low), COPIES],
        (scal, *grads, *parts),
        done=done,
    )


def rows_kernel(scal, mine, sent, passed, out):
    length, half = mine.shape[0], sent.shape[0]
    page, core = scal[3], scal[4]
    out[pl.ds(pl.multiple_of(page * length, length), length)] = mine[...]
    out[pl.ds(pl.multiple_of((1 - page) * length + core * half, half), half)] = sent[...]
    out[pl.ds(pl.multiple_of((1 - page) * length + (1 - core) * half, half), half)] = passed[...]


def all_rows(scal, mine, sent, passed):
    length, width = mine.shape
    return call(
        rows_kernel, "all_rows", 0, 8 * length * width, shape(2 * length, width), VMEM, [SMEM] + [VMEM] * 3, [],
        (scal, mine, sent, passed),
    )


def sum_columns(a):
    return a + swap_dp(a, 1) if grid_dp()[0] > 1 else lax.psum(a, "dp")


def local(
    tokens, lengths, boxes, query_weight, key_weight, value_weight, query_bias, key_bias, value_bias,
    box_key_weight, box_query_weight, out_weight, out_bias, first_gain, first_shift, up_weight, up_bias,
    down_weight, down_bias, second_gain, second_shift, output_grad,
):
    pages = lengths.shape[0]
    page_len = tokens.shape[0] // pages
    width = tokens.shape[1]
    hc = query_weight.shape[1]
    units = up_weight.shape[1]

    page = lax.axis_index("head") // (lax.axis_size("head") // pages)
    start = page * page_len
    rows = lax.dynamic_slice_in_dim(tokens, start, page_len, 0)
    grad_rows = lax.dynamic_slice_in_dim(output_grad, start, page_len, 0)
    box_rows = lax.dynamic_slice_in_dim(boxes, start, page_len, 1)
    length = lax.dynamic_slice_in_dim(lengths, page, 1, 0)[0]
    biases = jnp.concatenate([query_bias, key_bias, value_bias, up_bias])[None].astype(low)
    biases = jnp.concatenate([biases, swap_page(biases)], 0).astype(f32)
    vecs_one = jnp.stack([out_bias, first_gain, first_shift]).astype(f32)
    vecs_two = jnp.stack([down_bias, second_gain, second_shift]).astype(f32)
    frequency = (10000.0 ** (-jnp.arange(width // 4, dtype=f32) / (width // 4)))[None]
    z, y = place_dp()
    core = lax.axis_index("head") % (lax.axis_size("head") // pages)
    scal = jnp.stack([z, y, length, page, core]).astype(jnp.int32)
    rows_t = rows.T

    first = jnp.concatenate(
        [box_key_weight, box_query_weight, query_weight, key_weight, value_weight, out_weight.T], 1
    )
    line_1 = gather_line(first)
    tables = box_tables(after(box_rows.T, line_1[-1]).astype(f32), frequency)
    line_2 = gather_line(after(up_weight, *line_1[1:]))
    parts_1 = gather_early(line_1, (*tables, rows_t, rows, grad_rows, biases, scal, vecs_one, vecs_two), line_2[1:])
    line_3 = gather_line(after(down_weight.T, *line_2[1:]))
    parts_2 = gather_near(after(jnp.concatenate(line_2, 0), *parts_1[-2:], *line_3[1:]))

    pairs = hc // HEAD_DIM
    query, key, value, key_t, bk_t, bq, bk, bq_t = project(scal, rows, biases[:, : 3 * hc], parts_1)
    parts_3 = gather_near(jnp.concatenate(after(list(line_3), *parts_2[1:], query), 0))
    near_2, near_3 = parts_2[1:], parts_3[1:]
    parts_2 = gather_far(parts_2)
    parts_3 = gather_far(parts_3)
    ctx_a, probs_a = attend(1, scal, query, value, key_t, bk_t, bq, tables)
    mine, context, probs_b = attend_last(1, scal, query, value, key_t, bk_t, bq, tables, ctx_a, parts_1, near_2)
    mine = after(mine, *near_3, *parts_2[3:])
    hidden, hidden_low, scaled_one, inverse_one, active, slope = feed_up(
        scal, mine, swap_core(mine), rows, vecs_one, biases[:, 3 * hc :], parts_2
    )
    feed = feed_down(scal, active, parts_3, width)
    (result, grad_two, feed_low, sums_two), grads_3 = feed_back(
        scal, feed, swap_core(feed), hidden, grad_rows, vecs_two, active
    )
    grads_3 = scatter_far(grads_3)
    grad_inner, sums_up, mine = inner_back(scal, feed_low, slope, parts_3, parts_2)
    (grad_one, grad_context, sums_one), grads_2 = norm_back(
        scal, mine, swap_core(mine), grad_two, scaled_one, inverse_one, vecs_one, hidden_low, grad_inner, context,
        parts_1, grads_3[1:],
    )
    grads_3 = scatter_near(grads_3)
    grads_2 = scatter_far(grads_2)
    *grads_a, gbk_a, gbq_a = attend_back(
        0, 1, scal, grad_context, probs_a, query, key, value, bk, bq_t, tables, grads_3
    )
    sum_3 = scatter_line(grads_3)
    *grads_b, gbk_b, gbq_b = attend_back(
        1, pairs - 1, scal, grad_context, probs_b, query, key, value, bk, bq_t, tables, (*grads_2[1:], gbk_a)
    )
    grads_2 = scatter_near(after(list(grads_2), gbk_a))
    grads = [*grads_a, *grads_b]
    own_small, oth_small, grads_1 = project_back(
        scal, rows_t, grads, [gbk_a, gbk_b, gbq_a, gbq_b], (sums_up, sums_one, sums_two), (*grads_2, sum_3)
    )
    sum_2 = scatter_line(grads_2)
    grads_1 = scatter_far(grads_1)
    grads_1 = scatter_near(after(list(grads_1), sum_2))
    small = own_small + swap_page(after(oth_small, *grads_1))
    half = page_len // 2

    def send_half(mine):
        return swap_page(lax.dynamic_slice_in_dim(mine, core * half, half, 0))

    sent = send_half(after(result, *grads_1, small))
    mine = tokens_back(scal, grads, parts_1, width, grads_1)
    token_grad = (grad_one + (mine.astype(f32) + swap_core(mine).astype(f32))).astype(low)
    sent_grad = send_half(token_grad)
    small = sum_columns(small)
    small = sum_lines(small)
    sum_1 = scatter_line(grads_1, lambda: (sent, sent_grad, small))

    return (
        all_rows(scal, result, sent, swap_core(sent)),
        all_rows(scal, token_grad, sent_grad, swap_core(sent_grad)),
        sum_1[:, 2 * hc : 3 * hc],
        sum_1[:, 3 * hc : 4 * hc],
        sum_1[:, 4 * hc :],
        small[0, :hc],
        small[0, hc : 2 * hc],
        small[0, 2 * hc : 3 * hc],
        sum_1[:, :hc],
        sum_1[:, hc : 2 * hc],
        sum_2[:, units:].T,
        small[2, :width],
        small[3, :width],
        small[4, :width],
        sum_2[:, :units],
        small[1, :units],
        sum_3.T,
        small[5, :width],
        small[6, :width],
        small[7, :width],
    )


def solution(mesh):
    row, vec, mat, tam, all_ = P("dp", None), P("head"), P("dp", "head"), P("head", "dp"), P()
    return jax.shard_map(
        local,
        mesh=mesh,
        in_specs=(
            row, P("dp"), P(None, "dp"), mat, mat, mat, vec, vec, vec, mat, mat, tam, all_, all_, all_,
            mat, vec, tam, all_, all_, all_, row,
        ),
        out_specs=(
            row, row, mat, mat, mat, vec, vec, vec, mat, mat, tam, all_, all_, all_, mat, vec, tam,
            all_, all_, all_,
        ),
        check_vma=False,
    )
```

```python
import functools

import jax
import jax.numpy as jnp
from jax import lax
from jax.experimental import pallas as pl
from jax.experimental.pallas import tpu as pltpu
from jax.sharding import PartitionSpec as P

HEAD_DIM = 64
norm_eps = 1e-05
sqrt_half = 0.7071067811865476
inv_root_two_pi = 0.3989422804014327
low = jnp.bfloat16
f32 = jnp.float32


def dot(left, right, axes=((1,), (0,))):
    return lax.dot_general(left, right, (axes, ((), ())), preferred_element_type=f32)


def permute(a, axis, name, partner):
    pairs = [(i, partner(i)) for i in range(lax.axis_size(axis))]
    with jax.named_scope("%s_%d_%d" % (name, a.shape[0], a.shape[-1])):
        return lax.ppermute(a, axis, pairs)


def swap_core(a):
    return permute(a, "head", "core", lambda i: i ^ 1)


def swap_page(a):
    return permute(a, "head", "page", lambda i: i ^ 2)


def swap_dp(a, bit):
    return permute(a, "dp", "column", lambda i: i ^ bit)


def turn_dp(a, step):
    n = lax.axis_size("dp")
    return permute(a, "dp", "line", lambda i: (i + step) % n)


VMEM_LIMIT = 56 * 1024 * 1024
VMEM_SMALL = 24 * 1024 * 1024
SMALL = (
    "box_tables", "project", "attend", "attend_last", "feed_up", "feed_down", "feed_back", "tokens_back",
)
BLOCKS = 8


def grid_dp():
    return (4, 2) if lax.axis_size("dp") == 8 else (1, 1)


def place_dp():
    index = lax.axis_index("dp")
    return (index // 2, index % 2) if lax.axis_size("dp") == 8 else (index * 0, index * 0)


def after(value, *done):
    return lax.optimization_barrier((value, *done))[0] if done else value


def block_plan(kind):
    nz, ny = grid_dp()
    if nz == 1:
        return (((0, 0, 0),), ((1, 0, 0),))
    half = nz // 2

    def run(side, ky, start, end):
        return tuple((side, ky, k) for k in range(start, end))

    far = (run(1, 1, 0, half), run(1, 1, half, nz))
    if kind == "early":
        return tuple(run(*block, *cut) for cut in ((0, 1), (1, nz)) for block in ((0, 0), (1, 0), (0, 1))) + far
    if kind == "scatter":
        return (run(0, 0, 0, nz),) + tuple(run(*block, *cut) for block in ((1, 0), (0, 1)) for cut in ((0, half), (half, nz))) + far
    return tuple(run(*block, 0, nz) for block in ((0, 0), (1, 0), (0, 1))) + far


def gather_line(shard):
    nz, ny = grid_dp()
    if nz == 1:
        return [lax.all_gather(shard, "dp", axis=0, tiled=True)[None]]
    return [shard[None]] + [turn_dp(shard, ny * k)[None] for k in range(1, nz)]


def gather_near(line):
    if grid_dp()[0] == 1:
        return [line, swap_page(line)]
    return [line, swap_page(line), swap_dp(line, 1)]


def gather_far(parts, done=()):
    half = grid_dp()[0] // 2
    if half == 0:
        return parts
    line, across, beside = parts
    far_a, far_b = after((across[:half], beside[half:]), *done)
    return [line, across, beside, swap_dp(far_a, 1), swap_page(far_b)]


def gather_early(line, near_done, far_done):
    nz = grid_dp()[0]
    if nz == 1:
        return gather_near(line[0])
    own = gather_near(line[0])
    rest = gather_near(after(jnp.concatenate(line[1:], 0), *own, *near_done))
    cut = nz // 2 - 1
    far_a, far_b = after((jnp.concatenate([own[1], rest[1][:cut]], 0), rest[2][cut:]), *rest[1:], *far_done)
    return own + rest + [swap_dp(far_a, 1), swap_page(far_b)]


def add(a, b):
    return (a.astype(f32) + b.astype(f32)).astype(low)


def scatter_far(parts):
    if grid_dp()[0] == 1:
        return parts
    line, across_a, across_b, beside_a, beside_b, far_a, far_b = parts
    far_a = swap_page(far_a)
    far_b = swap_dp(far_b, 1)
    beside = jnp.concatenate([add(beside_a, far_a), beside_b], 0)
    across = jnp.concatenate([across_a, add(across_b, far_b)], 0)
    return [line, across, beside]


def scatter_near(parts):
    line = parts[0].astype(f32) + swap_page(parts[1]).astype(f32)
    if len(parts) > 2:
        line = line + swap_dp(parts[2], 1).astype(f32)
    return [line[0]] + [line[k].astype(low) for k in range(1, line.shape[0])]


def scatter_line(line, done=lambda: ()):
    nz, ny = grid_dp()
    if nz == 1:
        return lax.psum_scatter(line[0].astype(low), "dp", scatter_dimension=0, tiled=True).astype(f32)
    come = [turn_dp(line[k], ny * k) for k in range(1, nz)]
    return functools.reduce(jnp.add, [piece.astype(f32) for piece in after(come, *done())], line[0])


def sum_lines(a):
    nz, ny = grid_dp()
    return functools.reduce(jnp.add, [turn_dp(a, ny * k) for k in range(1, nz)], a)


def part_shapes(blocks, width):
    nz, ny = grid_dp()
    return [jax.ShapeDtypeStruct((len(p), blocks // (nz * ny), width), low) for p in block_plan("scatter")]


def slots(parts, place, dims, sign, turned, plan):
    nz, ny = dims
    found = []
    for part, blocks in zip(parts, plan):
        for i, (side, ky, kz) in enumerate(blocks):
            piece = part.at[i]
            rows = piece.shape[0]
            z = lax.rem(place[0] + (sign * kz) % nz, nz) if nz > 1 else 0
            y = lax.rem(place[1] + ky, ny) if ny > 1 else 0
            block = z * ny + y
            if not turned:
                found.append((piece, side, pl.multiple_of(block * rows, rows)))
                continue
            size = rows * nz * ny // BLOCKS
            for sub in range(rows // size):
                b = block * (rows // size) + sub
                b = lax.rem(lax.div(b, 2), 2) * 4 + lax.div(b, 4) * 2 + lax.rem(b, 2)
                found.append((piece.at[pl.ds(sub * size, size)], side, pl.multiple_of(b * size, size)))
    return found


def fetch(parts, whole, sems, place, plan, turned=False, columns=None, start=True):
    dims, plan = plan
    copies = []
    for i, (piece, side, row) in enumerate(slots(parts, place, dims, -1, turned, plan)):
        source = piece if columns is None else piece.at[:, pl.ds(columns[0], columns[1])]
        copies.append(pltpu.make_async_copy(source, whole.at[side, pl.ds(row, piece.shape[0])], sems.at[i]))
    for copy in copies if start else []:
        copy.start()
    return copies


def deal(whole, parts, sems, place, plan, turned=False, columns=None):
    dims, plan = plan
    copies = []
    for i, (piece, side, row) in enumerate(slots(parts, place, dims, 1, turned, plan)):
        target = piece if columns is None else piece.at[:, pl.ds(columns[0], columns[1])]
        copies.append(pltpu.make_async_copy(whole.at[side, pl.ds(row, piece.shape[0])], target, sems.at[i]))
    for copy in copies:
        copy.start()
    return copies


def plans(kind):
    return grid_dp(), block_plan(kind)


def finish(copies):
    for copy in copies:
        copy.wait()


SMEM = pl.BlockSpec(memory_space=pltpu.SMEM)
VMEM = pl.BlockSpec(memory_space=pltpu.VMEM)
ANYWHERE = pl.BlockSpec(memory_space=pl.ANY)
COPIES = pltpu.SemaphoreType.DMA((2 * BLOCKS,))


def call(kernel, name, flops, moved, outs, out_specs, in_specs, scratch, args, grid=None, exps=0, done=()):
    extra = {} if grid is None else {"grid": grid}

    def body(*refs):
        kernel(*refs[: len(args)], *refs[len(args) + len(done) :])

    return pl.pallas_call(
        body,
        out_shape=outs,
        in_specs=in_specs + [ANYWHERE] * len(done),
        out_specs=out_specs,
        scratch_shapes=scratch,
        compiler_params=pltpu.CompilerParams(vmem_limit_bytes=VMEM_SMALL if name in SMALL else VMEM_LIMIT),
        cost_estimate=pl.CostEstimate(flops=int(flops), bytes_accessed=int(moved), transcendentals=int(exps)),
        name=name,
        **extra,
    )(*args, *done)


def shape(*dims, dtype=low):
    return jax.ShapeDtypeStruct(dims, dtype)


NT = ((1,), (1,))


def project_kernel(count, plan, scal, rows, bias, *refs):
    parts, refs = refs[:count], refs[count:]
    (q_o, k_o, v_o, key_t, bk_t, bq, bk, bq_t), (box, proj, sems, more_sems) = refs[:8], refs[8:]
    hc = box.shape[2] // 2
    place = (scal[0], scal[1])
    first = fetch(parts, proj, more_sems, place, plan, False, (2 * hc, 4 * hc))
    second = fetch(parts, box, sems, place, plan, True, (0, 2 * hc))
    finish(first)
    heads = hc // HEAD_DIM
    pairs = [[], [], []]
    for side in range(2):
        qkv = (dot(rows[...], proj[side, :, : 3 * hc]) + bias[side : side + 1]).astype(low)
        for i in range(3):
            pairs[i].append(qkv[:, i * hc : (i + 1) * hc])

    def paired(own, other, axis):
        cut = [slice(h * HEAD_DIM, (h + 1) * HEAD_DIM) for h in range(heads)]
        both = [(own[c], other[c]) if axis == 0 else (own[:, c], other[:, c]) for c in cut]
        return jnp.concatenate([one for two in both for one in two], axis)

    for ref, two in zip((q_o, k_o, v_o), pairs):
        ref[...] = paired(*two, 1)
    key_t[...] = k_o[...].T
    finish(second)
    bk[...] = paired(box[0, :, :hc], box[1, :, :hc], 1)
    bq[...] = paired(box[0, :, hc:], box[1, :, hc:], 1)
    bk_t[...] = bk[...].T
    bq_t[...] = bq[...].T


def project(scal, rows, bias, parts, done=()):
    length, width = rows.shape
    hc = parts[0].shape[2] // 6
    return call(
        functools.partial(project_kernel, len(parts), plans("early")),
        "project",
        12 * length * width * hc,
        10e6,
        [shape(length, 2 * hc)] * 3 + [shape(2 * hc, length), shape(2 * hc, width), shape(width, 2 * hc)]
        + [shape(width, 2 * hc), shape(2 * hc, width)],
        [VMEM] * 8,
        [SMEM, VMEM, VMEM] + [ANYWHERE] * len(parts),
        [pltpu.VMEM((2, width, 2 * hc), low), pltpu.VMEM((2, width, 4 * hc), low), COPIES, COPIES],
        (scal, rows, bias, *parts),
        done=done,
    )


def attend_pair(scale, length, q, v, key_t, bk_t, bq, query_table, queryt_table, keyt_table, p_o):
    half = query_table.shape[1] // 2
    cos, sin = query_table[:, :half].astype(f32), query_table[:, half:].astype(f32)
    cos_t, sin_t = queryt_table[:half].astype(f32), queryt_table[half:].astype(f32)
    valid = lax.broadcasted_iota(jnp.int32, (1, key_t.shape[1]), 1) < length
    outs = []
    for j in range(2):
        at = slice(j * HEAD_DIM, (j + 1) * HEAD_DIM)
        a = dot(q[:, at], bk_t[at])
        a_s, a_c = a[:, :half], a[:, half:]
        turn = jnp.concatenate(
            [(a_s * cos + a_c * sin).astype(low), (a_c * cos - a_s * sin).astype(low)], 1
        )
        b = dot(bq[:, at], key_t[at])
        b_s, b_c = b[:half], b[half:]
        turn_t = jnp.concatenate(
            [(b_s * sin_t + b_c * cos_t).astype(low), (b_c * sin_t - b_s * cos_t).astype(low)], 0
        )
        raw = dot(q[:, at], key_t[at]) + dot(turn, keyt_table[...]) + dot(query_table[...], turn_t)
        scores = jnp.where(valid, raw * scale, -1e9)
        exponent = jnp.exp(scores - jnp.max(scores, -1, keepdims=True))
        probs = (exponent * (1.0 / jnp.sum(exponent, -1, keepdims=True))).astype(low)
        p_o[j] = probs
        outs.append(dot(probs, v[:, at]))
    return jnp.concatenate(outs, 1).astype(low)


def attend_kernel(scale, scal, q, v, key_t, bk_t, bq, query_table, queryt_table, keyt_table, ctx_o, p_o):
    ctx_o[...] = attend_pair(
        scale, scal[2], q, v, key_t, bk_t, bq, query_table, queryt_table, keyt_table, p_o
    )


def attend_last_kernel(
    scale, count, plan, scal, q, v, key_t, bk_t, bq, query_table, queryt_table, keyt_table, ctx_a, *refs
):
    parts, (part_o, ctx_o, p_o, out_w, pairs, sems) = refs[:count], refs[count:]
    step = pl.program_id(0)
    hc = out_w.shape[2] // 2

    @pl.when(step == 0)
    def _():
        fetch(parts, out_w, sems, (scal[0], scal[1]), plan, False, (4 * hc, 2 * hc))

    pairs[step] = attend_pair(
        scale, scal[2], q, v, key_t, bk_t, bq, query_table, queryt_table, keyt_table, p_o
    )

    @pl.when(step == pl.num_programs(0) - 1)
    def _():
        ctx = jnp.concatenate([ctx_a[...]] + [pairs[i] for i in range(pairs.shape[0])], 1)
        both = [sides(ctx, side) for side in range(2)]
        ctx_o[...] = jnp.concatenate(both, 1)
        finish(fetch(parts, out_w, sems, (scal[0], scal[1]), plan, False, (4 * hc, 2 * hc), False))
        part_o[...] = (dot(both[0], out_w[0, :, hc:], NT) + dot(both[1], out_w[1, :, hc:], NT)).astype(low)


def attend_specs(first, length, half):
    two = 2 * HEAD_DIM
    wide = pl.BlockSpec((length, two), lambda p: (0, first + p))
    return [
        SMEM,
        wide,
        wide,
        pl.BlockSpec((two, length), lambda p: (first + p, 0)),
        pl.BlockSpec((two, 2 * half), lambda p: (first + p, 0)),
        pl.BlockSpec((2 * half, two), lambda p: (0, first + p)),
    ] + [VMEM] * 3


def attend_flops(count, length, half):
    return 4 * count * length * (4 * half * HEAD_DIM + length * (4 * half + 2 * HEAD_DIM))


def attend(count, scal, q, v, key_t, bk_t, bq, tables, done=()):
    length, half = tables[0].shape[0], tables[0].shape[1] // 2
    two = 2 * HEAD_DIM
    return call(
        functools.partial(attend_kernel, HEAD_DIM**-0.5),
        "attend",
        attend_flops(count, length, half),
        count * 2e6,
        [shape(length, count * two), shape(2 * count, length, length)],
        [pl.BlockSpec((length, two), lambda p: (0, p)), pl.BlockSpec((2, length, length), lambda p: (p, 0, 0))],
        attend_specs(0, length, half),
        [],
        (scal, q, v, key_t, bk_t, bq, tables[0], tables[2], tables[3]),
        (count,),
        2 * count * length * length,
        done,
    )


def attend_last(first, scal, q, v, key_t, bk_t, bq, tables, ctx_a, parts, done=()):
    length, half = tables[0].shape[0], tables[0].shape[1] // 2
    width, hc = 2 * half, parts[0].shape[2] // 6
    count = hc // HEAD_DIM - first
    two = 2 * HEAD_DIM
    return call(
        functools.partial(attend_last_kernel, HEAD_DIM**-0.5, len(parts), plans("early")),
        "attend_last",
        attend_flops(count, length, half),
        count * 2e6,
        [shape(length, width), shape(length, 2 * hc), shape(2 * count, length, length)],
        [
            pl.BlockSpec((length, width), lambda p: (0, 0)),
            pl.BlockSpec((length, 2 * hc), lambda p: (0, 0)),
            pl.BlockSpec((2, length, length), lambda p: (p, 0, 0)),
        ],
        attend_specs(first, length, half) + [VMEM] + [ANYWHERE] * len(parts),
        [pltpu.VMEM((2, width, 2 * hc), low), pltpu.VMEM((count, length, two), low), COPIES],
        (scal, q, v, key_t, bk_t, bq, tables[0], tables[2], tables[3], ctx_a, *parts),
        (count,),
        2 * count * length * length,
        done,
    )


def sides(values, side):
    heads = values.shape[1] // HEAD_DIM
    return jnp.concatenate([values[:, h * HEAD_DIM : (h + 1) * HEAD_DIM] for h in range(side, heads, 2)], 1)


def tables_kernel(boxes, frequency, query_o, key_o, queryt_o, keyt_o):
    width = frequency.shape[1]
    half = 2 * width
    for c in range(2):
        angles = boxes[:, c : c + 1] * frequency[...]
        cosine, sine = jnp.cos(angles), jnp.sin(angles)
        at, past = slice(c * width, (c + 1) * width), slice(half + c * width, half + (c + 1) * width)
        query_o[:, at] = cosine.astype(low)
        query_o[:, past] = sine.astype(low)
    key_o[:, :half] = query_o[:, half:]
    key_o[:, half:] = query_o[:, :half]
    queryt_o[...] = query_o[...].T
    keyt_o[:half] = queryt_o[half:]
    keyt_o[half:] = queryt_o[:half]


def box_tables(boxes, frequency):
    length, half = boxes.shape[0], 2 * frequency.shape[1]
    return call(
        tables_kernel,
        "box_tables",
        40 * length * half,
        3e6,
        [shape(length, 2 * half)] * 2 + [shape(2 * half, length)] * 2,
        [VMEM] * 4,
        [VMEM] * 2,
        [],
        (boxes, frequency),
    )


def standard(values):
    centered = values - jnp.mean(values, -1, keepdims=True)
    inverse = lax.rsqrt(jnp.mean(centered * centered, -1, keepdims=True) + norm_eps)
    return centered * inverse, inverse


def standard_back(upstream, scaled, inverse):
    return inverse * (
        upstream - jnp.mean(upstream, -1, keepdims=True) - scaled * jnp.mean(upstream * scaled, -1, keepdims=True)
    )


def col(values):
    return jnp.sum(values, 0, keepdims=True)


def feed_up_kernel(count, plan, scal, mine, theirs, rows, vecs, bias, *refs):
    ups, refs = refs[:count], refs[count:]
    (hidden_o, active_o, slope_o), (up, sems) = refs[:3], refs[3:]
    copies = fetch(ups, up, sems, (scal[0], scal[1]), plan)
    total = rows[...].astype(f32) + (mine[...].astype(f32) + theirs[...].astype(f32)) + vecs[0:1]
    scaled, _ = standard(total)
    hidden = scaled * vecs[1:2] + vecs[2:3]
    hidden_o[...] = hidden
    hidden_low = hidden.astype(low)
    finish(copies)
    width = up.shape[2]
    size = 256
    for side in range(2):
        for at in range(0, width, size):
            inner = dot(hidden_low, up[side, :, at : at + size]) + bias[side : side + 1, at : at + size]
            cumulative = 0.5 * (1.0 + lax.erf(inner * sqrt_half))
            density = jnp.exp(-0.5 * inner * inner) * inv_root_two_pi
            active_o[:, side * width + at : side * width + at + size] = (inner * cumulative).astype(low)
            slope_o[:, side * width + at : side * width + at + size] = (cumulative + inner * density).astype(low)


def feed_up(scal, mine, theirs, rows, vecs, bias, ups, done=()):
    length, width = rows.shape
    units = ups[0].shape[2]
    return call(
        functools.partial(feed_up_kernel, len(ups), plans("gather")),
        "feed_up",
        4 * length * width * units,
        11e6,
        [
            shape(length, width, dtype=f32),
            shape(length, 2 * units),
            shape(length, 2 * units),
        ],
        [VMEM] * 3,
        [SMEM] + [VMEM] * 5 + [ANYWHERE] * len(ups),
        [pltpu.VMEM((2, width, units), low), COPIES],
        (scal, mine, theirs, rows, vecs, bias, *ups),
        exps=2 * length * units,
        done=done,
    )


def feed_down_kernel(count, plan, scal, active, *refs):
    downs, (part_o, down, sems) = refs[:count], refs[count:]
    finish(fetch(downs, down, sems, (scal[0], scal[1]), plan))
    units = down.shape[2]
    part_o[...] = (dot(active[:, :units], down[0], NT) + dot(active[:, units:], down[1], NT)).astype(low)


def feed_down(scal, active, downs, width, done=()):
    length, units = active.shape[0], active.shape[1] // 2
    return call(
        functools.partial(feed_down_kernel, len(downs), plans("gather")),
        "feed_down",
        4 * length * width * units,
        5e6,
        shape(length, width),
        VMEM,
        [SMEM, VMEM] + [ANYWHERE] * len(downs),
        [pltpu.VMEM((2, width, units), low), COPIES],
        (scal, active, *downs),
        done=done,
    )


def feed_back_kernel(count, plan, scal, mine, theirs, hidden, grad_out, vecs, active, *refs):
    (result_o, grad_o, low_o, sums_o), outs, (grads, sems) = refs[:4], refs[4 : 4 + count], refs[4 + count :]
    scaled, inverse = standard(hidden[...] + (mine[...].astype(f32) + theirs[...].astype(f32)) + vecs[0:1])
    result_o[...] = (scaled * vecs[1:2] + vecs[2:3]).astype(low)
    grad = grad_out[...].astype(f32)
    sums_o[1:2] = col(grad * scaled)
    sums_o[2:3] = col(grad)
    grad = standard_back(grad * vecs[1:2], scaled, inverse)
    sums_o[0:1] = col(grad)
    grad_o[...] = grad
    grad_low = grad.astype(low)
    low_o[...] = grad_low
    turned = grad_low.T
    units = grads.shape[2]
    for side in range(2):
        grads[side] = dot(turned, active[:, side * units : (side + 1) * units]).astype(low)
    finish(deal(grads, outs, sems, (scal[0], scal[1]), plan))


def feed_back(scal, mine, theirs, hidden, grad_out, vecs, active):
    length, width = hidden.shape
    units = active.shape[1] // 2
    parts = part_shapes(width, units)
    out = call(
        functools.partial(feed_back_kernel, len(parts), plans("scatter")),
        "feed_back",
        4 * length * width * units,
        12e6,
        [shape(length, width), shape(length, width, dtype=f32), shape(length, width), shape(3, width, dtype=f32)] + parts,
        [VMEM] * 4 + [ANYWHERE] * len(parts),
        [SMEM] + [VMEM] * 6,
        [pltpu.VMEM((2, width, units), low), COPIES],
        (scal, mine, theirs, hidden, grad_out, vecs, active),
    )
    return out[:4], out[4:]


def inner_back_kernel(count, plan, scal, grad_low, slope, *refs):
    downs, ups, refs = refs[:count], refs[count : 2 * count], refs[2 * count :]
    (inner_o, sums_o, part_o), (down, up, sems, more_sems) = refs[:3], refs[3:]
    place = (scal[0], scal[1])
    first = fetch(downs, down, sems, place, plan)
    second = fetch(ups, up, more_sems, place, plan)
    finish(first)
    units = up.shape[2]
    for side in range(2):
        at = slice(side * units, (side + 1) * units)
        grad = (dot(grad_low[...], down[side]) * slope[:, at].astype(f32)).astype(low)
        inner_o[:, at] = grad
        sums_o[side : side + 1] = col(grad.astype(f32))
    finish(second)
    part = dot(inner_o[:, :units], up[0], NT) + dot(inner_o[:, units:], up[1], NT)
    part_o[...] = part.astype(low)


def inner_back(scal, grad_low, slope, downs, ups):
    length, width = grad_low.shape
    units = slope.shape[1] // 2
    return call(
        functools.partial(inner_back_kernel, len(ups), plans("gather")),
        "inner_back",
        8 * length * width * units,
        10e6,
        [shape(length, 2 * units), shape(2, units, dtype=f32), shape(length, width)],
        [VMEM] * 3,
        [SMEM] + [VMEM] * 2 + [ANYWHERE] * (2 * len(ups)),
        [pltpu.VMEM((2, width, units), low)] * 2 + [COPIES] * 2,
        (scal, grad_low, slope, *downs, *ups),
    )


def norm_back_kernel(count, given, plan, given_plan, scal, mine, theirs, grad_two, first, second, rows, vecs, grad_inner, ctx, *refs):
    weights, refs = refs[:given], refs[given:]
    (grad_o, dctx_o, sums_o), outs, (out_w, grads, sems) = refs[:3], refs[3 : 3 + count], refs[3 + count :]
    place = (scal[0], scal[1])
    hc = out_w.shape[2] // 2
    copies = fetch(weights, out_w, sems, place, given_plan, False, (4 * hc, 2 * hc))
    grad = grad_two[...] + (mine[...].astype(f32) + theirs[...].astype(f32))
    scaled, inverse = standard(rows[...].astype(f32) + (first[...].astype(f32) + second[...].astype(f32)) + vecs[0:1])
    hidden_low = (scaled * vecs[1:2] + vecs[2:3]).astype(low)
    sums_o[1:2] = col(grad * scaled)
    sums_o[2:3] = col(grad)
    grad = standard_back(grad * vecs[1:2], scaled, inverse)
    sums_o[0:1] = col(grad)
    grad_o[...] = grad
    grad_low = grad.astype(low)
    finish(copies)
    both = [dot(grad_low, out_w[side, :, hc:]).astype(low) for side in range(2)]
    cut = [slice(h * HEAD_DIM, (h + 1) * HEAD_DIM) for h in range(hc // HEAD_DIM)]
    dctx_o[...] = jnp.concatenate([one[:, c] for c in cut for one in both], 1)
    units = grads.shape[2] - hc
    turned = hidden_low.T
    for side in range(2):
        grads[side, :, :units] = dot(turned, grad_inner[:, side * units : (side + 1) * units]).astype(low)
    grad_ctx = dot(grad_low.T, ctx[...]).astype(low)
    for side in range(2):
        grads[side, :, units:] = grad_ctx[:, side * hc : (side + 1) * hc]
    finish(deal(grads, outs, sems, place, plan))


def norm_back(scal, mine, theirs, grad_two, first, second, rows, vecs, grad_inner, ctx, weights, done=()):
    length, width = grad_two.shape
    units, hc = grad_inner.shape[1] // 2, ctx.shape[1] // 2
    parts = part_shapes(width, units + hc)
    out = call(
        functools.partial(norm_back_kernel, len(parts), len(weights), plans("scatter"), plans("early")),
        "norm_back",
        4 * length * width * (units + 2 * hc),
        14e6,
        [shape(length, width, dtype=f32), shape(length, 2 * hc), shape(3, width, dtype=f32)] + parts,
        [VMEM] * 3 + [ANYWHERE] * len(parts),
        [SMEM] + [VMEM] * 9 + [ANYWHERE] * len(weights),
        [pltpu.VMEM((2, width, 2 * hc), low), pltpu.VMEM((2, width, units + hc), low), COPIES],
        (scal, mine, theirs, grad_two, first, second, rows, vecs, grad_inner, ctx, *weights),
        done=done,
    )
    return out[:3], out[3:]


def attend_back_kernel(
    scale, scal, dctx, probs, q, k, v, bk, bq_t, key_table, queryt_table,
    dq_o, dk_o, dv_o, gbk_o, gbq_o,
):
    half = key_table.shape[1] // 2
    sin, cos = key_table[:, :half].astype(f32), key_table[:, half:].astype(f32)
    cos_t, sin_t = queryt_table[:half].astype(f32), queryt_table[half:].astype(f32)
    qt2, vt2, dctxt2 = q[...].T, v[...].T, dctx[...].T
    dqs, dks, dvs, gbks = [], [], [], []
    for j in range(2):
        at = slice(j * HEAD_DIM, (j + 1) * HEAD_DIM)
        weights = probs[j]
        wide = weights.astype(f32)
        dprobs = dot(dctx[:, at], vt2[at])
        inner = jnp.sum(wide * dprobs, -1, keepdims=True)
        draw = (scale * (wide * (dprobs - inner))).astype(low)
        dvs.append(dot(dctxt2[at], weights))
        g = dot(draw, key_table[...])
        g_u, g_l = g[:, :half], g[:, half:]
        da = jnp.concatenate(
            [(g_u * cos - g_l * sin).astype(low), (g_u * sin + g_l * cos).astype(low)], 1
        )
        dqs.append(dot(draw, k[:, at]) + dot(da, bk[:, at]))
        gbks.append(dot(qt2[at], da))
        g = dot(queryt_table[...], draw)
        g_u, g_l = g[:half], g[half:]
        db = jnp.concatenate(
            [(g_u * sin_t - g_l * cos_t).astype(low), (g_u * cos_t + g_l * sin_t).astype(low)], 0
        )
        dks.append(dot(qt2[at], draw) + dot(bq_t[at], db))
        gbq_o[:, at] = dot(db, k[:, at]).astype(low)
    dq_o[...] = jnp.concatenate(dqs, 1).astype(low)
    dk_o[...] = jnp.concatenate(dks, 0).astype(low).T
    dv_o[...] = jnp.concatenate(dvs, 0).astype(low).T
    gbk_o[...] = jnp.concatenate(gbks, 0).astype(low)


def attend_back(first, count, scal, dctx, probs, q, k, v, bk, bq_t, tables, done=()):
    length = dctx.shape[0]
    half = tables[0].shape[1] // 2
    width, two = 2 * half, 2 * HEAD_DIM
    pair = pl.BlockSpec((length, two), lambda p: (0, first + p))
    out = pl.BlockSpec((length, two), lambda p: (0, p))
    flops = 4 * count * length * (8 * half * HEAD_DIM + length * (4 * half + 4 * HEAD_DIM))
    return call(
        functools.partial(attend_back_kernel, HEAD_DIM**-0.5),
        "attend_back",
        flops,
        count * 2e6,
        [shape(length, count * two)] * 3 + [shape(count * two, width), shape(width, count * two)],
        [out] * 3 + [pl.BlockSpec((two, width), lambda p: (p, 0)), pl.BlockSpec((width, two), lambda p: (0, p))],
        [SMEM, pair, pl.BlockSpec((2, length, length), lambda p: (p, 0, 0))]
        + [pair] * 3
        + [pl.BlockSpec((width, two), lambda p: (0, first + p)), pl.BlockSpec((two, width), lambda p: (first + p, 0))]
        + [VMEM] * 2,
        [],
        (scal, dctx, probs, q, k, v, bk, bq_t, tables[1], tables[2]),
        (count,),
        done=done,
    )


def project_back_kernel(
    count, plan, scal, rows_t, dq_a, dk_a, dv_a, dq_b, dk_b, dv_b, gbk_a, gbk_b, gbq_a, gbq_b, ups, ones, twos, *refs
):
    sums, outs, (grads, turned, sems) = refs[:2], refs[2 : 2 + count], refs[2 + count :]
    for side, ref in enumerate(sums):
        ref[...] = jnp.zeros(ref.shape, f32)
        ref[1:2, : ups.shape[1]] = ups[side : side + 1]
        ref[2:5, : ones.shape[1]] = ones[...]
        ref[5:8, : twos.shape[1]] = twos[...]
    size = turned.shape[2] // 2
    gbk = jnp.concatenate([gbk_a[...], gbk_b[...]], 0).T
    gbq = jnp.concatenate([gbq_a[...], gbq_b[...]], 1)
    for side in range(2):
        turned[side, :, :size] = sides(gbk, side)
        turned[side, :, size:] = sides(gbq, side)
    for i, (one, two) in enumerate(((dq_a, dq_b), (dk_a, dk_b), (dv_a, dv_b))):
        value = jnp.concatenate([one[...], two[...]], 1)
        value = jnp.concatenate([sides(value, side) for side in range(2)], 1)
        total = col(value.astype(f32))
        grad = dot(rows_t[...], value).astype(low)
        for side in range(2):
            sums[side][0:1, i * size : (i + 1) * size] = total[:, side * size : (side + 1) * size]
            grads[side, :, (2 + i) * size : (3 + i) * size] = grad[:, side * size : (side + 1) * size]
    rows = turned.shape[1] // BLOCKS
    for b in range(BLOCKS):
        to = ((b // 2) % 2) * 4 + (b // 4) * 2 + b % 2
        for side in range(2):
            grads[side, b * rows : (b + 1) * rows, : 2 * size] = turned[side, to * rows : (to + 1) * rows]
    finish(deal(grads, outs, sems, (scal[0], scal[1]), plan))


def project_back(scal, rows_t, grads, boxes, sums, done=()):
    width, length = rows_t.shape
    cols = grads[0].shape[1] + grads[3].shape[1]
    parts = part_shapes(width, 5 * cols // 2)
    out = call(
        functools.partial(project_back_kernel, len(parts), plans("scatter")),
        "project_back",
        6 * length * width * cols,
        cols * 15e3,
        [shape(8, 5 * cols // 2, dtype=f32)] * 2 + parts,
        [VMEM] * 2 + [ANYWHERE] * len(parts),
        [SMEM] + [VMEM] * 14,
        [pltpu.VMEM((2, width, 5 * cols // 2), low), pltpu.VMEM((2, width, cols), low), COPIES],
        (scal, rows_t, *grads, *boxes, *sums),
        done=done,
    )
    return out[0], out[1], out[2:]


def tokens_back_kernel(count, plan, scal, dq_a, dk_a, dv_a, dq_b, dk_b, dv_b, *refs):
    parts, (part_o, proj, sems) = refs[:count], refs[count:]
    hc = proj.shape[2] // 4
    copies = fetch(parts, proj, sems, (scal[0], scal[1]), plan, False, (2 * hc, 4 * hc))
    both = [jnp.concatenate([a[...], b[...]], 1) for a, b in ((dq_a, dq_b), (dk_a, dk_b), (dv_a, dv_b))]
    grads = [jnp.concatenate([sides(g, side) for g in both], 1) for side in range(2)]
    finish(copies)
    total = dot(grads[0], proj[0, :, : 3 * hc], NT) + dot(grads[1], proj[1, :, : 3 * hc], NT)
    part_o[...] = total.astype(low)


def tokens_back(scal, grads, parts, width, done=()):
    length = grads[0].shape[0]
    hc = parts[0].shape[2] // 6
    return call(
        functools.partial(tokens_back_kernel, len(parts), plans("early")),
        "tokens_back",
        12 * length * width * hc,
        5e6,
        shape(length, width),
        VMEM,
        [SMEM] + [VMEM] * 6 + [ANYWHERE] * len(parts),
        [pltpu.VMEM((2, width, 4 * hc), low), COPIES],
        (scal, *grads, *parts),
        done=done,
    )


def rows_kernel(scal, mine, sent, passed, out):
    length, half = mine.shape[0], sent.shape[0]
    page, core = scal[3], scal[4]
    out[pl.ds(pl.multiple_of(page * length, length), length)] = mine[...]
    out[pl.ds(pl.multiple_of((1 - page) * length + core * half, half), half)] = sent[...]
    out[pl.ds(pl.multiple_of((1 - page) * length + (1 - core) * half, half), half)] = passed[...]


def all_rows(scal, mine, sent, passed):
    length, width = mine.shape
    return call(
        rows_kernel, "all_rows", 0, 8 * length * width, shape(2 * length, width), VMEM, [SMEM] + [VMEM] * 3, [],
        (scal, mine, sent, passed),
    )


def sum_columns(a):
    return a + swap_dp(a, 1) if grid_dp()[0] > 1 else lax.psum(a, "dp")


def local(
    tokens, lengths, boxes, query_weight, key_weight, value_weight, query_bias, key_bias, value_bias,
    box_key_weight, box_query_weight, out_weight, out_bias, first_gain, first_shift, up_weight, up_bias,
    down_weight, down_bias, second_gain, second_shift, output_grad,
):
    pages = lengths.shape[0]
    page_len = tokens.shape[0] // pages
    width = tokens.shape[1]
    hc = query_weight.shape[1]
    units = up_weight.shape[1]

    page = lax.axis_index("head") // (lax.axis_size("head") // pages)
    start = page * page_len
    rows = lax.dynamic_slice_in_dim(tokens, start, page_len, 0)
    grad_rows = lax.dynamic_slice_in_dim(output_grad, start, page_len, 0)
    box_rows = lax.dynamic_slice_in_dim(boxes, start, page_len, 1)
    length = lax.dynamic_slice_in_dim(lengths, page, 1, 0)[0]
    biases = jnp.concatenate([query_bias, key_bias, value_bias, up_bias])[None].astype(low)
    biases = jnp.concatenate([biases, swap_page(biases)], 0).astype(f32)
    vecs_one = jnp.stack([out_bias, first_gain, first_shift]).astype(f32)
    vecs_two = jnp.stack([down_bias, second_gain, second_shift]).astype(f32)
    frequency = (10000.0 ** (-jnp.arange(width // 4, dtype=f32) / (width // 4)))[None]
    z, y = place_dp()
    core = lax.axis_index("head") % (lax.axis_size("head") // pages)
    at = jnp.arange(5, dtype=jnp.int32)
    scal = sum(jnp.where(at == i, value.astype(jnp.int32), 0) for i, value in enumerate((z, y, length, page, core)))
    rows_t = rows.T

    first = jnp.concatenate(
        [box_key_weight, box_query_weight, query_weight, key_weight, value_weight, out_weight.T], 1
    )
    line_1 = gather_line(first)
    tables = box_tables(after(box_rows.T, line_1[-1]).astype(f32), frequency)
    line_2 = gather_line(after(up_weight, *line_1[1:]))
    parts_1 = gather_early(line_1, (*tables, rows_t, rows, grad_rows, biases, scal, vecs_one, vecs_two), line_2[1:])
    line_3 = gather_line(after(down_weight.T, *line_2[1:]))
    parts_2 = gather_near(after(jnp.concatenate(line_2, 0), *parts_1[-2:]))

    pairs = hc // HEAD_DIM
    query, key, value, key_t, bk_t, bq, bk, bq_t = project(scal, rows, biases[:, : 3 * hc], parts_1)
    parts_3 = gather_near(jnp.concatenate(after(list(line_3), *parts_2[1:], query), 0))
    near_2, near_3 = parts_2[1:], parts_3[1:]
    parts_2 = gather_far(parts_2)
    parts_3 = gather_far(parts_3)
    ctx_a, probs_a = attend(1, scal, query, value, key_t, bk_t, bq, tables)
    mine, context, probs_b = attend_last(1, scal, query, value, key_t, bk_t, bq, tables, ctx_a, parts_1, near_2)
    mine = after(mine, *near_3, *parts_2[3:])
    attn, attn_theirs = mine, swap_core(mine)
    hidden, active, slope = feed_up(
        scal, attn, attn_theirs, rows, vecs_one, biases[:, 3 * hc :], parts_2
    )
    feed = feed_down(scal, active, parts_3, width)
    (result, grad_two, feed_low, sums_two), grads_3 = feed_back(
        scal, feed, swap_core(feed), hidden, grad_rows, vecs_two, active
    )
    grads_3 = scatter_far(grads_3)
    grad_inner, sums_up, mine = inner_back(scal, feed_low, slope, parts_3, parts_2)
    (grad_one, grad_context, sums_one), grads_2 = norm_back(
        scal, mine, swap_core(mine), grad_two, attn, attn_theirs, rows, vecs_one, grad_inner, context,
        parts_1, grads_3[1:],
    )
    grads_3 = scatter_near(grads_3)
    grads_2 = scatter_far(grads_2)
    *grads_a, gbk_a, gbq_a = attend_back(
        0, 1, scal, grad_context, probs_a, query, key, value, bk, bq_t, tables, grads_3
    )
    sum_3 = scatter_line(grads_3)
    *grads_b, gbk_b, gbq_b = attend_back(
        1, pairs - 1, scal, grad_context, probs_b, query, key, value, bk, bq_t, tables, (*grads_2[1:], gbk_a)
    )
    grads_2 = scatter_near(after(list(grads_2), gbk_a))
    grads = [*grads_a, *grads_b]
    own_small, oth_small, grads_1 = project_back(
        scal, rows_t, grads, [gbk_a, gbk_b, gbq_a, gbq_b], (sums_up, sums_one, sums_two), (*grads_2, sum_3)
    )
    sum_2 = scatter_line(grads_2)
    grads_1 = scatter_far(grads_1)
    grads_1 = scatter_near(after(list(grads_1), sum_2))
    small = own_small + swap_page(after(oth_small, *grads_1))
    half = page_len // 2

    def send_half(mine):
        return swap_page(lax.dynamic_slice_in_dim(mine, core * half, half, 0))

    sent = send_half(after(result, *grads_1, small))
    mine = tokens_back(scal, grads, parts_1, width, grads_1)
    token_grad = (grad_one + (mine.astype(f32) + swap_core(mine).astype(f32))).astype(low)
    sent_grad = send_half(token_grad)
    small = sum_columns(small)
    small = sum_lines(small)
    sum_1 = scatter_line(grads_1, lambda: (sent, sent_grad, small))

    return (
        all_rows(scal, result, sent, swap_core(sent)),
        all_rows(scal, token_grad, sent_grad, swap_core(sent_grad)),
        sum_1[:, 2 * hc : 3 * hc],
        sum_1[:, 3 * hc : 4 * hc],
        sum_1[:, 4 * hc :],
        small[0, :hc],
        small[0, hc : 2 * hc],
        small[0, 2 * hc : 3 * hc],
        sum_1[:, :hc],
        sum_1[:, hc : 2 * hc],
        sum_2[:, units:].T,
        small[2, :width],
        small[3, :width],
        small[4, :width],
        sum_2[:, :units],
        small[1, :units],
        sum_3.T,
        small[5, :width],
        small[6, :width],
        small[7, :width],
    )


def solution(mesh):
    row, vec, mat, tam, all_ = P("dp", None), P("head"), P("dp", "head"), P("head", "dp"), P()
    return jax.shard_map(
        local,
        mesh=mesh,
        in_specs=(
            row, P("dp"), P(None, "dp"), mat, mat, mat, vec, vec, vec, mat, mat, tam, all_, all_, all_,
            mat, vec, tam, all_, all_, all_, row,
        ),
        out_specs=(
            row, row, mat, mat, mat, vec, vec, vec, mat, mat, tam, all_, all_, all_, mat, vec, tam,
            all_, all_, all_,
        ),
        check_vma=False,
    )
```

```python
import functools

import jax
import jax.numpy as jnp
from jax import lax
from jax.experimental import pallas as pl
from jax.experimental.pallas import tpu as pltpu
from jax.sharding import PartitionSpec as P

HEAD_DIM = 64
norm_eps = 1e-05
sqrt_half = 0.7071067811865476
inv_root_two_pi = 0.3989422804014327
low = jnp.bfloat16
f32 = jnp.float32


def dot(left, right, axes=((1,), (0,))):
    return lax.dot_general(left, right, (axes, ((), ())), preferred_element_type=f32)


def permute(a, axis, name, partner):
    pairs = [(i, partner(i)) for i in range(lax.axis_size(axis))]
    with jax.named_scope("%s_%d_%d" % (name, a.shape[0], a.shape[-1])):
        return lax.ppermute(a, axis, pairs)


def swap_core(a):
    return permute(a, "head", "core", lambda i: i ^ 1)


def swap_page(a):
    return permute(a, "head", "page", lambda i: i ^ 2)


def swap_dp(a, bit):
    return permute(a, "dp", "column", lambda i: i ^ bit)


def turn_dp(a, step):
    n = lax.axis_size("dp")
    return permute(a, "dp", "line", lambda i: (i + step) % n)


VMEM_LIMIT = 56 * 1024 * 1024
VMEM_SMALL = 24 * 1024 * 1024
SMALL = (
    "box_tables", "project", "attend", "attend_last", "feed_up", "feed_down", "feed_back", "tokens_back", "all_rows",
)
BLOCKS = 8


def grid_dp():
    return (4, 2) if lax.axis_size("dp") == 8 else (1, 1)


def place_dp():
    index = lax.axis_index("dp")
    return (index // 2, index % 2) if lax.axis_size("dp") == 8 else (index * 0, index * 0)


def after(value, *done):
    return lax.optimization_barrier((value, *done))[0] if done else value


def block_plan(kind):
    nz, ny = grid_dp()
    if nz == 1:
        return (((0, 0, 0),), ((1, 0, 0),))
    half = nz // 2

    def run(side, ky, start, end):
        return tuple((side, ky, k) for k in range(start, end))

    far = (run(1, 1, 0, half), run(1, 1, half, nz))
    if kind == "early":
        return tuple(run(*block, *cut) for cut in ((0, 1), (1, nz)) for block in ((0, 0), (1, 0), (0, 1))) + far
    if kind == "scatter":
        return (run(0, 0, 0, nz),) + tuple(run(*block, *cut) for block in ((1, 0), (0, 1)) for cut in ((0, half), (half, nz))) + far
    return tuple(run(*block, 0, nz) for block in ((0, 0), (1, 0), (0, 1))) + far


def gather_line(shard):
    nz, ny = grid_dp()
    if nz == 1:
        return [lax.all_gather(shard, "dp", axis=0, tiled=True)[None]]
    return [shard[None]] + [turn_dp(shard, ny * k)[None] for k in range(1, nz)]


def gather_near(line):
    if grid_dp()[0] == 1:
        return [line, swap_page(line)]
    return [line, swap_page(line), swap_dp(line, 1)]


def gather_far(parts, done=()):
    half = grid_dp()[0] // 2
    if half == 0:
        return parts
    line, across, beside = parts
    far_a, far_b = after((across[:half], beside[half:]), *done)
    return [line, across, beside, swap_dp(far_a, 1), swap_page(far_b)]


def gather_early(line, near_done, far_done):
    nz = grid_dp()[0]
    if nz == 1:
        return gather_near(line[0])
    own = gather_near(line[0])
    rest = gather_near(after(jnp.concatenate(line[1:], 0), *own, *near_done))
    cut = nz // 2 - 1
    far_a, far_b = after((jnp.concatenate([own[1], rest[1][:cut]], 0), rest[2][cut:]), *rest[1:], *far_done)
    return own + rest + [swap_dp(far_a, 1), swap_page(far_b)]


def add(a, b):
    return (a.astype(f32) + b.astype(f32)).astype(low)


def scatter_far(parts):
    if grid_dp()[0] == 1:
        return parts
    line, across_a, across_b, beside_a, beside_b, far_a, far_b = parts
    far_a = swap_page(far_a)
    far_b = swap_dp(far_b, 1)
    beside = jnp.concatenate([add(beside_a, far_a), beside_b], 0)
    across = jnp.concatenate([across_a, add(across_b, far_b)], 0)
    return [line, across, beside]


def scatter_near(parts):
    line = parts[0].astype(f32) + swap_page(parts[1]).astype(f32)
    if len(parts) > 2:
        line = line + swap_dp(parts[2], 1).astype(f32)
    return [line[0]] + [line[k].astype(low) for k in range(1, line.shape[0])]


def scatter_line(line, done=lambda: ()):
    nz, ny = grid_dp()
    if nz == 1:
        return lax.psum_scatter(line[0].astype(low), "dp", scatter_dimension=0, tiled=True).astype(f32)
    come = [turn_dp(line[k], ny * k) for k in range(1, nz)]
    return functools.reduce(jnp.add, [piece.astype(f32) for piece in after(come, *done())], line[0])


def sum_lines(a):
    nz, ny = grid_dp()
    return functools.reduce(jnp.add, [turn_dp(a, ny * k) for k in range(1, nz)], a)


def part_shapes(blocks, width):
    nz, ny = grid_dp()
    return [jax.ShapeDtypeStruct((len(p), blocks // (nz * ny), width), low) for p in block_plan("scatter")]


def slots(parts, place, dims, sign, turned, plan):
    nz, ny = dims
    found = []
    for part, blocks in zip(parts, plan):
        for i, (side, ky, kz) in enumerate(blocks):
            piece = part.at[i]
            rows = piece.shape[0]
            z = lax.rem(place[0] + (sign * kz) % nz, nz) if nz > 1 else 0
            y = lax.rem(place[1] + ky, ny) if ny > 1 else 0
            block = z * ny + y
            if not turned:
                found.append((piece, side, pl.multiple_of(block * rows, rows)))
                continue
            size = rows * nz * ny // BLOCKS
            for sub in range(rows // size):
                b = block * (rows // size) + sub
                b = lax.rem(lax.div(b, 2), 2) * 4 + lax.div(b, 4) * 2 + lax.rem(b, 2)
                found.append((piece.at[pl.ds(sub * size, size)], side, pl.multiple_of(b * size, size)))
    return found


def fetch(parts, whole, sems, place, plan, turned=False, columns=None, start=True):
    dims, plan = plan
    copies = []
    for i, (piece, side, row) in enumerate(slots(parts, place, dims, -1, turned, plan)):
        source = piece if columns is None else piece.at[:, pl.ds(columns[0], columns[1])]
        copies.append(pltpu.make_async_copy(source, whole.at[side, pl.ds(row, piece.shape[0])], sems.at[i]))
    for copy in copies if start else []:
        copy.start()
    return copies


def deal(whole, parts, sems, place, plan, turned=False, columns=None):
    dims, plan = plan
    copies = []
    for i, (piece, side, row) in enumerate(slots(parts, place, dims, 1, turned, plan)):
        target = piece if columns is None else piece.at[:, pl.ds(columns[0], columns[1])]
        copies.append(pltpu.make_async_copy(whole.at[side, pl.ds(row, piece.shape[0])], target, sems.at[i]))
    for copy in copies:
        copy.start()
    return copies


def plans(kind):
    return grid_dp(), block_plan(kind)


def finish(copies):
    for copy in copies:
        copy.wait()


SMEM = pl.BlockSpec(memory_space=pltpu.SMEM)
VMEM = pl.BlockSpec(memory_space=pltpu.VMEM)
ANYWHERE = pl.BlockSpec(memory_space=pl.ANY)
COPIES = pltpu.SemaphoreType.DMA((2 * BLOCKS,))


def call(kernel, name, flops, moved, outs, out_specs, in_specs, scratch, args, grid=None, exps=0, done=()):
    extra = {} if grid is None else {"grid": grid}

    def body(*refs):
        kernel(*refs[: len(args)], *refs[len(args) + len(done) :])

    return pl.pallas_call(
        body,
        out_shape=outs,
        in_specs=in_specs + [ANYWHERE] * len(done),
        out_specs=out_specs,
        scratch_shapes=scratch,
        compiler_params=pltpu.CompilerParams(vmem_limit_bytes=VMEM_SMALL if name in SMALL else VMEM_LIMIT),
        cost_estimate=pl.CostEstimate(flops=int(flops), bytes_accessed=int(moved), transcendentals=int(exps)),
        name=name,
        **extra,
    )(*args, *done)


def shape(*dims, dtype=low):
    return jax.ShapeDtypeStruct(dims, dtype)


NT = ((1,), (1,))


def project_kernel(count, plan, scal, rows, bias, *refs):
    parts, refs = refs[:count], refs[count:]
    (q_o, k_o, v_o, key_t, bk_t, bq, bk, bq_t), (box, proj, sems, more_sems) = refs[:8], refs[8:]
    hc = box.shape[2] // 2
    place = (scal[0], scal[1])
    first = fetch(parts, proj, more_sems, place, plan, False, (2 * hc, 4 * hc))
    second = fetch(parts, box, sems, place, plan, True, (0, 2 * hc))
    finish(first)
    heads = hc // HEAD_DIM
    pairs = [[], [], []]
    for side in range(2):
        qkv = (dot(rows[...], proj[side, :, : 3 * hc]) + bias[side : side + 1]).astype(low)
        for i in range(3):
            pairs[i].append(qkv[:, i * hc : (i + 1) * hc])

    def paired(own, other, axis):
        cut = [slice(h * HEAD_DIM, (h + 1) * HEAD_DIM) for h in range(heads)]
        both = [(own[c], other[c]) if axis == 0 else (own[:, c], other[:, c]) for c in cut]
        return jnp.concatenate([one for two in both for one in two], axis)

    for ref, two in zip((q_o, k_o, v_o), pairs):
        ref[...] = paired(*two, 1)
    key_t[...] = k_o[...].T
    finish(second)
    bk[...] = paired(box[0, :, :hc], box[1, :, :hc], 1)
    bq[...] = paired(box[0, :, hc:], box[1, :, hc:], 1)
    bk_t[...] = bk[...].T
    bq_t[...] = bq[...].T


def project(scal, rows, bias, parts, done=()):
    length, width = rows.shape
    hc = parts[0].shape[2] // 6
    return call(
        functools.partial(project_kernel, len(parts), plans("early")),
        "project",
        12 * length * width * hc,
        10e6,
        [shape(length, 2 * hc)] * 3 + [shape(2 * hc, length), shape(2 * hc, width), shape(width, 2 * hc)]
        + [shape(width, 2 * hc), shape(2 * hc, width)],
        [VMEM] * 8,
        [SMEM, VMEM, VMEM] + [ANYWHERE] * len(parts),
        [pltpu.VMEM((2, width, 2 * hc), low), pltpu.VMEM((2, width, 4 * hc), low), COPIES, COPIES],
        (scal, rows, bias, *parts),
        done=done,
    )


def attend_pair(scale, length, q, v, key_t, bk_t, bq, query_table, queryt_table, keyt_table, p_o):
    half = query_table.shape[1] // 2
    cos, sin = query_table[:, :half].astype(f32), query_table[:, half:].astype(f32)
    cos_t, sin_t = queryt_table[:half].astype(f32), queryt_table[half:].astype(f32)
    valid = lax.broadcasted_iota(jnp.int32, (1, key_t.shape[1]), 1) < length
    outs = []
    for j in range(2):
        at = slice(j * HEAD_DIM, (j + 1) * HEAD_DIM)
        a = dot(q[:, at], bk_t[at])
        a_s, a_c = a[:, :half], a[:, half:]
        turn = jnp.concatenate(
            [(a_s * cos + a_c * sin).astype(low), (a_c * cos - a_s * sin).astype(low)], 1
        )
        b = dot(bq[:, at], key_t[at])
        b_s, b_c = b[:half], b[half:]
        turn_t = jnp.concatenate(
            [(b_s * sin_t + b_c * cos_t).astype(low), (b_c * sin_t - b_s * cos_t).astype(low)], 0
        )
        raw = dot(q[:, at], key_t[at]) + dot(turn, keyt_table[...]) + dot(query_table[...], turn_t)
        scores = jnp.where(valid, raw * scale, -1e9)
        exponent = jnp.exp(scores - jnp.max(scores, -1, keepdims=True))
        probs = (exponent * (1.0 / jnp.sum(exponent, -1, keepdims=True))).astype(low)
        p_o[j] = probs
        outs.append(dot(probs, v[:, at]))
    return jnp.concatenate(outs, 1).astype(low)


def attend_kernel(scale, scal, q, v, key_t, bk_t, bq, query_table, queryt_table, keyt_table, ctx_o, p_o):
    ctx_o[...] = attend_pair(
        scale, scal[2], q, v, key_t, bk_t, bq, query_table, queryt_table, keyt_table, p_o
    )


def attend_last_kernel(
    scale, count, plan, scal, q, v, key_t, bk_t, bq, query_table, queryt_table, keyt_table, ctx_a, *refs
):
    parts, (part_o, ctx_o, p_o, out_w, pairs, sems) = refs[:count], refs[count:]
    step = pl.program_id(0)
    hc = out_w.shape[2] // 2

    @pl.when(step == 0)
    def _():
        fetch(parts, out_w, sems, (scal[0], scal[1]), plan, False, (4 * hc, 2 * hc))

    pairs[step] = attend_pair(
        scale, scal[2], q, v, key_t, bk_t, bq, query_table, queryt_table, keyt_table, p_o
    )

    @pl.when(step == pl.num_programs(0) - 1)
    def _():
        ctx = jnp.concatenate([ctx_a[...]] + [pairs[i] for i in range(pairs.shape[0])], 1)
        both = [sides(ctx, side) for side in range(2)]
        ctx_o[...] = jnp.concatenate(both, 1)
        finish(fetch(parts, out_w, sems, (scal[0], scal[1]), plan, False, (4 * hc, 2 * hc), False))
        part_o[...] = (dot(both[0], out_w[0, :, hc:], NT) + dot(both[1], out_w[1, :, hc:], NT)).astype(low)


def attend_specs(first, length, half):
    two = 2 * HEAD_DIM
    wide = pl.BlockSpec((length, two), lambda p: (0, first + p))
    return [
        SMEM,
        wide,
        wide,
        pl.BlockSpec((two, length), lambda p: (first + p, 0)),
        pl.BlockSpec((two, 2 * half), lambda p: (first + p, 0)),
        pl.BlockSpec((2 * half, two), lambda p: (0, first + p)),
    ] + [VMEM] * 3


def attend_flops(count, length, half):
    return 4 * count * length * (4 * half * HEAD_DIM + length * (4 * half + 2 * HEAD_DIM))


def attend(count, scal, q, v, key_t, bk_t, bq, tables, done=()):
    length, half = tables[0].shape[0], tables[0].shape[1] // 2
    two = 2 * HEAD_DIM
    return call(
        functools.partial(attend_kernel, HEAD_DIM**-0.5),
        "attend",
        attend_flops(count, length, half),
        count * 2e6,
        [shape(length, count * two), shape(2 * count, length, length)],
        [pl.BlockSpec((length, two), lambda p: (0, p)), pl.BlockSpec((2, length, length), lambda p: (p, 0, 0))],
        attend_specs(0, length, half),
        [],
        (scal, q, v, key_t, bk_t, bq, tables[0], tables[2], tables[3]),
        (count,),
        2 * count * length * length,
        done,
    )


def attend_last(first, scal, q, v, key_t, bk_t, bq, tables, ctx_a, parts, done=()):
    length, half = tables[0].shape[0], tables[0].shape[1] // 2
    width, hc = 2 * half, parts[0].shape[2] // 6
    count = hc // HEAD_DIM - first
    two = 2 * HEAD_DIM
    return call(
        functools.partial(attend_last_kernel, HEAD_DIM**-0.5, len(parts), plans("early")),
        "attend_last",
        attend_flops(count, length, half),
        count * 2e6,
        [shape(length, width), shape(length, 2 * hc), shape(2 * count, length, length)],
        [
            pl.BlockSpec((length, width), lambda p: (0, 0)),
            pl.BlockSpec((length, 2 * hc), lambda p: (0, 0)),
            pl.BlockSpec((2, length, length), lambda p: (p, 0, 0)),
        ],
        attend_specs(first, length, half) + [VMEM] + [ANYWHERE] * len(parts),
        [pltpu.VMEM((2, width, 2 * hc), low), pltpu.VMEM((count, length, two), low), COPIES],
        (scal, q, v, key_t, bk_t, bq, tables[0], tables[2], tables[3], ctx_a, *parts),
        (count,),
        2 * count * length * length,
        done,
    )


def sides(values, side):
    heads = values.shape[1] // HEAD_DIM
    return jnp.concatenate([values[:, h * HEAD_DIM : (h + 1) * HEAD_DIM] for h in range(side, heads, 2)], 1)


def tables_kernel(boxes, frequency, query_o, key_o, queryt_o, keyt_o):
    width = frequency.shape[1]
    half = 2 * width
    for c in range(2):
        angles = boxes[:, c : c + 1] * frequency[...]
        cosine, sine = jnp.cos(angles), jnp.sin(angles)
        at, past = slice(c * width, (c + 1) * width), slice(half + c * width, half + (c + 1) * width)
        query_o[:, at] = cosine.astype(low)
        query_o[:, past] = sine.astype(low)
    key_o[:, :half] = query_o[:, half:]
    key_o[:, half:] = query_o[:, :half]
    queryt_o[...] = query_o[...].T
    keyt_o[:half] = queryt_o[half:]
    keyt_o[half:] = queryt_o[:half]


def box_tables(boxes, frequency):
    length, half = boxes.shape[0], 2 * frequency.shape[1]
    return call(
        tables_kernel,
        "box_tables",
        40 * length * half,
        3e6,
        [shape(length, 2 * half)] * 2 + [shape(2 * half, length)] * 2,
        [VMEM] * 4,
        [VMEM] * 2,
        [],
        (boxes, frequency),
    )


def standard(values):
    centered = values - jnp.mean(values, -1, keepdims=True)
    inverse = lax.rsqrt(jnp.mean(centered * centered, -1, keepdims=True) + norm_eps)
    return centered * inverse, inverse


def standard_back(upstream, scaled, inverse):
    return inverse * (
        upstream - jnp.mean(upstream, -1, keepdims=True) - scaled * jnp.mean(upstream * scaled, -1, keepdims=True)
    )


def col(values):
    return jnp.sum(values, 0, keepdims=True)


def feed_up_kernel(count, plan, scal, mine, theirs, rows, vecs, bias, *refs):
    ups, refs = refs[:count], refs[count:]
    (hidden_o, active_o, slope_o), (up, sems) = refs[:3], refs[3:]
    copies = fetch(ups, up, sems, (scal[0], scal[1]), plan)
    total = rows[...].astype(f32) + (mine[...].astype(f32) + theirs[...].astype(f32)) + vecs[0:1]
    scaled, _ = standard(total)
    hidden = scaled * vecs[1:2] + vecs[2:3]
    hidden_o[...] = hidden
    hidden_low = hidden.astype(low)
    finish(copies)
    width = up.shape[2]
    size = 256
    for side in range(2):
        for at in range(0, width, size):
            inner = dot(hidden_low, up[side, :, at : at + size]) + bias[side : side + 1, at : at + size]
            cumulative = 0.5 * (1.0 + lax.erf(inner * sqrt_half))
            density = jnp.exp(-0.5 * inner * inner) * inv_root_two_pi
            active_o[:, side * width + at : side * width + at + size] = (inner * cumulative).astype(low)
            slope_o[:, side * width + at : side * width + at + size] = (cumulative + inner * density).astype(low)


def feed_up(scal, mine, theirs, rows, vecs, bias, ups, done=()):
    length, width = rows.shape
    units = ups[0].shape[2]
    return call(
        functools.partial(feed_up_kernel, len(ups), plans("gather")),
        "feed_up",
        4 * length * width * units,
        11e6,
        [
            shape(length, width, dtype=f32),
            shape(length, 2 * units),
            shape(length, 2 * units),
        ],
        [VMEM] * 3,
        [SMEM] + [VMEM] * 5 + [ANYWHERE] * len(ups),
        [pltpu.VMEM((2, width, units), low), COPIES],
        (scal, mine, theirs, rows, vecs, bias, *ups),
        exps=2 * length * units,
        done=done,
    )


def feed_down_kernel(count, plan, scal, active, *refs):
    downs, (part_o, down, sems) = refs[:count], refs[count:]
    finish(fetch(downs, down, sems, (scal[0], scal[1]), plan))
    units = down.shape[2]
    part_o[...] = (dot(active[:, :units], down[0], NT) + dot(active[:, units:], down[1], NT)).astype(low)


def feed_down(scal, active, downs, width, done=()):
    length, units = active.shape[0], active.shape[1] // 2
    return call(
        functools.partial(feed_down_kernel, len(downs), plans("gather")),
        "feed_down",
        4 * length * width * units,
        5e6,
        shape(length, width),
        VMEM,
        [SMEM, VMEM] + [ANYWHERE] * len(downs),
        [pltpu.VMEM((2, width, units), low), COPIES],
        (scal, active, *downs),
        done=done,
    )


def feed_back_kernel(count, plan, scal, mine, theirs, hidden, grad_out, vecs, active, *refs):
    (result_o, grad_o, low_o, sums_o), outs, (grads, sems) = refs[:4], refs[4 : 4 + count], refs[4 + count :]
    scaled, inverse = standard(hidden[...] + (mine[...].astype(f32) + theirs[...].astype(f32)) + vecs[0:1])
    result_o[...] = (scaled * vecs[1:2] + vecs[2:3]).astype(low)
    grad = grad_out[...].astype(f32)
    sums_o[1:2] = col(grad * scaled)
    sums_o[2:3] = col(grad)
    grad = standard_back(grad * vecs[1:2], scaled, inverse)
    sums_o[0:1] = col(grad)
    grad_o[...] = grad
    grad_low = grad.astype(low)
    low_o[...] = grad_low
    turned = grad_low.T
    units = grads.shape[2]
    for side in range(2):
        grads[side] = dot(turned, active[:, side * units : (side + 1) * units]).astype(low)
    finish(deal(grads, outs, sems, (scal[0], scal[1]), plan))


def feed_back(scal, mine, theirs, hidden, grad_out, vecs, active):
    length, width = hidden.shape
    units = active.shape[1] // 2
    parts = part_shapes(width, units)
    out = call(
        functools.partial(feed_back_kernel, len(parts), plans("scatter")),
        "feed_back",
        4 * length * width * units,
        12e6,
        [shape(length, width), shape(length, width, dtype=f32), shape(length, width), shape(3, width, dtype=f32)] + parts,
        [VMEM] * 4 + [ANYWHERE] * len(parts),
        [SMEM] + [VMEM] * 6,
        [pltpu.VMEM((2, width, units), low), COPIES],
        (scal, mine, theirs, hidden, grad_out, vecs, active),
    )
    return out[:4], out[4:]


def inner_back_kernel(count, plan, scal, grad_low, slope, *refs):
    downs, ups, refs = refs[:count], refs[count : 2 * count], refs[2 * count :]
    (inner_o, sums_o, part_o), (down, up, sems, more_sems) = refs[:3], refs[3:]
    place = (scal[0], scal[1])
    first = fetch(downs, down, sems, place, plan)
    second = fetch(ups, up, more_sems, place, plan)
    finish(first)
    units = up.shape[2]
    for side in range(2):
        at = slice(side * units, (side + 1) * units)
        grad = (dot(grad_low[...], down[side]) * slope[:, at].astype(f32)).astype(low)
        inner_o[:, at] = grad
        sums_o[side : side + 1] = col(grad.astype(f32))
    finish(second)
    part = dot(inner_o[:, :units], up[0], NT) + dot(inner_o[:, units:], up[1], NT)
    part_o[...] = part.astype(low)


def inner_back(scal, grad_low, slope, downs, ups):
    length, width = grad_low.shape
    units = slope.shape[1] // 2
    return call(
        functools.partial(inner_back_kernel, len(ups), plans("gather")),
        "inner_back",
        8 * length * width * units,
        10e6,
        [shape(length, 2 * units), shape(2, units, dtype=f32), shape(length, width)],
        [VMEM] * 3,
        [SMEM] + [VMEM] * 2 + [ANYWHERE] * (2 * len(ups)),
        [pltpu.VMEM((2, width, units), low)] * 2 + [COPIES] * 2,
        (scal, grad_low, slope, *downs, *ups),
    )


def norm_back_kernel(count, given, plan, given_plan, scal, mine, theirs, grad_two, first, second, rows, vecs, grad_inner, ctx, *refs):
    weights, refs = refs[:given], refs[given:]
    (grad_o, dctx_o, sums_o), outs, (out_w, grads, sems) = refs[:3], refs[3 : 3 + count], refs[3 + count :]
    place = (scal[0], scal[1])
    hc = out_w.shape[2] // 2
    copies = fetch(weights, out_w, sems, place, given_plan, False, (4 * hc, 2 * hc))
    grad = grad_two[...] + (mine[...].astype(f32) + theirs[...].astype(f32))
    scaled, inverse = standard(rows[...].astype(f32) + (first[...].astype(f32) + second[...].astype(f32)) + vecs[0:1])
    hidden_low = (scaled * vecs[1:2] + vecs[2:3]).astype(low)
    sums_o[1:2] = col(grad * scaled)
    sums_o[2:3] = col(grad)
    grad = standard_back(grad * vecs[1:2], scaled, inverse)
    sums_o[0:1] = col(grad)
    grad_o[...] = grad
    grad_low = grad.astype(low)
    finish(copies)
    both = [dot(grad_low, out_w[side, :, hc:]).astype(low) for side in range(2)]
    cut = [slice(h * HEAD_DIM, (h + 1) * HEAD_DIM) for h in range(hc // HEAD_DIM)]
    dctx_o[...] = jnp.concatenate([one[:, c] for c in cut for one in both], 1)
    units = grads.shape[2] - hc
    turned = hidden_low.T
    for side in range(2):
        grads[side, :, :units] = dot(turned, grad_inner[:, side * units : (side + 1) * units]).astype(low)
    grad_ctx = dot(grad_low.T, ctx[...]).astype(low)
    for side in range(2):
        grads[side, :, units:] = grad_ctx[:, side * hc : (side + 1) * hc]
    finish(deal(grads, outs, sems, place, plan))


def norm_back(scal, mine, theirs, grad_two, first, second, rows, vecs, grad_inner, ctx, weights, done=()):
    length, width = grad_two.shape
    units, hc = grad_inner.shape[1] // 2, ctx.shape[1] // 2
    parts = part_shapes(width, units + hc)
    out = call(
        functools.partial(norm_back_kernel, len(parts), len(weights), plans("scatter"), plans("early")),
        "norm_back",
        4 * length * width * (units + 2 * hc),
        14e6,
        [shape(length, width, dtype=f32), shape(length, 2 * hc), shape(3, width, dtype=f32)] + parts,
        [VMEM] * 3 + [ANYWHERE] * len(parts),
        [SMEM] + [VMEM] * 9 + [ANYWHERE] * len(weights),
        [pltpu.VMEM((2, width, 2 * hc), low), pltpu.VMEM((2, width, units + hc), low), COPIES],
        (scal, mine, theirs, grad_two, first, second, rows, vecs, grad_inner, ctx, *weights),
        done=done,
    )
    return out[:3], out[3:]


def attend_back_kernel(
    scale, scal, dctx, probs, q, k, v, bk, bq_t, key_table, queryt_table,
    dq_o, dk_o, dv_o, gbk_o, gbq_o,
):
    half = key_table.shape[1] // 2
    sin, cos = key_table[:, :half].astype(f32), key_table[:, half:].astype(f32)
    cos_t, sin_t = queryt_table[:half].astype(f32), queryt_table[half:].astype(f32)
    qt2, vt2, dctxt2 = q[...].T, v[...].T, dctx[...].T
    dqs, dks, dvs, gbks = [], [], [], []
    for j in range(2):
        at = slice(j * HEAD_DIM, (j + 1) * HEAD_DIM)
        weights = probs[j]
        wide = weights.astype(f32)
        dprobs = dot(dctx[:, at], vt2[at])
        inner = jnp.sum(wide * dprobs, -1, keepdims=True)
        draw = (scale * (wide * (dprobs - inner))).astype(low)
        dvs.append(dot(dctxt2[at], weights))
        g = dot(draw, key_table[...])
        g_u, g_l = g[:, :half], g[:, half:]
        da = jnp.concatenate(
            [(g_u * cos - g_l * sin).astype(low), (g_u * sin + g_l * cos).astype(low)], 1
        )
        dqs.append(dot(draw, k[:, at]) + dot(da, bk[:, at]))
        gbks.append(dot(qt2[at], da))
        g = dot(queryt_table[...], draw)
        g_u, g_l = g[:half], g[half:]
        db = jnp.concatenate(
            [(g_u * sin_t - g_l * cos_t).astype(low), (g_u * cos_t + g_l * sin_t).astype(low)], 0
        )
        dks.append(dot(qt2[at], draw) + dot(bq_t[at], db))
        gbq_o[:, at] = dot(db, k[:, at]).astype(low)
    dq_o[...] = jnp.concatenate(dqs, 1).astype(low)
    dk_o[...] = jnp.concatenate(dks, 0).astype(low).T
    dv_o[...] = jnp.concatenate(dvs, 0).astype(low).T
    gbk_o[...] = jnp.concatenate(gbks, 0).astype(low)


def attend_back(first, count, scal, dctx, probs, q, k, v, bk, bq_t, tables, done=()):
    length = dctx.shape[0]
    half = tables[0].shape[1] // 2
    width, two = 2 * half, 2 * HEAD_DIM
    pair = pl.BlockSpec((length, two), lambda p: (0, first + p))
    out = pl.BlockSpec((length, two), lambda p: (0, p))
    flops = 4 * count * length * (8 * half * HEAD_DIM + length * (4 * half + 4 * HEAD_DIM))
    return call(
        functools.partial(attend_back_kernel, HEAD_DIM**-0.5),
        "attend_back",
        flops,
        count * 2e6,
        [shape(length, count * two)] * 3 + [shape(count * two, width), shape(width, count * two)],
        [out] * 3 + [pl.BlockSpec((two, width), lambda p: (p, 0)), pl.BlockSpec((width, two), lambda p: (0, p))],
        [SMEM, pair, pl.BlockSpec((2, length, length), lambda p: (p, 0, 0))]
        + [pair] * 3
        + [pl.BlockSpec((width, two), lambda p: (0, first + p)), pl.BlockSpec((two, width), lambda p: (first + p, 0))]
        + [VMEM] * 2,
        [],
        (scal, dctx, probs, q, k, v, bk, bq_t, tables[1], tables[2]),
        (count,),
        done=done,
    )


def project_back_kernel(
    count, plan, scal, rows_t, dq_a, dk_a, dv_a, dq_b, dk_b, dv_b, gbk_a, gbk_b, gbq_a, gbq_b, ups, ones, twos, *refs
):
    sums, outs, (grads, turned, sems) = refs[:2], refs[2 : 2 + count], refs[2 + count :]
    for side, ref in enumerate(sums):
        ref[...] = jnp.zeros(ref.shape, f32)
        ref[1:2, : ups.shape[1]] = ups[side : side + 1]
        ref[2:5, : ones.shape[1]] = ones[...]
        ref[5:8, : twos.shape[1]] = twos[...]
    size = turned.shape[2] // 2
    gbk = jnp.concatenate([gbk_a[...], gbk_b[...]], 0).T
    gbq = jnp.concatenate([gbq_a[...], gbq_b[...]], 1)
    for side in range(2):
        turned[side, :, :size] = sides(gbk, side)
        turned[side, :, size:] = sides(gbq, side)
    for i, (one, two) in enumerate(((dq_a, dq_b), (dk_a, dk_b), (dv_a, dv_b))):
        value = jnp.concatenate([one[...], two[...]], 1)
        value = jnp.concatenate([sides(value, side) for side in range(2)], 1)
        total = col(value.astype(f32))
        grad = dot(rows_t[...], value).astype(low)
        for side in range(2):
            sums[side][0:1, i * size : (i + 1) * size] = total[:, side * size : (side + 1) * size]
            grads[side, :, (2 + i) * size : (3 + i) * size] = grad[:, side * size : (side + 1) * size]
    rows = turned.shape[1] // BLOCKS
    for b in range(BLOCKS):
        to = ((b // 2) % 2) * 4 + (b // 4) * 2 + b % 2
        for side in range(2):
            grads[side, b * rows : (b + 1) * rows, : 2 * size] = turned[side, to * rows : (to + 1) * rows]
    finish(deal(grads, outs, sems, (scal[0], scal[1]), plan))


def project_back(scal, rows_t, grads, boxes, sums, done=()):
    width, length = rows_t.shape
    cols = grads[0].shape[1] + grads[3].shape[1]
    parts = part_shapes(width, 5 * cols // 2)
    out = call(
        functools.partial(project_back_kernel, len(parts), plans("scatter")),
        "project_back",
        6 * length * width * cols,
        cols * 15e3,
        [shape(8, 5 * cols // 2, dtype=f32)] * 2 + parts,
        [VMEM] * 2 + [ANYWHERE] * len(parts),
        [SMEM] + [VMEM] * 14,
        [pltpu.VMEM((2, width, 5 * cols // 2), low), pltpu.VMEM((2, width, cols), low), COPIES],
        (scal, rows_t, *grads, *boxes, *sums),
        done=done,
    )
    return out[0], out[1], out[2:]


def tokens_back_kernel(count, plan, scal, dq_a, dk_a, dv_a, dq_b, dk_b, dv_b, *refs):
    parts, (part_o, proj, sems) = refs[:count], refs[count:]
    hc = proj.shape[2] // 4
    copies = fetch(parts, proj, sems, (scal[0], scal[1]), plan, False, (2 * hc, 4 * hc))
    both = [jnp.concatenate([a[...], b[...]], 1) for a, b in ((dq_a, dq_b), (dk_a, dk_b), (dv_a, dv_b))]
    grads = [jnp.concatenate([sides(g, side) for g in both], 1) for side in range(2)]
    finish(copies)
    total = dot(grads[0], proj[0, :, : 3 * hc], NT) + dot(grads[1], proj[1, :, : 3 * hc], NT)
    part_o[...] = total.astype(low)


def tokens_back(scal, grads, parts, width, done=()):
    length = grads[0].shape[0]
    hc = parts[0].shape[2] // 6
    return call(
        functools.partial(tokens_back_kernel, len(parts), plans("early")),
        "tokens_back",
        12 * length * width * hc,
        5e6,
        shape(length, width),
        VMEM,
        [SMEM] + [VMEM] * 6 + [ANYWHERE] * len(parts),
        [pltpu.VMEM((2, width, 4 * hc), low), COPIES],
        (scal, *grads, *parts),
        done=done,
    )


def rows_kernel(scal, mine, sent, passed, out):
    length, half = mine.shape[0], sent.shape[0]
    page, core = scal[3], scal[4]
    out[pl.ds(pl.multiple_of(page * length, length), length)] = mine[...]
    out[pl.ds(pl.multiple_of((1 - page) * length + core * half, half), half)] = sent[...]
    out[pl.ds(pl.multiple_of((1 - page) * length + (1 - core) * half, half), half)] = passed[...]


def all_rows(scal, mine, sent, passed):
    length, width = mine.shape
    return call(
        rows_kernel, "all_rows", 0, 8 * length * width, shape(2 * length, width), VMEM, [SMEM] + [VMEM] * 3, [],
        (scal, mine, sent, passed),
    )


def sum_columns(a):
    return a + swap_dp(a, 1) if grid_dp()[0] > 1 else lax.psum(a, "dp")


def local(
    tokens, lengths, boxes, query_weight, key_weight, value_weight, query_bias, key_bias, value_bias,
    box_key_weight, box_query_weight, out_weight, out_bias, first_gain, first_shift, up_weight, up_bias,
    down_weight, down_bias, second_gain, second_shift, output_grad,
):
    pages = lengths.shape[0]
    page_len = tokens.shape[0] // pages
    width = tokens.shape[1]
    hc = query_weight.shape[1]
    units = up_weight.shape[1]

    page = lax.axis_index("head") // (lax.axis_size("head") // pages)
    start = page * page_len
    rows = lax.dynamic_slice_in_dim(tokens, start, page_len, 0)
    grad_rows = lax.dynamic_slice_in_dim(output_grad, start, page_len, 0)
    box_rows = lax.dynamic_slice_in_dim(boxes, start, page_len, 1)
    length = lax.dynamic_slice_in_dim(lengths, page, 1, 0)[0]
    biases = jnp.concatenate([query_bias, key_bias, value_bias, up_bias])[None].astype(low)
    biases = jnp.concatenate([biases, swap_page(biases)], 0).astype(f32)
    vecs_one = jnp.stack([out_bias, first_gain, first_shift]).astype(f32)
    vecs_two = jnp.stack([down_bias, second_gain, second_shift]).astype(f32)
    frequency = (10000.0 ** (-jnp.arange(width // 4, dtype=f32) / (width // 4)))[None]
    z, y = place_dp()
    core = lax.axis_index("head") % (lax.axis_size("head") // pages)
    at = jnp.arange(5, dtype=jnp.int32)
    scal = sum(jnp.where(at == i, value.astype(jnp.int32), 0) for i, value in enumerate((z, y, length, page, core)))
    rows_t = rows.T

    first = jnp.concatenate(
        [box_key_weight, box_query_weight, query_weight, key_weight, value_weight, out_weight.T], 1
    )
    line_1 = gather_line(first)
    tables = box_tables(after(box_rows.T, line_1[-1]).astype(f32), frequency)
    line_2 = gather_line(after(up_weight, *line_1[1:]))
    parts_1 = gather_early(line_1, (*tables, rows_t, rows, grad_rows, biases, scal, vecs_one, vecs_two), line_2[1:])
    line_3 = gather_line(after(down_weight.T, *line_2[1:]))
    parts_2 = gather_near(after(jnp.concatenate(line_2, 0), *parts_1[-2:]))

    pairs = hc // HEAD_DIM
    query, key, value, key_t, bk_t, bq, bk, bq_t = project(scal, rows, biases[:, : 3 * hc], parts_1)
    parts_3 = gather_near(jnp.concatenate(after(list(line_3), *parts_2[1:], query), 0))
    near_2, near_3 = parts_2[1:], parts_3[1:]
    parts_2 = gather_far(parts_2)
    parts_3 = gather_far(parts_3)
    ctx_a, probs_a = attend(1, scal, query, value, key_t, bk_t, bq, tables)
    mine, context, probs_b = attend_last(1, scal, query, value, key_t, bk_t, bq, tables, ctx_a, parts_1, near_2)
    mine = after(mine, *near_3, *parts_2[3:])
    attn, attn_theirs = mine, swap_core(mine)
    hidden, active, slope = feed_up(
        scal, attn, attn_theirs, rows, vecs_one, biases[:, 3 * hc :], parts_2
    )
    feed = feed_down(scal, active, parts_3, width)
    (result, grad_two, feed_low, sums_two), grads_3 = feed_back(
        scal, feed, swap_core(feed), hidden, grad_rows, vecs_two, active
    )
    grads_3 = scatter_far(grads_3)
    grad_inner, sums_up, mine = inner_back(scal, feed_low, slope, parts_3, parts_2)
    (grad_one, grad_context, sums_one), grads_2 = norm_back(
        scal, mine, swap_core(mine), grad_two, attn, attn_theirs, rows, vecs_one, grad_inner, context,
        parts_1, grads_3[1:],
    )
    grads_3 = scatter_near(grads_3)
    grads_2 = scatter_far(grads_2)
    *grads_a, gbk_a, gbq_a = attend_back(
        0, 1, scal, grad_context, probs_a, query, key, value, bk, bq_t, tables, grads_3
    )
    sum_3 = scatter_line(grads_3)
    *grads_b, gbk_b, gbq_b = attend_back(
        1, pairs - 1, scal, grad_context, probs_b, query, key, value, bk, bq_t, tables, (*grads_2[1:], gbk_a)
    )
    grads_2 = scatter_near(after(list(grads_2), gbk_a))
    grads = [*grads_a, *grads_b]
    own_small, oth_small, grads_1 = project_back(
        scal, rows_t, grads, [gbk_a, gbk_b, gbq_a, gbq_b], (sums_up, sums_one, sums_two), (*grads_2, sum_3)
    )
    sum_2 = scatter_line(grads_2)
    grads_1 = scatter_far(grads_1)
    grads_1 = scatter_near(after(list(grads_1), sum_2))
    small = own_small + swap_page(after(oth_small, *grads_1))
    half = page_len // 2

    def send_half(mine):
        return swap_page(lax.dynamic_slice_in_dim(mine, core * half, half, 0))

    sent = send_half(after(result, *grads_1, small))
    mine = tokens_back(scal, grads, parts_1, width, grads_1)
    token_grad = (grad_one + (mine.astype(f32) + swap_core(mine).astype(f32))).astype(low)
    sent_grad = send_half(token_grad)
    small = sum_columns(small)
    small = sum_lines(small)
    sum_1 = scatter_line(grads_1, lambda: (sent, sent_grad, small))

    return (
        all_rows(scal, result, sent, swap_core(sent)),
        all_rows(scal, token_grad, sent_grad, swap_core(sent_grad)),
        sum_1[:, 2 * hc : 3 * hc],
        sum_1[:, 3 * hc : 4 * hc],
        sum_1[:, 4 * hc :],
        small[0, :hc],
        small[0, hc : 2 * hc],
        small[0, 2 * hc : 3 * hc],
        sum_1[:, :hc],
        sum_1[:, hc : 2 * hc],
        sum_2[:, units:].T,
        small[2, :width],
        small[3, :width],
        small[4, :width],
        sum_2[:, :units],
        small[1, :units],
        sum_3.T,
        small[5, :width],
        small[6, :width],
        small[7, :width],
    )


def solution(mesh):
    row, vec, mat, tam, all_ = P("dp", None), P("head"), P("dp", "head"), P("head", "dp"), P()
    return jax.shard_map(
        local,
        mesh=mesh,
        in_specs=(
            row, P("dp"), P(None, "dp"), mat, mat, mat, vec, vec, vec, mat, mat, tam, all_, all_, all_,
            mat, vec, tam, all_, all_, all_, row,
        ),
        out_specs=(
            row, row, mat, mat, mat, vec, vec, vec, mat, mat, tam, all_, all_, all_, mat, vec, tam,
            all_, all_, all_,
        ),
        check_vma=False,
    )
```

```python
import functools

import jax
import jax.numpy as jnp
from jax import lax
from jax.experimental import pallas as pl
from jax.experimental.pallas import tpu as pltpu
from jax.sharding import PartitionSpec as P

HEAD_DIM = 64
norm_eps = 1e-05
sqrt_half = 0.7071067811865476
inv_root_two_pi = 0.3989422804014327
low = jnp.bfloat16
f32 = jnp.float32


def dot(left, right, axes=((1,), (0,))):
    return lax.dot_general(left, right, (axes, ((), ())), preferred_element_type=f32)


def permute(a, axis, name, partner):
    pairs = [(i, partner(i)) for i in range(lax.axis_size(axis))]
    with jax.named_scope("%s_%d_%d" % (name, a.shape[0], a.shape[-1])):
        return lax.ppermute(a, axis, pairs)


def swap_core(a):
    return permute(a, "head", "core", lambda i: i ^ 1)


def swap_page(a):
    return permute(a, "head", "page", lambda i: i ^ 2)


def swap_dp(a, bit):
    return permute(a, "dp", "column", lambda i: i ^ bit)


def turn_dp(a, step):
    n = lax.axis_size("dp")
    return permute(a, "dp", "line", lambda i: (i + step) % n)


VMEM_LIMIT = 56 * 1024 * 1024
VMEM_SMALL = 24 * 1024 * 1024
SMALL = (
    "box_tables", "project", "attend", "attend_last", "feed_up", "feed_down", "feed_back", "tokens_back", "all_rows",
)
BLOCKS = 8


def grid_dp():
    return (4, 2) if lax.axis_size("dp") == 8 else (1, 1)


def place_dp():
    index = lax.axis_index("dp")
    return (index // 2, index % 2) if lax.axis_size("dp") == 8 else (index * 0, index * 0)


def after(value, *done):
    return lax.optimization_barrier((value, *done))[0] if done else value


def block_plan(kind):
    nz, ny = grid_dp()
    if nz == 1:
        return (((0, 0, 0),), ((1, 0, 0),))
    half = nz // 2

    def run(side, ky, start, end):
        return tuple((side, ky, k) for k in range(start, end))

    far = (run(1, 1, 0, half), run(1, 1, half, nz))
    if kind == "early":
        return tuple(run(*block, *cut) for cut in ((0, 1), (1, nz)) for block in ((0, 0), (1, 0), (0, 1))) + far
    if kind == "scatter":
        return (run(0, 0, 0, nz),) + tuple(run(*block, *cut) for block in ((1, 0), (0, 1)) for cut in ((0, half), (half, nz))) + far
    return tuple(run(*block, 0, nz) for block in ((0, 0), (1, 0), (0, 1))) + far


def gather_line(shard):
    nz, ny = grid_dp()
    if nz == 1:
        return [lax.all_gather(shard, "dp", axis=0, tiled=True)[None]]
    return [shard[None]] + [turn_dp(shard, ny * k)[None] for k in range(1, nz)]


def gather_near(line):
    if grid_dp()[0] == 1:
        return [line, swap_page(line)]
    return [line, swap_page(line), swap_dp(line, 1)]


def gather_far(parts, done=()):
    half = grid_dp()[0] // 2
    if half == 0:
        return parts
    line, across, beside = parts
    far_a, far_b = after((across[:half], beside[half:]), *done)
    return [line, across, beside, swap_dp(far_a, 1), swap_page(far_b)]


def gather_early(line, near_done, far_done):
    nz = grid_dp()[0]
    if nz == 1:
        return gather_near(line[0])
    own = gather_near(line[0])
    rest = gather_near(after(jnp.concatenate(line[1:], 0), *own, *near_done))
    cut = nz // 2 - 1
    far_a, far_b = after((jnp.concatenate([own[1], rest[1][:cut]], 0), rest[2][cut:]), *rest[1:], *far_done)
    return own + rest + [swap_dp(far_a, 1), swap_page(far_b)]


def add(a, b):
    return (a.astype(f32) + b.astype(f32)).astype(low)


def scatter_far(parts):
    if grid_dp()[0] == 1:
        return parts
    line, across_a, across_b, beside_a, beside_b, far_a, far_b = parts
    far_a = swap_page(far_a)
    far_b = swap_dp(far_b, 1)
    beside = jnp.concatenate([add(beside_a, far_a), beside_b], 0)
    across = jnp.concatenate([across_a, add(across_b, far_b)], 0)
    return [line, across, beside]


def scatter_near(parts):
    line = parts[0].astype(f32) + swap_page(parts[1]).astype(f32)
    if len(parts) > 2:
        line = line + swap_dp(parts[2], 1).astype(f32)
    return [line[0]] + [line[k].astype(low) for k in range(1, line.shape[0])]


def scatter_line(line, done=lambda: ()):
    nz, ny = grid_dp()
    if nz == 1:
        return lax.psum_scatter(line[0].astype(low), "dp", scatter_dimension=0, tiled=True).astype(f32)
    come = [turn_dp(line[k], ny * k) for k in range(1, nz)]
    return functools.reduce(jnp.add, [piece.astype(f32) for piece in after(come, *done())], line[0])


def sum_lines(a):
    nz, ny = grid_dp()
    return functools.reduce(jnp.add, [turn_dp(a, ny * k) for k in range(1, nz)], a)


def part_shapes(blocks, width):
    nz, ny = grid_dp()
    return [jax.ShapeDtypeStruct((len(p), blocks // (nz * ny), width), low) for p in block_plan("scatter")]


def slots(parts, place, dims, sign, turned, plan):
    nz, ny = dims
    found = []
    for part, blocks in zip(parts, plan):
        for i, (side, ky, kz) in enumerate(blocks):
            piece = part.at[i]
            rows = piece.shape[0]
            z = lax.rem(place[0] + (sign * kz) % nz, nz) if nz > 1 else 0
            y = lax.rem(place[1] + ky, ny) if ny > 1 else 0
            block = z * ny + y
            if not turned:
                found.append((piece, side, pl.multiple_of(block * rows, rows)))
                continue
            size = rows * nz * ny // BLOCKS
            for sub in range(rows // size):
                b = block * (rows // size) + sub
                b = lax.rem(lax.div(b, 2), 2) * 4 + lax.div(b, 4) * 2 + lax.rem(b, 2)
                found.append((piece.at[pl.ds(sub * size, size)], side, pl.multiple_of(b * size, size)))
    return found


def fetch(parts, whole, sems, place, plan, turned=False, columns=None, start=True):
    dims, plan = plan
    copies = []
    for i, (piece, side, row) in enumerate(slots(parts, place, dims, -1, turned, plan)):
        source = piece if columns is None else piece.at[:, pl.ds(columns[0], columns[1])]
        copies.append(pltpu.make_async_copy(source, whole.at[side, pl.ds(row, piece.shape[0])], sems.at[i]))
    for copy in copies if start else []:
        copy.start()
    return copies


def deal(whole, parts, sems, place, plan, turned=False, columns=None):
    dims, plan = plan
    copies = []
    for i, (piece, side, row) in enumerate(slots(parts, place, dims, 1, turned, plan)):
        target = piece if columns is None else piece.at[:, pl.ds(columns[0], columns[1])]
        copies.append(pltpu.make_async_copy(whole.at[side, pl.ds(row, piece.shape[0])], target, sems.at[i]))
    for copy in copies:
        copy.start()
    return copies


def plans(kind):
    return grid_dp(), block_plan(kind)


def finish(copies):
    for copy in copies:
        copy.wait()


SMEM = pl.BlockSpec(memory_space=pltpu.SMEM)
VMEM = pl.BlockSpec(memory_space=pltpu.VMEM)
ANYWHERE = pl.BlockSpec(memory_space=pl.ANY)
COPIES = pltpu.SemaphoreType.DMA((2 * BLOCKS,))


def call(kernel, name, flops, moved, outs, out_specs, in_specs, scratch, args, grid=None, exps=0, done=()):
    extra = {} if grid is None else {"grid": grid}

    def body(*refs):
        kernel(*refs[: len(args)], *refs[len(args) + len(done) :])

    return pl.pallas_call(
        body,
        out_shape=outs,
        in_specs=in_specs + [ANYWHERE] * len(done),
        out_specs=out_specs,
        scratch_shapes=scratch,
        compiler_params=pltpu.CompilerParams(vmem_limit_bytes=VMEM_SMALL if name in SMALL else VMEM_LIMIT),
        cost_estimate=pl.CostEstimate(flops=int(flops), bytes_accessed=int(moved), transcendentals=int(exps)),
        name=name,
        **extra,
    )(*args, *done)


def shape(*dims, dtype=low):
    return jax.ShapeDtypeStruct(dims, dtype)


NT = ((1,), (1,))


def project_kernel(count, plan, scal, rows, bias, *refs):
    parts, refs = refs[:count], refs[count:]
    (q_o, k_o, v_o, key_t, bk_t, bq, bk, bq_t), (box, proj, sems, more_sems) = refs[:8], refs[8:]
    hc = box.shape[2] // 2
    place = (scal[0], scal[1])
    first = fetch(parts, proj, more_sems, place, plan, False, (2 * hc, 4 * hc))
    second = fetch(parts, box, sems, place, plan, True, (0, 2 * hc))
    finish(first)
    heads = hc // HEAD_DIM
    pairs = [[], [], []]
    for side in range(2):
        qkv = (dot(rows[...], proj[side, :, : 3 * hc]) + bias[side : side + 1]).astype(low)
        for i in range(3):
            pairs[i].append(qkv[:, i * hc : (i + 1) * hc])

    def paired(own, other, axis):
        cut = [slice(h * HEAD_DIM, (h + 1) * HEAD_DIM) for h in range(heads)]
        both = [(own[c], other[c]) if axis == 0 else (own[:, c], other[:, c]) for c in cut]
        return jnp.concatenate([one for two in both for one in two], axis)

    for ref, two in zip((q_o, k_o, v_o), pairs):
        ref[...] = paired(*two, 1)
    key_t[...] = k_o[...].T
    finish(second)
    bk[...] = paired(box[0, :, :hc], box[1, :, :hc], 1)
    bq[...] = paired(box[0, :, hc:], box[1, :, hc:], 1)
    bk_t[...] = bk[...].T
    bq_t[...] = bq[...].T


def project(scal, rows, bias, parts, done=()):
    length, width = rows.shape
    hc = parts[0].shape[2] // 6
    return call(
        functools.partial(project_kernel, len(parts), plans("early")),
        "project",
        12 * length * width * hc,
        10e6,
        [shape(length, 2 * hc)] * 3 + [shape(2 * hc, length), shape(2 * hc, width), shape(width, 2 * hc)]
        + [shape(width, 2 * hc), shape(2 * hc, width)],
        [VMEM] * 8,
        [SMEM, VMEM, VMEM] + [ANYWHERE] * len(parts),
        [pltpu.VMEM((2, width, 2 * hc), low), pltpu.VMEM((2, width, 4 * hc), low), COPIES, COPIES],
        (scal, rows, bias, *parts),
        done=done,
    )


def attend_pair(scale, length, q, v, key_t, bk_t, bq, query_table, queryt_table, keyt_table, p_o):
    half = query_table.shape[1] // 2
    cos, sin = query_table[:, :half].astype(f32), query_table[:, half:].astype(f32)
    cos_t, sin_t = queryt_table[:half].astype(f32), queryt_table[half:].astype(f32)
    valid = lax.broadcasted_iota(jnp.int32, (1, key_t.shape[1]), 1) < length
    outs = []
    for j in range(2):
        at = slice(j * HEAD_DIM, (j + 1) * HEAD_DIM)
        a = dot(q[:, at], bk_t[at])
        a_s, a_c = a[:, :half], a[:, half:]
        turn = jnp.concatenate(
            [(a_s * cos + a_c * sin).astype(low), (a_c * cos - a_s * sin).astype(low)], 1
        )
        b = dot(bq[:, at], key_t[at])
        b_s, b_c = b[:half], b[half:]
        turn_t = jnp.concatenate(
            [(b_s * sin_t + b_c * cos_t).astype(low), (b_c * sin_t - b_s * cos_t).astype(low)], 0
        )
        raw = dot(q[:, at], key_t[at]) + dot(turn, keyt_table[...]) + dot(query_table[...], turn_t)
        scores = jnp.where(valid, raw * scale, -1e9)
        exponent = jnp.exp(scores - jnp.max(scores, -1, keepdims=True))
        probs = (exponent * (1.0 / jnp.sum(exponent, -1, keepdims=True))).astype(low)
        p_o[j] = probs
        outs.append(dot(probs, v[:, at]))
    return jnp.concatenate(outs, 1).astype(low)


def attend_kernel(scale, scal, q, v, key_t, bk_t, bq, query_table, queryt_table, keyt_table, ctx_o, p_o):
    ctx_o[...] = attend_pair(
        scale, scal[2], q, v, key_t, bk_t, bq, query_table, queryt_table, keyt_table, p_o
    )


def attend_last_kernel(
    scale, count, plan, scal, q, v, key_t, bk_t, bq, query_table, queryt_table, keyt_table, ctx_a, *refs
):
    parts, (part_o, ctx_o, p_o, out_w, pairs, sems) = refs[:count], refs[count:]
    step = pl.program_id(0)
    hc = out_w.shape[2] // 2

    @pl.when(step == 0)
    def _():
        fetch(parts, out_w, sems, (scal[0], scal[1]), plan, False, (4 * hc, 2 * hc))

    pairs[step] = attend_pair(
        scale, scal[2], q, v, key_t, bk_t, bq, query_table, queryt_table, keyt_table, p_o
    )

    @pl.when(step == pl.num_programs(0) - 1)
    def _():
        ctx = jnp.concatenate([ctx_a[...]] + [pairs[i] for i in range(pairs.shape[0])], 1)
        both = [sides(ctx, side) for side in range(2)]
        ctx_o[...] = jnp.concatenate(both, 1)
        finish(fetch(parts, out_w, sems, (scal[0], scal[1]), plan, False, (4 * hc, 2 * hc), False))
        part_o[...] = (dot(both[0], out_w[0, :, hc:], NT) + dot(both[1], out_w[1, :, hc:], NT)).astype(low)


def attend_specs(first, length, half):
    two = 2 * HEAD_DIM
    wide = pl.BlockSpec((length, two), lambda p: (0, first + p))
    return [
        SMEM,
        wide,
        wide,
        pl.BlockSpec((two, length), lambda p: (first + p, 0)),
        pl.BlockSpec((two, 2 * half), lambda p: (first + p, 0)),
        pl.BlockSpec((2 * half, two), lambda p: (0, first + p)),
    ] + [VMEM] * 3


def attend_flops(count, length, half):
    return 4 * count * length * (4 * half * HEAD_DIM + length * (4 * half + 2 * HEAD_DIM))


def attend(count, scal, q, v, key_t, bk_t, bq, tables, done=()):
    length, half = tables[0].shape[0], tables[0].shape[1] // 2
    two = 2 * HEAD_DIM
    return call(
        functools.partial(attend_kernel, HEAD_DIM**-0.5),
        "attend",
        attend_flops(count, length, half),
        count * 2e6,
        [shape(length, count * two), shape(2 * count, length, length)],
        [pl.BlockSpec((length, two), lambda p: (0, p)), pl.BlockSpec((2, length, length), lambda p: (p, 0, 0))],
        attend_specs(0, length, half),
        [],
        (scal, q, v, key_t, bk_t, bq, tables[0], tables[2], tables[3]),
        (count,),
        2 * count * length * length,
        done,
    )


def attend_last(first, scal, q, v, key_t, bk_t, bq, tables, ctx_a, parts, done=()):
    length, half = tables[0].shape[0], tables[0].shape[1] // 2
    width, hc = 2 * half, parts[0].shape[2] // 6
    count = hc // HEAD_DIM - first
    two = 2 * HEAD_DIM
    return call(
        functools.partial(attend_last_kernel, HEAD_DIM**-0.5, len(parts), plans("early")),
        "attend_last",
        attend_flops(count, length, half),
        count * 2e6,
        [shape(length, width), shape(length, 2 * hc), shape(2 * count, length, length)],
        [
            pl.BlockSpec((length, width), lambda p: (0, 0)),
            pl.BlockSpec((length, 2 * hc), lambda p: (0, 0)),
            pl.BlockSpec((2, length, length), lambda p: (p, 0, 0)),
        ],
        attend_specs(first, length, half) + [VMEM] + [ANYWHERE] * len(parts),
        [pltpu.VMEM((2, width, 2 * hc), low), pltpu.VMEM((count, length, two), low), COPIES],
        (scal, q, v, key_t, bk_t, bq, tables[0], tables[2], tables[3], ctx_a, *parts),
        (count,),
        2 * count * length * length,
        done,
    )


def sides(values, side):
    heads = values.shape[1] // HEAD_DIM
    return jnp.concatenate([values[:, h * HEAD_DIM : (h + 1) * HEAD_DIM] for h in range(side, heads, 2)], 1)


def tables_kernel(boxes, frequency, query_o, key_o, queryt_o, keyt_o):
    width = frequency.shape[1]
    half = 2 * width
    for c in range(2):
        angles = boxes[:, c : c + 1] * frequency[...]
        cosine, sine = jnp.cos(angles), jnp.sin(angles)
        at, past = slice(c * width, (c + 1) * width), slice(half + c * width, half + (c + 1) * width)
        query_o[:, at] = cosine.astype(low)
        query_o[:, past] = sine.astype(low)
    key_o[:, :half] = query_o[:, half:]
    key_o[:, half:] = query_o[:, :half]
    queryt_o[...] = query_o[...].T
    keyt_o[:half] = queryt_o[half:]
    keyt_o[half:] = queryt_o[:half]


def box_tables(boxes, frequency):
    length, half = boxes.shape[0], 2 * frequency.shape[1]
    return call(
        tables_kernel,
        "box_tables",
        40 * length * half,
        3e6,
        [shape(length, 2 * half)] * 2 + [shape(2 * half, length)] * 2,
        [VMEM] * 4,
        [VMEM] * 2,
        [],
        (boxes, frequency),
    )


def standard(values):
    centered = values - jnp.mean(values, -1, keepdims=True)
    inverse = lax.rsqrt(jnp.mean(centered * centered, -1, keepdims=True) + norm_eps)
    return centered * inverse, inverse


def standard_back(upstream, scaled, inverse):
    return inverse * (
        upstream - jnp.mean(upstream, -1, keepdims=True) - scaled * jnp.mean(upstream * scaled, -1, keepdims=True)
    )


def col(values):
    return jnp.sum(values, 0, keepdims=True)


def feed_up_kernel(count, plan, scal, mine, theirs, rows, vecs, bias, *refs):
    ups, refs = refs[:count], refs[count:]
    (hidden_o, active_o, slope_o), (up, sems) = refs[:3], refs[3:]
    copies = fetch(ups, up, sems, (scal[0], scal[1]), plan)
    total = rows[...].astype(f32) + (mine[...].astype(f32) + theirs[...].astype(f32)) + vecs[0:1]
    scaled, _ = standard(total)
    hidden = scaled * vecs[1:2] + vecs[2:3]
    hidden_o[...] = hidden
    hidden_low = hidden.astype(low)
    finish(copies)
    width = up.shape[2]
    size = 256
    for side in range(2):
        for at in range(0, width, size):
            inner = dot(hidden_low, up[side, :, at : at + size]) + bias[side : side + 1, at : at + size]
            cumulative = 0.5 * (1.0 + lax.erf(inner * sqrt_half))
            density = jnp.exp(-0.5 * inner * inner) * inv_root_two_pi
            active_o[:, side * width + at : side * width + at + size] = (inner * cumulative).astype(low)
            slope_o[:, side * width + at : side * width + at + size] = (cumulative + inner * density).astype(low)


def feed_up(scal, mine, theirs, rows, vecs, bias, ups, done=()):
    length, width = rows.shape
    units = ups[0].shape[2]
    return call(
        functools.partial(feed_up_kernel, len(ups), plans("gather")),
        "feed_up",
        4 * length * width * units,
        11e6,
        [
            shape(length, width, dtype=f32),
            shape(length, 2 * units),
            shape(length, 2 * units),
        ],
        [VMEM] * 3,
        [SMEM] + [VMEM] * 5 + [ANYWHERE] * len(ups),
        [pltpu.VMEM((2, width, units), low), COPIES],
        (scal, mine, theirs, rows, vecs, bias, *ups),
        exps=2 * length * units,
        done=done,
    )


def feed_down_kernel(count, plan, scal, active, *refs):
    downs, (part_o, down, sems) = refs[:count], refs[count:]
    finish(fetch(downs, down, sems, (scal[0], scal[1]), plan))
    units = down.shape[2]
    part_o[...] = (dot(active[:, :units], down[0], NT) + dot(active[:, units:], down[1], NT)).astype(low)


def feed_down(scal, active, downs, width, done=()):
    length, units = active.shape[0], active.shape[1] // 2
    return call(
        functools.partial(feed_down_kernel, len(downs), plans("gather")),
        "feed_down",
        4 * length * width * units,
        5e6,
        shape(length, width),
        VMEM,
        [SMEM, VMEM] + [ANYWHERE] * len(downs),
        [pltpu.VMEM((2, width, units), low), COPIES],
        (scal, active, *downs),
        done=done,
    )


def feed_back_kernel(count, plan, scal, mine, theirs, hidden, grad_out, vecs, active, *refs):
    (result_o, grad_o, low_o, sums_o), outs, (grads, sems) = refs[:4], refs[4 : 4 + count], refs[4 + count :]
    scaled, inverse = standard(hidden[...] + (mine[...].astype(f32) + theirs[...].astype(f32)) + vecs[0:1])
    result_o[...] = (scaled * vecs[1:2] + vecs[2:3]).astype(low)
    grad = grad_out[...].astype(f32)
    sums_o[1:2] = col(grad * scaled)
    sums_o[2:3] = col(grad)
    grad = standard_back(grad * vecs[1:2], scaled, inverse)
    sums_o[0:1] = col(grad)
    grad_o[...] = grad
    grad_low = grad.astype(low)
    low_o[...] = grad_low
    turned = grad_low.T
    units = grads.shape[2]
    for side in range(2):
        grads[side] = dot(turned, active[:, side * units : (side + 1) * units]).astype(low)
    finish(deal(grads, outs, sems, (scal[0], scal[1]), plan))


def feed_back(scal, mine, theirs, hidden, grad_out, vecs, active):
    length, width = hidden.shape
    units = active.shape[1] // 2
    parts = part_shapes(width, units)
    out = call(
        functools.partial(feed_back_kernel, len(parts), plans("scatter")),
        "feed_back",
        4 * length * width * units,
        12e6,
        [shape(length, width), shape(length, width, dtype=f32), shape(length, width), shape(3, width, dtype=f32)] + parts,
        [VMEM] * 4 + [ANYWHERE] * len(parts),
        [SMEM] + [VMEM] * 6,
        [pltpu.VMEM((2, width, units), low), COPIES],
        (scal, mine, theirs, hidden, grad_out, vecs, active),
    )
    return out[:4], out[4:]


def inner_back_kernel(count, plan, scal, grad_low, slope, *refs):
    downs, ups, refs = refs[:count], refs[count : 2 * count], refs[2 * count :]
    (inner_o, sums_o, part_o), (down, up, sems, more_sems) = refs[:3], refs[3:]
    place = (scal[0], scal[1])
    first = fetch(downs, down, sems, place, plan)
    second = fetch(ups, up, more_sems, place, plan)
    finish(first)
    units = up.shape[2]
    for side in range(2):
        at = slice(side * units, (side + 1) * units)
        grad = (dot(grad_low[...], down[side]) * slope[:, at].astype(f32)).astype(low)
        inner_o[:, at] = grad
        sums_o[side : side + 1] = col(grad.astype(f32))
    finish(second)
    part = dot(inner_o[:, :units], up[0], NT) + dot(inner_o[:, units:], up[1], NT)
    part_o[...] = part.astype(low)


def inner_back(scal, grad_low, slope, downs, ups):
    length, width = grad_low.shape
    units = slope.shape[1] // 2
    return call(
        functools.partial(inner_back_kernel, len(ups), plans("gather")),
        "inner_back",
        8 * length * width * units,
        10e6,
        [shape(length, 2 * units), shape(2, units, dtype=f32), shape(length, width)],
        [VMEM] * 3,
        [SMEM] + [VMEM] * 2 + [ANYWHERE] * (2 * len(ups)),
        [pltpu.VMEM((2, width, units), low)] * 2 + [COPIES] * 2,
        (scal, grad_low, slope, *downs, *ups),
    )


def norm_back_kernel(count, given, plan, given_plan, scal, mine, theirs, grad_two, first, second, rows, vecs, grad_inner, ctx, *refs):
    weights, refs = refs[:given], refs[given:]
    (grad_o, dctx_o, sums_o), outs, (out_w, grads, sems) = refs[:3], refs[3 : 3 + count], refs[3 + count :]
    place = (scal[0], scal[1])
    hc = out_w.shape[2] // 2
    copies = fetch(weights, out_w, sems, place, given_plan, False, (4 * hc, 2 * hc))
    grad = grad_two[...] + (mine[...].astype(f32) + theirs[...].astype(f32))
    scaled, inverse = standard(rows[...].astype(f32) + (first[...].astype(f32) + second[...].astype(f32)) + vecs[0:1])
    hidden_low = (scaled * vecs[1:2] + vecs[2:3]).astype(low)
    sums_o[1:2] = col(grad * scaled)
    sums_o[2:3] = col(grad)
    grad = standard_back(grad * vecs[1:2], scaled, inverse)
    sums_o[0:1] = col(grad)
    grad_o[...] = grad
    grad_low = grad.astype(low)
    finish(copies)
    both = [dot(grad_low, out_w[side, :, hc:]).astype(low) for side in range(2)]
    cut = [slice(h * HEAD_DIM, (h + 1) * HEAD_DIM) for h in range(hc // HEAD_DIM)]
    dctx_o[...] = jnp.concatenate([one[:, c] for c in cut for one in both], 1)
    units = grads.shape[2] - hc
    turned = hidden_low.T
    for side in range(2):
        grads[side, :, :units] = dot(turned, grad_inner[:, side * units : (side + 1) * units]).astype(low)
    grad_ctx = dot(grad_low.T, ctx[...]).astype(low)
    for side in range(2):
        grads[side, :, units:] = grad_ctx[:, side * hc : (side + 1) * hc]
    finish(deal(grads, outs, sems, place, plan))


def norm_back(scal, mine, theirs, grad_two, first, second, rows, vecs, grad_inner, ctx, weights, done=()):
    length, width = grad_two.shape
    units, hc = grad_inner.shape[1] // 2, ctx.shape[1] // 2
    parts = part_shapes(width, units + hc)
    out = call(
        functools.partial(norm_back_kernel, len(parts), len(weights), plans("scatter"), plans("early")),
        "norm_back",
        4 * length * width * (units + 2 * hc),
        14e6,
        [shape(length, width, dtype=f32), shape(length, 2 * hc), shape(3, width, dtype=f32)] + parts,
        [VMEM] * 3 + [ANYWHERE] * len(parts),
        [SMEM] + [VMEM] * 9 + [ANYWHERE] * len(weights),
        [pltpu.VMEM((2, width, 2 * hc), low), pltpu.VMEM((2, width, units + hc), low), COPIES],
        (scal, mine, theirs, grad_two, first, second, rows, vecs, grad_inner, ctx, *weights),
        done=done,
    )
    return out[:3], out[3:]


def attend_back_kernel(
    scale, scal, dctx, probs, q, k, v, bk, bq_t, key_table, queryt_table,
    dq_o, dk_o, dv_o, gbk_o, gbq_o,
):
    half = key_table.shape[1] // 2
    sin, cos = key_table[:, :half].astype(f32), key_table[:, half:].astype(f32)
    cos_t, sin_t = queryt_table[:half].astype(f32), queryt_table[half:].astype(f32)
    qt2, vt2, dctxt2 = q[...].T, v[...].T, dctx[...].T
    dqs, dks, dvs, gbks = [], [], [], []
    for j in range(2):
        at = slice(j * HEAD_DIM, (j + 1) * HEAD_DIM)
        weights = probs[j]
        wide = weights.astype(f32)
        dprobs = dot(dctx[:, at], vt2[at])
        inner = jnp.sum(wide * dprobs, -1, keepdims=True)
        draw = (scale * (wide * (dprobs - inner))).astype(low)
        dvs.append(dot(dctxt2[at], weights))
        g = dot(draw, key_table[...])
        g_u, g_l = g[:, :half], g[:, half:]
        da = jnp.concatenate(
            [(g_u * cos - g_l * sin).astype(low), (g_u * sin + g_l * cos).astype(low)], 1
        )
        dqs.append(dot(draw, k[:, at]) + dot(da, bk[:, at]))
        gbks.append(dot(qt2[at], da))
        g = dot(queryt_table[...], draw)
        g_u, g_l = g[:half], g[half:]
        db = jnp.concatenate(
            [(g_u * sin_t - g_l * cos_t).astype(low), (g_u * cos_t + g_l * sin_t).astype(low)], 0
        )
        dks.append(dot(qt2[at], draw) + dot(bq_t[at], db))
        gbq_o[:, at] = dot(db, k[:, at]).astype(low)
    dq_o[...] = jnp.concatenate(dqs, 1).astype(low)
    dk_o[...] = jnp.concatenate(dks, 0).astype(low).T
    dv_o[...] = jnp.concatenate(dvs, 0).astype(low).T
    gbk_o[...] = jnp.concatenate(gbks, 0).astype(low)


def attend_back(first, count, scal, dctx, probs, q, k, v, bk, bq_t, tables, done=()):
    length = dctx.shape[0]
    half = tables[0].shape[1] // 2
    width, two = 2 * half, 2 * HEAD_DIM
    pair = pl.BlockSpec((length, two), lambda p: (0, first + p))
    out = pl.BlockSpec((length, two), lambda p: (0, p))
    flops = 4 * count * length * (8 * half * HEAD_DIM + length * (4 * half + 4 * HEAD_DIM))
    return call(
        functools.partial(attend_back_kernel, HEAD_DIM**-0.5),
        "attend_back",
        flops,
        count * 2e6,
        [shape(length, count * two)] * 3 + [shape(count * two, width), shape(width, count * two)],
        [out] * 3 + [pl.BlockSpec((two, width), lambda p: (p, 0)), pl.BlockSpec((width, two), lambda p: (0, p))],
        [SMEM, pair, pl.BlockSpec((2, length, length), lambda p: (p, 0, 0))]
        + [pair] * 3
        + [pl.BlockSpec((width, two), lambda p: (0, first + p)), pl.BlockSpec((two, width), lambda p: (first + p, 0))]
        + [VMEM] * 2,
        [],
        (scal, dctx, probs, q, k, v, bk, bq_t, tables[1], tables[2]),
        (count,),
        done=done,
    )


def project_back_kernel(
    count, plan, scal, rows_t, dq_a, dk_a, dv_a, dq_b, dk_b, dv_b, gbk_a, gbk_b, gbq_a, gbq_b, ups, ones, twos, *refs
):
    sums, outs, (grads, turned, sems) = refs[:2], refs[2 : 2 + count], refs[2 + count :]
    for side, ref in enumerate(sums):
        ref[...] = jnp.zeros(ref.shape, f32)
        ref[1:2, : ups.shape[1]] = ups[side : side + 1]
        ref[2:5, : ones.shape[1]] = ones[...]
        ref[5:8, : twos.shape[1]] = twos[...]
    size = turned.shape[2] // 2
    gbk = jnp.concatenate([gbk_a[...], gbk_b[...]], 0).T
    gbq = jnp.concatenate([gbq_a[...], gbq_b[...]], 1)
    for side in range(2):
        turned[side, :, :size] = sides(gbk, side)
        turned[side, :, size:] = sides(gbq, side)
    for i, (one, two) in enumerate(((dq_a, dq_b), (dk_a, dk_b), (dv_a, dv_b))):
        value = jnp.concatenate([one[...], two[...]], 1)
        value = jnp.concatenate([sides(value, side) for side in range(2)], 1)
        total = col(value.astype(f32))
        grad = dot(rows_t[...], value).astype(low)
        for side in range(2):
            sums[side][0:1, i * size : (i + 1) * size] = total[:, side * size : (side + 1) * size]
            grads[side, :, (2 + i) * size : (3 + i) * size] = grad[:, side * size : (side + 1) * size]
    rows = turned.shape[1] // BLOCKS
    for b in range(BLOCKS):
        to = ((b // 2) % 2) * 4 + (b // 4) * 2 + b % 2
        for side in range(2):
            grads[side, b * rows : (b + 1) * rows, : 2 * size] = turned[side, to * rows : (to + 1) * rows]
    finish(deal(grads, outs, sems, (scal[0], scal[1]), plan))


def project_back(scal, rows_t, grads, boxes, sums, done=()):
    width, length = rows_t.shape
    cols = grads[0].shape[1] + grads[3].shape[1]
    parts = part_shapes(width, 5 * cols // 2)
    out = call(
        functools.partial(project_back_kernel, len(parts), plans("scatter")),
        "project_back",
        6 * length * width * cols,
        cols * 15e3,
        [shape(8, 5 * cols // 2, dtype=f32)] * 2 + parts,
        [VMEM] * 2 + [ANYWHERE] * len(parts),
        [SMEM] + [VMEM] * 14,
        [pltpu.VMEM((2, width, 5 * cols // 2), low), pltpu.VMEM((2, width, cols), low), COPIES],
        (scal, rows_t, *grads, *boxes, *sums),
        done=done,
    )
    return out[0], out[1], out[2:]


def tokens_back_kernel(count, plan, scal, dq_a, dk_a, dv_a, dq_b, dk_b, dv_b, *refs):
    parts, (part_o, proj, sems) = refs[:count], refs[count:]
    hc = proj.shape[2] // 4
    copies = fetch(parts, proj, sems, (scal[0], scal[1]), plan, False, (2 * hc, 4 * hc))
    both = [jnp.concatenate([a[...], b[...]], 1) for a, b in ((dq_a, dq_b), (dk_a, dk_b), (dv_a, dv_b))]
    grads = [jnp.concatenate([sides(g, side) for g in both], 1) for side in range(2)]
    finish(copies)
    total = dot(grads[0], proj[0, :, : 3 * hc], NT) + dot(grads[1], proj[1, :, : 3 * hc], NT)
    part_o[...] = total.astype(low)


def tokens_back(scal, grads, parts, width, done=()):
    length = grads[0].shape[0]
    hc = parts[0].shape[2] // 6
    return call(
        functools.partial(tokens_back_kernel, len(parts), plans("early")),
        "tokens_back",
        12 * length * width * hc,
        5e6,
        shape(length, width),
        VMEM,
        [SMEM] + [VMEM] * 6 + [ANYWHERE] * len(parts),
        [pltpu.VMEM((2, width, 4 * hc), low), COPIES],
        (scal, *grads, *parts),
        done=done,
    )


def rows_kernel(scal, mine, sent, passed, out):
    length, half = mine.shape[0], sent.shape[0]
    page, core = scal[3], scal[4]
    out[pl.ds(pl.multiple_of(page * length, length), length)] = mine[...]
    out[pl.ds(pl.multiple_of((1 - page) * length + core * half, half), half)] = sent[...]
    out[pl.ds(pl.multiple_of((1 - page) * length + (1 - core) * half, half), half)] = passed[...]


def all_rows(scal, mine, sent, passed):
    length, width = mine.shape
    return call(
        rows_kernel, "all_rows", 0, 8 * length * width, shape(2 * length, width), VMEM, [SMEM] + [VMEM] * 3, [],
        (scal, mine, sent, passed),
    )


def sum_columns(a):
    return a + swap_dp(a, 1) if grid_dp()[0] > 1 else lax.psum(a, "dp")


def local(
    tokens, lengths, boxes, query_weight, key_weight, value_weight, query_bias, key_bias, value_bias,
    box_key_weight, box_query_weight, out_weight, out_bias, first_gain, first_shift, up_weight, up_bias,
    down_weight, down_bias, second_gain, second_shift, output_grad,
):
    pages = lengths.shape[0]
    page_len = tokens.shape[0] // pages
    width = tokens.shape[1]
    hc = query_weight.shape[1]
    units = up_weight.shape[1]

    page = lax.axis_index("head") // (lax.axis_size("head") // pages)
    start = page * page_len
    rows = lax.dynamic_slice_in_dim(tokens, start, page_len, 0)
    grad_rows = lax.dynamic_slice_in_dim(output_grad, start, page_len, 0)
    box_rows = lax.dynamic_slice_in_dim(boxes, start, page_len, 1)
    length = lax.dynamic_slice_in_dim(lengths, page, 1, 0)[0]
    biases = jnp.concatenate([query_bias, key_bias, value_bias, up_bias])[None].astype(low)
    biases = jnp.concatenate([biases, swap_page(biases)], 0).astype(f32)
    vecs_one = jnp.stack([out_bias, first_gain, first_shift]).astype(f32)
    vecs_two = jnp.stack([down_bias, second_gain, second_shift]).astype(f32)
    frequency = (10000.0 ** (-jnp.arange(width // 4, dtype=f32) / (width // 4)))[None]
    z, y = place_dp()
    core = lax.axis_index("head") % (lax.axis_size("head") // pages)
    at = jnp.arange(5, dtype=jnp.int32)
    scal = sum(jnp.where(at == i, value.astype(jnp.int32), 0) for i, value in enumerate((z, y, length, page, core)))
    rows_t = rows.T

    first = jnp.concatenate(
        [box_key_weight, box_query_weight, query_weight, key_weight, value_weight, out_weight.T], 1
    )
    line_1 = gather_line(first)
    tables = box_tables(after(box_rows.T, line_1[-1]).astype(f32), frequency)
    line_2 = gather_line(after(up_weight, *line_1[1:]))
    parts_1 = gather_early(line_1, (*tables, rows_t, rows, grad_rows, biases, scal, vecs_one, vecs_two), line_2[1:])
    line_3 = gather_line(after(down_weight.T, *line_2[1:]))
    parts_2 = gather_near(after(jnp.concatenate(line_2, 0), *parts_1[-2:]))

    pairs = hc // HEAD_DIM
    query, key, value, key_t, bk_t, bq, bk, bq_t = project(scal, rows, biases[:, : 3 * hc], parts_1)
    ctx_a, probs_a = attend(1, scal, query, value, key_t, bk_t, bq, tables)
    parts_3 = gather_near(jnp.concatenate(after(list(line_3), *parts_2[1:], ctx_a), 0))
    near_2, near_3 = parts_2[1:], parts_3[1:]
    parts_2 = gather_far(parts_2)
    parts_3 = gather_far(parts_3)
    mine, context, probs_b = attend_last(1, scal, query, value, key_t, bk_t, bq, tables, ctx_a, parts_1, near_2)
    mine = after(mine, *near_3, *parts_2[3:])
    attn, attn_theirs = mine, swap_core(mine)
    hidden, active, slope = feed_up(
        scal, attn, attn_theirs, rows, vecs_one, biases[:, 3 * hc :], parts_2
    )
    feed = feed_down(scal, active, parts_3, width)
    (result, grad_two, feed_low, sums_two), grads_3 = feed_back(
        scal, feed, swap_core(feed), hidden, grad_rows, vecs_two, active
    )
    grads_3 = scatter_far(grads_3)
    grad_inner, sums_up, mine = inner_back(scal, feed_low, slope, parts_3, parts_2)
    (grad_one, grad_context, sums_one), grads_2 = norm_back(
        scal, mine, swap_core(mine), grad_two, attn, attn_theirs, rows, vecs_one, grad_inner, context,
        parts_1, grads_3[1:],
    )
    grads_3 = scatter_near(grads_3)
    grads_2 = scatter_far(grads_2)
    *grads_a, gbk_a, gbq_a = attend_back(
        0, 1, scal, grad_context, probs_a, query, key, value, bk, bq_t, tables, grads_3
    )
    sum_3 = scatter_line(grads_3)
    *grads_b, gbk_b, gbq_b = attend_back(
        1, pairs - 1, scal, grad_context, probs_b, query, key, value, bk, bq_t, tables, (*grads_2[1:], gbk_a)
    )
    grads_2 = scatter_near(after(list(grads_2), gbk_a))
    grads = [*grads_a, *grads_b]
    own_small, oth_small, grads_1 = project_back(
        scal, rows_t, grads, [gbk_a, gbk_b, gbq_a, gbq_b], (sums_up, sums_one, sums_two), (*grads_2, sum_3)
    )
    sum_2 = scatter_line(grads_2)
    grads_1 = scatter_far(grads_1)
    grads_1 = scatter_near(after(list(grads_1), sum_2))
    small = own_small + swap_page(after(oth_small, *grads_1))
    half = page_len // 2

    def send_half(mine):
        return swap_page(lax.dynamic_slice_in_dim(mine, core * half, half, 0))

    sent = send_half(after(result, *grads_1, small))
    mine = tokens_back(scal, grads, parts_1, width, grads_1)
    token_grad = (grad_one + (mine.astype(f32) + swap_core(mine).astype(f32))).astype(low)
    sent_grad = send_half(token_grad)
    small = sum_columns(small)
    small = sum_lines(small)
    sum_1 = scatter_line(grads_1, lambda: (sent, sent_grad, small))

    return (
        all_rows(scal, result, sent, swap_core(sent)),
        all_rows(scal, token_grad, sent_grad, swap_core(sent_grad)),
        sum_1[:, 2 * hc : 3 * hc],
        sum_1[:, 3 * hc : 4 * hc],
        sum_1[:, 4 * hc :],
        small[0, :hc],
        small[0, hc : 2 * hc],
        small[0, 2 * hc : 3 * hc],
        sum_1[:, :hc],
        sum_1[:, hc : 2 * hc],
        sum_2[:, units:].T,
        small[2, :width],
        small[3, :width],
        small[4, :width],
        sum_2[:, :units],
        small[1, :units],
        sum_3.T,
        small[5, :width],
        small[6, :width],
        small[7, :width],
    )


def solution(mesh):
    row, vec, mat, tam, all_ = P("dp", None), P("head"), P("dp", "head"), P("head", "dp"), P()
    return jax.shard_map(
        local,
        mesh=mesh,
        in_specs=(
            row, P("dp"), P(None, "dp"), mat, mat, mat, vec, vec, vec, mat, mat, tam, all_, all_, all_,
            mat, vec, tam, all_, all_, all_, row,
        ),
        out_specs=(
            row, row, mat, mat, mat, vec, vec, vec, mat, mat, tam, all_, all_, all_, mat, vec, tam,
            all_, all_, all_,
        ),
        check_vma=False,
    )
```
